256 devices in a mesh: gx: 8 (over z), gy: 32 (over y, x, core).
Axes of the slice: x: 4, y: 4, z: 8, core: 2. Of those that a mesh axis runs over, the one named last changes fastest.
Arguments:
- background: float32 [16, 128, 256, 128], P(None, 'gx', 'gy'), may hold values from -6 to 6
- conductivity: float32 [128, 256, 128], P('gx', 'gy'), may hold values from 0.5 to 4
- perturbation: float32 [128, 256, 128], P('gx', 'gy'), may hold values from -6 to 6
- electrodes: int32 [16], replicated, may hold values from 0 to 4194303
- pattern: int32 [16, 2], replicated, may hold values from 0 to 15, as said below
Outputs:
- tangent_fields: float32 [16, 128, 256, 128], P(None, 'gx', 'gy')
- sensitivity: float32 [128, 256, 128], P('gx', 'gy')
The draws below stay inside these ranges and needn't reach their ends.
Inputs may be any that keep to these rules, and one draw needn't show every extreme that they name: `pattern`: each row names two different electrodes, and the first column names every electrode once.
All inputs are finite; a program needn't handle non-finite values.
Results may differ from the reference program's by a relative error of at most 0.00021.
Values sent between devices are 32-bit elements; how exact they have to be, the bound alone decides.
No kernel may reach another device: no remote copies, remote signals or barrier semaphores. Data moves between devices by JAX's collectives and lax.ppermute only.
A program may use at most 64 MiB of HBM per device.

```python
import math
import jax
import jax.numpy as jnp
from jax import lax

F = 16
E = 16
ITERS = 2
NX = 128
NY = 256
NZ = 128


def draw_pattern(key, part):
    key = jax.random.fold_in(key, 11)
    first_key, second_key = jax.random.split(key)
    first = jax.random.permutation(first_key, E).astype(jnp.int32)
    offset = jax.random.randint(second_key, (E,), 1, E).astype(jnp.int32)
    second = (first + offset) % E
    return jnp.stack([first, second], axis=1).astype(jnp.int32)


def with_ends(drawn, key, least, largest):
    longest = drawn.shape.index(max(drawn.shape))
    spots = []
    for shift in (0, 1):
        where = [jax.random.randint(jax.random.fold_in(key, axis), (), 0, length) for axis, length in enumerate(drawn.shape)]
        where[longest] = (where[longest] + shift) % drawn.shape[longest]
        spots.append(tuple(where))
    return drawn.at[spots[0]].set(least).at[spots[1]].set(largest)


def block_levels(key, shape, cuts, least, largest):
    loudness = 1.0
    for axis_at, shards_of in cuts:
        steps = jax.random.uniform(jax.random.fold_in(jax.random.fold_in(key, 6), axis_at), (shards_of,), jnp.float32, least / len(cuts), largest / len(cuts))
        loudness = loudness * jnp.repeat(jnp.exp(steps), shape[axis_at] // shards_of).reshape((-1,) + (1,) * (len(shape) - 1 - axis_at))
    return loudness


def bell_draw(key, dims, width, bound, shards=(), kind=jnp.bfloat16):
    values = jax.random.normal(key, dims, jnp.float32) * width
    if len(shards) > 0:
        values = block_levels(key, dims, shards, -0.22, 0.18) * values
    return jnp.clip(values, min=-bound, max=bound).astype(kind)


def setup_inputs(seed: int = 0) -> dict:
    splits = jax.random.split(jax.random.key(seed), 6)
    return {
        "background": bell_draw(splits[0], (F, NX, NY, NZ), 1.0, 6.0, ((1, 8), (2, 32)), jnp.float32),
        "conductivity": jnp.clip(jnp.exp(math.log(4.0) - 2.0794415 * jax.random.uniform(splits[1], (NX, NY, NZ), jnp.float32) ** block_levels(splits[1], (NX, NY, NZ), ((0, 8), (1, 32)), -0.2, 0.2)), 0.5, 4.0),
        "perturbation": bell_draw(splits[2], (NX, NY, NZ), 1.0, 6.0, ((0, 8), (1, 32)), jnp.float32),
        "electrodes": with_ends(jax.random.randint(splits[3], (E,), 0, NX * NY * NZ), jax.random.fold_in(splits[3], 1), 0, (NX * NY * NZ) - 1).astype(jnp.int32),
        "pattern": draw_pattern(jax.random.fold_in(splits[5], 71), 0),
    }


def neighbour_views(padded):
    lead = padded.ndim - 3

    def view(dx, dy, dz):
        idx = [slice(None)] * lead
        idx += [slice(1 + dx, padded.shape[lead] - 1 + dx), slice(1 + dy, padded.shape[lead + 1] - 1 + dy), slice(1 + dz, padded.shape[lead + 2] - 1 + dz)]
        return padded[tuple(idx)]
    moves = [(1, 0, 0), (-1, 0, 0), (0, 1, 0), (0, -1, 0), (0, 0, 1), (0, 0, -1)]
    return (view(0, 0, 0), [view(a, b, c) for a, b, c in moves])

def stencil(field_pad, sigma_pad):
    centre, others = neighbour_views(field_pad)
    scent, sothers = neighbour_views(sigma_pad)
    result = 0.05 * centre
    for qj, sj in zip(others, sothers):
        result = result + 0.5 * (scent + sj) * (centre - qj)
    return result

def tangent_source(back_pad, pert_pad):
    centre, others = neighbour_views(back_pad)
    pcent, pothers = neighbour_views(pert_pad)
    result = jnp.zeros_like(centre)
    for qj, pj in zip(others, pothers):
        result = result - 0.5 * (pcent + pj) * (centre - qj)
    return result

def sens_terms(back_pad, adj_pad):
    centre, others = neighbour_views(back_pad)
    acent, aothers = neighbour_views(adj_pad)
    result = jnp.zeros(centre.shape[1:], jnp.float32)
    for qj, aj in zip(others, aothers):
        result = result - 0.5 * lax.optimization_barrier(jnp.sum((centre - qj) * (acent - aj), axis=0))
    return result

def gram(left, right):
    count = left.shape[0]
    return jnp.dot(left.reshape(count, -1), right.reshape(count, -1).T, precision=lax.Precision.HIGHEST)

def combine(coeff, fields):
    count = fields.shape[0]
    return jnp.dot(coeff.T, fields.reshape(count, -1), precision=lax.Precision.HIGHEST).reshape(fields.shape)

def chol_solve(matrix, rhs):
    factor = jnp.linalg.cholesky(matrix)
    return jax.scipy.linalg.cho_solve((factor, True), rhs)

def pad_fields(fields):
    return jnp.pad(fields, ((0, 0), (1, 1), (1, 1), (1, 1)))

def block_solve(rhs, sigma_pad):
    solution = jnp.zeros_like(rhs)
    resid = rhs
    search = rhs
    norms = gram(resid, resid)
    for step in range(ITERS):
        image = stencil(pad_fields(search), sigma_pad)
        curv = gram(search, image)
        alpha = chol_solve(curv, norms)
        solution = solution + combine(alpha, search)
        resid = resid - combine(alpha, image)
        if step + 1 < ITERS:
            fresh = gram(resid, resid)
            beta = chol_solve(norms, fresh)
            search = resid + combine(beta, search)
            norms = fresh
    return solution

def reference(background, conductivity, perturbation, electrodes, pattern):
    sigma_pad = jnp.pad(conductivity, 1)
    back_pad = pad_fields(background)
    rhs = tangent_source(back_pad, jnp.pad(perturbation, 1))
    tangent = block_solve(rhs, sigma_pad)
    count = tangent.shape[0]
    flat = tangent.reshape(count, -1)
    probe = flat[:, electrodes]
    measured = probe[:, pattern[:, 0]] - probe[:, pattern[:, 1]]
    weight = jnp.zeros(probe.shape, jnp.float32).at[:, pattern[:, 0]].add(measured).at[:, pattern[:, 1]].add(-measured)
    inject = jnp.zeros(flat.shape, jnp.float32).at[:, electrodes].add(weight)
    damping = 80.0 / math.sqrt(NX * NY * NZ)
    adj_rhs = damping * tangent + 8.0 * inject.reshape(tangent.shape)
    adjoint = block_solve(adj_rhs, sigma_pad)
    sens = sens_terms(back_pad, pad_fields(adjoint))
    return (tangent, sens)
```

```python
import math

import jax
import jax.numpy as jnp
from jax import lax
from jax.experimental import pallas as pl
from jax.experimental.pallas import tpu as pltpu
from jax.sharding import PartitionSpec as P

SHIFT = 12.0
F = 16
LANES = 128
HALO = 4
HIGHEST = lax.Precision.HIGHEST
V0, V1, V2, E0, E1 = range(5)
HALO_ROWS = 48


def tile_at(y):
    return slice(y * F, (y + 1) * F)


def pack_kernel(bg_ref, cond_ref, pert_ref, own_ref, up_ref, down_ref):
    size_x, size_y = cond_ref.shape[0], cond_ref.shape[1]

    def plane(x, carry):
        for y in range(size_y):
            tile = bg_ref[pl.ds(x * size_y + y, F, stride=size_x * size_y), :]
            own_ref[x, tile_at(y), :] = tile
            if y >= size_y - HALO:
                up_ref[x, tile_at(y - size_y + HALO), :] = tile
            if y < HALO:
                down_ref[x, tile_at(y), :] = tile
        cond, pert = cond_ref[x], pert_ref[x]
        own_ref[x, 128:136, :] = cond
        own_ref[x, 136:144, :] = pert
        up_ref[x, 64:72, :] = jnp.concatenate([cond[4:8], pert[4:8]], axis=0)
        down_ref[x, 64:72, :] = jnp.concatenate([cond[0:4], pert[0:4]], axis=0)
        return carry

    lax.fori_loop(0, size_x, plane, 0)


def pack(background, conductivity, perturbation):
    shape = jax.ShapeDtypeStruct
    return pl.pallas_call(
        pack_kernel,
        out_shape=(
            shape((16, 144, LANES), jnp.float32),
            shape((16, 72, LANES), jnp.float32),
            shape((16, 72, LANES), jnp.float32),
        ),
        compiler_params=pltpu.CompilerParams(vmem_limit_bytes=16 * 2**20),
        name="pack_y",
    )(background, conductivity, perturbation)


def run_copies(pairs, sems):
    copies = [pltpu.make_async_copy(s, d, sems.at[i]) for i, (s, d) in enumerate(pairs)]
    for c in copies:
        c.start()
    return copies


def edge_layout():
    low, high, at = [], [], 0
    for k in range(HALO):
        low.append((4 - k, 12 + k, at))
        at += (8 + 2 * k) * F + 32
    at = 0
    for k in range(HALO):
        high.append((1 + k, 15 - k, at))
        at += (14 - 2 * k) * F + 32
    return low, high, at


EDGE_LOW, EDGE_HIGH, EDGE_ROWS = edge_layout()
PACK_COPIES = 46


def pack_x_kernel(own_ref, left_ref, right_ref, up_ref, down_ref, sems):
    pairs = []
    for out, table, base in ((up_ref, EDGE_LOW, 12), (down_ref, EDGE_HIGH, 0)):
        for k, (y0, y1, at) in enumerate(table):
            x = base + k
            pieces = []
            if y0 < 4:
                pieces.append((left_ref, y0 * F, 64))
            pieces.append((own_ref, 0, 128))
            if y1 > 12:
                pieces.append((right_ref, 0, (y1 - 12) * F))
            pieces += [(own_ref, 128, 144), (left_ref, 64, 72), (right_ref, 64, 72)]
            for ref, a, b in pieces:
                pairs.append((ref.at[x, pl.ds(a, b - a)], out.at[pl.ds(at, b - a)]))
                at += b - a
    for c in run_copies(pairs, sems):
        c.wait()


def pack_x(own, left, right):
    shape = jax.ShapeDtypeStruct((EDGE_ROWS, LANES), jnp.float32)
    anywhere = pl.BlockSpec(memory_space=pl.ANY)
    return pl.pallas_call(
        pack_x_kernel,
        out_shape=(shape, shape),
        in_specs=[anywhere] * 3,
        out_specs=(anywhere, anywhere),
        scratch_shapes=[pltpu.SemaphoreType.DMA((PACK_COPIES,))],
        compiler_params=pltpu.CompilerParams(vmem_limit_bytes=2 * 2**20),
        name="pack_x",
    )(own, left, right)


def lane_ids(rows):
    return lax.broadcasted_iota(jnp.int32, (rows, LANES), 1)


def faces(cells, fx, fy, fz, dd, sign, base):
    lane = lane_ids(16)
    edge = (lane == 0) | (lane == LANES - 1)
    half = 0.5 * sign

    def plane(x, carry):
        c = cells[x]
        fx[x] = half * (c + cells[jnp.minimum(x + 1, 23)])
        fy[x] = half * (c + pltpu.roll(c, 15, 0))
        fz[x] = jnp.where(lane == LANES - 1, 0.0, half * (c + pltpu.roll(c, LANES - 1, 1)))
        dd[x] = base + jnp.where(edge, half * c, 0.0)
        return carry

    lax.fori_loop(0, 24, plane, 0)


def stencil_plane(src, coeffs, x, y0, y1, mask_x, mask_y, emit):
    fx, fy, fz, dd = coeffs
    q = src[x, tile_at(y0), :]
    flux = fy[x, y0 - 1 : y0, :] * (q - src[x, tile_at(y0 - 1), :])
    for y in range(y0, y1):
        nxt = src[x, tile_at(y + 1), :]
        row = slice(y, y + 1)
        later = fy[x, row, :] * (nxt - q)
        fz_at = fz[x, row, :] * (pltpu.roll(q, LANES - 1, 1) - q)
        out = dd[x, row, :] * q + (flux - later)
        out = out + fx[x - 1, row, :] * (q - src[x - 1, tile_at(y), :])
        out = out - fx[x, row, :] * (src[x + 1, tile_at(y), :] - q)
        out = out + (pltpu.roll(fz_at, 1, 1) - fz_at)
        mask = mask_x
        if y < 4:
            mask = mask_y[0] if mask is None else mask * mask_y[0]
        elif y >= 12:
            mask = mask_y[1] if mask is None else mask * mask_y[1]
        if mask is not None:
            out = out * mask
        emit(y, out)
        flux, q = later, nxt


def put_split(s_ref, block, lo_base, lane_at, value):
    hi = value.astype(jnp.bfloat16)
    s_ref[block * F : (block + 1) * F, pl.ds(lane_at, LANES)] = hi
    if lo_base is not None:
        lo = (value - hi.astype(jnp.float32)).astype(jnp.bfloat16)
        at = lo_base + block * F
        s_ref[at : at + F, pl.ds(lane_at, LANES)] = lo


def row_of(x, y):
    if isinstance(x, int) and x == 3:
        return 160 + (y - 4)
    if isinstance(x, int) and x == 20:
        return 168 + (y - 4)
    if y == 3:
        return 128 + (x - 4)
    if y == 12:
        return 144 + (x - 4)
    return (x - 4) * 8 + (y - 4)


def lane_of(x, y):
    at = row_of(x, y) * LANES
    return at if isinstance(at, int) else pl.multiple_of(at, LANES)


def kept(x, y):
    if isinstance(x, int) and x in (3, 20):
        return 4 <= y < 12
    if isinstance(x, int):
        return False
    return 3 <= y <= 12


def sweep(src, dst, coeffs, reach, masks, s_ref, block, lo_base):
    mask_x, mask_y = masks

    def emit_at(x):
        def emit(y, out):
            if dst is not None:
                dst[x, tile_at(y), :] = out
            if s_ref is not None and kept(x, y):
                put_split(s_ref, block, lo_base, lane_of(x, y), out)

        return emit

    for step in range(1, reach + 1):
        y0, y1 = 4 - (reach - step), 12 + (reach - step)
        for x, mask in ((4 - step, mask_x[0]), (19 + step, mask_x[1])):
            stencil_plane(src, coeffs, x, y0, y1, mask, mask_y, emit_at(x))

    def plane(x, carry):
        stencil_plane(src, coeffs, x, 4 - reach, 12 + reach, None, mask_y, emit_at(x))
        return carry

    lax.fori_loop(4, 20, plane, 0)


def krylov_kernel(
    elec_ref, own_ref, left_ref, right_ref, low_ref, high_ref, s_ref, pay_ref,
    bext, v0, v1, v2, e0, e1, t_ref, cond, pert, cx, cy, cz, cd, px, py, pz, pd, gram, sems,
):
    pairs = [
        (own_ref.at[:, pl.ds(0, 128)], bext.at[pl.ds(4, 16), pl.ds(64, 128)]),
        (own_ref.at[:, pl.ds(128, 16)], bext.at[pl.ds(4, 16), pl.ds(256, 16)]),
        (left_ref.at[:, pl.ds(0, 64)], bext.at[pl.ds(4, 16), pl.ds(0, 64)]),
        (left_ref.at[:, pl.ds(64, 8)], bext.at[pl.ds(4, 16), pl.ds(272, 8)]),
        (right_ref.at[:, pl.ds(0, 64)], bext.at[pl.ds(4, 16), pl.ds(192, 64)]),
        (right_ref.at[:, pl.ds(64, 8)], bext.at[pl.ds(4, 16), pl.ds(280, 8)]),
    ]
    for ref, table, base in ((low_ref, EDGE_LOW, 0), (high_ref, EDGE_HIGH, 20)):
        for k, (y0, y1, at) in enumerate(table):
            count = (y1 - y0) * F
            pairs.append((ref.at[pl.ds(at, count)], bext.at[base + k, pl.ds(y0 * F, count)]))
            pairs.append((ref.at[pl.ds(at + count, 32)], bext.at[base + k, pl.ds(256, 32)]))
    copies = run_copies(pairs, sems)

    gx, gy = lax.axis_index("gx"), lax.axis_index("gy")
    last_x, last_y = lax.axis_size("gx") - 1, lax.axis_size("gy") - 1
    one, zero = jnp.float32(1), jnp.float32(0)
    mask_x = (jnp.where(gx > 0, one, zero), jnp.where(gx < last_x, one, zero))
    mask_y = (jnp.where(gy > 0, one, zero), jnp.where(gy < last_y, one, zero))
    masks = (mask_x, mask_y)
    total_y = 8 * (last_y + 1)

    sub = lax.broadcasted_iota(jnp.int32, (F, LANES), 0)
    lane = lane_ids(F)
    ids = jnp.zeros((F, LANES), jnp.int32)
    for e in range(F):
        ids = jnp.where(sub == e, elec_ref[e], ids)
    ids = ids - lane

    def unit_plane(x):
        at_x = gx * 16 + x - 4
        good_x = (at_x >= 0) & (at_x < 16 * (last_x + 1))
        for y in range(2, 14):
            at_y = gy * 8 + y - 4
            good = good_x & (at_y >= 0) & (at_y < total_y)
            here = jnp.where(good, (at_x * total_y + at_y) * LANES, -(2**20))
            value = jnp.where(ids == here, 1.0, 0.0)
            e0[x, tile_at(y), :] = value
            if kept(x, y):
                put_split(s_ref, E0, None, lane_of(x, y), value)

    for x in (2, 3, 20, 21):
        unit_plane(x)

    def unit_loop(x, carry):
        unit_plane(x)
        return carry

    lax.fori_loop(4, 20, unit_loop, 0)
    s_ref[80 + E0 * F : 80 + (E0 + 1) * F, :] = jnp.zeros((F, s_ref.shape[1]), jnp.bfloat16)
    for c in copies:
        c.wait()

    def coeff_plane(x, carry):
        own, left, right = bext[x, 256:272, :], bext[x, 272:280, :], bext[x, 280:288, :]
        cond[x] = jnp.concatenate([left[0:4], own[0:8], right[0:4]], axis=0)
        pert[x] = jnp.concatenate([left[4:8], own[8:16], right[4:8]], axis=0)
        return carry

    lax.fori_loop(0, 24, coeff_plane, 0)
    faces(cond, cx, cy, cz, cd, 1.0, 0.05 - SHIFT)
    faces(pert, px, py, pz, pd, -1.0, 0.0)
    ccoef, pcoef = (cx, cy, cz, cd), (px, py, pz, pd)

    sweep(bext, v0, pcoef, 3, masks, s_ref, V0, 80)
    sweep(v0, v1, ccoef, 2, masks, s_ref, V1, 80)
    sweep(v1, v2, ccoef, 1, masks, s_ref, V2, 80)
    sweep(v2, None, ccoef, 0, masks, t_ref, 0, 32)
    sweep(e0, e1, ccoef, 1, masks, s_ref, E1, 80)
    sweep(e1, None, ccoef, 0, masks, t_ref, 1, 32)

    gram[...] = jnp.zeros_like(gram)
    chunk = 1024

    def gram_step(i, carry):
        at = pl.ds(pl.multiple_of(i * chunk, chunk), chunk)
        left = s_ref[:, at]
        right = jnp.concatenate([left, t_ref[:, at]], axis=0)
        gram[...] += lax.dot_general(
            left, right, (((1,), (1,)), ((), ())), preferred_element_type=jnp.float32
        )
        return carry

    lax.fori_loop(0, 128 * LANES // chunk, gram_step, 0)
    both = gram[0:80, :] + gram[80:160, :]

    def block(row, col, lo):
        rows = both[row * F : (row + 1) * F]
        return rows[:, col : col + F] + rows[:, lo : lo + F]

    def pair(row, col):
        return block(row, col * F, 80 + col * F)

    v3, e2 = (160, 192), (176, 208)
    blocks = [
        pair(V0, V0), pair(V0, V1), pair(V1, V1), pair(V1, V2), pair(V2, V2), block(V2, *v3),
        pair(V0, E0), pair(V1, E0), pair(V2, E0), block(E0, *v3), block(E1, *v3),
        pair(E0, E0), pair(E0, E1), pair(E1, E1), block(E1, *e2), jnp.zeros((F, F), jnp.float32),
    ]
    pay_ref[0:16, :] = jnp.concatenate(blocks[:8], axis=1)
    pay_ref[16:32, :] = jnp.concatenate(blocks[8:], axis=1)


CELLS = 176 * LANES


def krylov(electrodes, own, left, right, low, high):
    anywhere = pl.BlockSpec(memory_space=pl.ANY)
    field = pltpu.VMEM((24, 256, LANES), jnp.float32)
    coeff = pltpu.VMEM((24, 16, LANES), jnp.float32)
    return pl.pallas_call(
        krylov_kernel,
        out_shape=(
            jax.ShapeDtypeStruct((160, CELLS), jnp.bfloat16),
            jax.ShapeDtypeStruct((32, LANES), jnp.float32),
        ),
        in_specs=[pl.BlockSpec(memory_space=pltpu.SMEM)] + [anywhere] * 5,
        scratch_shapes=[pltpu.VMEM((24, 288, LANES), jnp.float32)]
        + [field] * 5
        + [pltpu.VMEM((64, 128 * LANES), jnp.bfloat16)]
        + [coeff] * 10
        + [pltpu.VMEM((160, 224), jnp.float32), pltpu.SemaphoreType.DMA((22,))],
        compiler_params=pltpu.CompilerParams(vmem_limit_bytes=48 * 2**20),
        name="krylov",
    )(electrodes, own, left, right, low, high)


def matmul(a, b, dims=((1,), (0,))):
    return lax.dot_general(
        a, b, (dims, ((), ())), precision=HIGHEST, preferred_element_type=jnp.float32
    )


def galerkin(m0, m1, m2, m3):
    a12 = m2 + SHIFT * m1
    work = jnp.concatenate(
        [
            jnp.concatenate([m1 + SHIFT * m0, a12, m0], axis=1),
            jnp.concatenate([a12, m3 + SHIFT * m2, m1], axis=1),
        ],
        axis=0,
    )
    sub = lax.broadcasted_iota(jnp.int32, work.shape, 0)
    for k in range(2 * F):
        row = work[k : k + 1, :]
        row = row / row[:, k : k + 1]
        work = jnp.where(sub == k, row, work - work[:, k : k + 1] * row)
    return work[:, 2 * F :]


def final_kernel(
    pattern_ref, parts_ref, own_ref, left_ref, right_ref, low_ref, high_ref, s_hbm,
    out_ref, sens_ref, bg, adj, s_ref, sems, *, damping,
):
    pairs = [
        (own_ref.at[:, pl.ds(0, 128)], bg.at[pl.ds(1, 16), pl.ds(16, 128)]),
        (left_ref.at[:, pl.ds(48, 16)], bg.at[pl.ds(1, 16), pl.ds(0, 16)]),
        (right_ref.at[:, pl.ds(0, 16)], bg.at[pl.ds(1, 16), pl.ds(144, 16)]),
        (low_ref.at[pl.ds(EDGE_LOW[3][2] + 3 * F, 128)], bg.at[0, pl.ds(16, 128)]),
        (high_ref.at[pl.ds(EDGE_HIGH[0][2] + 3 * F, 128)], bg.at[17, pl.ds(16, 128)]),
        (s_hbm, s_ref),
    ]
    copies = run_copies(pairs, sems)

    total = jnp.sum(parts_ref[...], axis=0)

    def part(k):
        r, c = (k // 8) * F, (k % 8) * F
        return total[r : r + F, c : c + F]

    m = [part(k) for k in range(6)]
    p = [part(6), part(7), part(8), part(9).T, part(10).T]
    e = [part(k) for k in range(11, 15)]
    y = galerkin(*m[:4])
    y0, y1 = y[0:F], y[F:]
    probe = matmul(y0, p[0], ((0,), (0,))) + matmul(y1, p[1], ((0,), (0,)))
    lane = lax.broadcasted_iota(jnp.int32, (F, F), 1)
    sub = lax.broadcasted_iota(jnp.int32, (F, F), 0)
    first, second = jnp.zeros((F, F), jnp.int32), jnp.zeros((F, F), jnp.int32)
    for i in range(F):
        first = jnp.where(sub == i, pattern_ref[i, 0], first)
        second = jnp.where(sub == i, pattern_ref[i, 1], second)
    pairing = jnp.where(lane == first, 1.0, 0.0) - jnp.where(lane == second, 1.0, 0.0)
    measured = matmul(probe, pairing, ((1,), (1,)))
    weight = 8.0 * matmul(measured, pairing)
    z = jnp.concatenate([damping * y0, damping * y1, weight.T], axis=0)
    rows = []
    for k in range(4):
        rows.append(jnp.concatenate([m[k], m[k + 1], p[k]], axis=1))
        rows.append(jnp.concatenate([m[k + 1], m[k + 2], p[k + 1]], axis=1))
        rows.append(jnp.concatenate([p[k].T, p[k + 1].T, e[k]], axis=1))
    nz = matmul(jnp.concatenate(rows, axis=0), z)
    moments = [matmul(z, nz[48 * k : 48 * (k + 1)], ((0,), (0,))) for k in range(4)]
    q = galerkin(*moments)
    z0, z1 = matmul(z, q[0:F]), matmul(z, q[F:])
    mix = jnp.concatenate(
        [z0[0:F], z0[F : 2 * F] + z1[0:F], z1[F : 2 * F], z0[2 * F :], z1[2 * F :]], axis=0
    )
    mix = jnp.concatenate(
        [jnp.concatenate([y, jnp.zeros((48, F), jnp.float32)], axis=0), mix], axis=1
    ).T
    hi = mix.astype(jnp.bfloat16)
    lo = (mix - hi.astype(jnp.float32)).astype(jnp.bfloat16)
    both = jnp.concatenate([hi, lo], axis=0)
    both = jnp.concatenate([both, both], axis=1)
    for c in copies:
        c.wait()

    def combine(at, count):
        out = jnp.dot(both, s_ref[:, pl.ds(at, count)], preferred_element_type=jnp.float32)
        return out[0:32] + out[32:64]

    def plane(x, carry):
        out = combine(pl.multiple_of(x * 8 * LANES, 8 * LANES), 8 * LANES)
        for k in range(8):
            cols = slice(k * LANES, (k + 1) * LANES)
            out_ref[pl.ds(x * 8 + k, F, stride=128), :] = out[0:F, cols]
            adj[x + 1, tile_at(k + 1), :] = out[F:, cols]
        return carry

    lax.fori_loop(0, 16, plane, 0)
    for part_at in range(6):
        out = combine((128 + 8 * part_at) * LANES, 8 * LANES)
        for k in range(8):
            value = out[F:, k * LANES : (k + 1) * LANES]
            if part_at < 2:
                adj[1 + 8 * part_at + k, tile_at(0), :] = value
            elif part_at < 4:
                adj[1 + 8 * (part_at - 2) + k, tile_at(9), :] = value
            else:
                adj[17 * (part_at - 4), tile_at(k + 1), :] = value

    lane = lane_ids(F)

    def sens_plane(x, carry):
        b, a = bg[x, tile_at(1), :], adj[x, tile_at(1), :]
        before = (b - bg[x, tile_at(0), :]) * (a - adj[x, tile_at(0), :])
        for k in range(1, 9):
            bn, an = bg[x, tile_at(k + 1), :], adj[x, tile_at(k + 1), :]
            after = (bn - b) * (an - a)
            total = before + after
            for s in (x - 1, x + 1):
                total = total + (bg[s, tile_at(k), :] - b) * (adj[s, tile_at(k), :] - a)
            own = b * a
            up = (pltpu.roll(b, LANES - 1, 1) - b) * (pltpu.roll(a, LANES - 1, 1) - a)
            up = jnp.where(lane == LANES - 1, own, up)
            down = jnp.where(lane == 0, own, pltpu.roll(up, 1, 1))
            total = total + (up + down)
            sens_ref[x - 1, k - 1 : k, :] = -0.5 * jnp.sum(total, axis=0, keepdims=True)
            before, b, a = after, bn, an
        return carry

    lax.fori_loop(1, 17, sens_plane, 0)


def final(pattern, parts, own, left, right, low, high, s, damping):
    anywhere = pl.BlockSpec(memory_space=pl.ANY)
    vmem = pl.BlockSpec(memory_space=pltpu.VMEM)

    def kernel(*refs):
        final_kernel(*refs, damping=damping)

    return pl.pallas_call(
        kernel,
        out_shape=(
            jax.ShapeDtypeStruct((2048, LANES), jnp.float32),
            jax.ShapeDtypeStruct((16, 8, LANES), jnp.float32),
        ),
        in_specs=[pl.BlockSpec(memory_space=pltpu.SMEM), vmem] + [anywhere] * 6,
        scratch_shapes=[
            pltpu.VMEM((18, 160, LANES), jnp.float32),
            pltpu.VMEM((18, 160, LANES), jnp.float32),
            pltpu.VMEM((160, CELLS), jnp.bfloat16),
            pltpu.SemaphoreType.DMA((6,)),
        ],
        compiler_params=pltpu.CompilerParams(vmem_limit_bytes=40 * 2**20),
        name="final",
    )(pattern, parts, own, left, right, low, high, s)


def spread(block, axis, count, groups=None):
    copies = jnp.broadcast_to(block[None], (count,) + block.shape)
    return lax.all_to_all(copies, axis, 0, 0, axis_index_groups=groups)


def on_device(background, conductivity, perturbation, electrodes, pattern):
    size_x, size_y, size_z = conductivity.shape
    count_x, count_y = lax.axis_size("gx"), lax.axis_size("gy")
    up_y = [(i, i + 1) for i in range(count_y - 1)]
    up_x = [(i, i + 1) for i in range(count_x - 1)]
    down_y, down_x = [(j, i) for i, j in up_y], [(j, i) for i, j in up_x]
    own, up, down = pack(background.reshape(-1, size_z), conductivity, perturbation)
    left = lax.ppermute(up, "gy", up_y)
    right = lax.ppermute(down, "gy", down_y)
    up, down = pack_x(own, left, right)
    low = lax.ppermute(up, "gx", up_x)
    high = lax.ppermute(down, "gx", down_x)
    s, pay = krylov(electrodes, own, left, right, low, high)
    pay = pay + lax.ppermute(pay, "gy", [(i, i ^ 1) for i in range(count_y)])
    pay = jnp.sum(spread(pay, "gx", count_x), axis=0)
    chips = count_y // 2
    groups = [[2 * i + core for i in range(chips)] for core in range(2)]
    parts = spread(pay, "gy", chips, groups)
    cells = size_x * size_y * size_z * count_x * count_y
    tangent, sens = final(
        pattern, parts, own, left, right, low, high, s, 80.0 / math.sqrt(cells)
    )
    return tangent.reshape(background.shape), sens


def solution(mesh):
    in_specs = (P(None, "gx", "gy", None), P("gx", "gy", None), P("gx", "gy", None), P(), P())
    out_specs = (P(None, "gx", "gy", None), P("gx", "gy", None))
    return jax.shard_map(
        on_device, mesh=mesh, in_specs=in_specs, out_specs=out_specs, check_vma=False
    )
```

```python
import math

import jax
import jax.numpy as jnp
from jax import lax
from jax.experimental import pallas as pl
from jax.experimental.pallas import tpu as pltpu
from jax.sharding import PartitionSpec as P

SHIFT = 12.0
F = 16
LANES = 128
HALO = 4
HIGHEST = lax.Precision.HIGHEST
V0, V1, V2, E0, E1, V3, E2 = 0, 32, 64, 96, 112, 144, 176
KEPT, ALL_ROWS = 144, 208
WIDE = 10 * LANES
MB = 2**20


def tile_at(y):
    return slice(y * F, (y + 1) * F)


def run_copies(pairs, sems, first=0):
    copies = [
        pltpu.make_async_copy(s, d, sems.at[first + i]) for i, (s, d) in enumerate(pairs)
    ]
    for c in copies:
        c.start()
    return copies


def wait_all(copies):
    for c in copies:
        c.wait()


def odd(axis):
    return lax.rem(lax.axis_index(axis), 2) == 1


def pack_kernel(bg_hbm, cond_hbm, pert_hbm, own_ref, core_ref, chip_ref, bg, cond_v, pert_v, sems):
    size_x, size_y = cond_v.shape[0], cond_v.shape[1]
    pairs = [(cond_hbm, cond_v), (pert_hbm, pert_v), (bg_hbm, bg)]
    wait_all(run_copies(pairs, sems))

    def fill(top_ref, bottom_ref):
        def plane(x, carry):
            for y in range(size_y):
                tile = bg[pl.ds(x * size_y + y, F, stride=size_x * size_y), :]
                own_ref[x, tile_at(y), :] = tile
                if y >= size_y - HALO:
                    top_ref[x, tile_at(y - size_y + HALO), :] = tile
                if y < HALO:
                    bottom_ref[x, tile_at(y), :] = tile
            cond, pert = cond_v[x], pert_v[x]
            own_ref[x, 128:136, :] = cond
            own_ref[x, 136:144, :] = pert
            top_ref[x, 64:72, :] = jnp.concatenate([cond[4:8], pert[4:8]], axis=0)
            bottom_ref[x, 64:72, :] = jnp.concatenate([cond[0:4], pert[0:4]], axis=0)
            return carry

        lax.fori_loop(0, size_x, plane, 0, unroll=4)

    @pl.when(odd("gy"))
    def _():
        fill(chip_ref, core_ref)

    @pl.when(jnp.logical_not(odd("gy")))
    def _():
        fill(core_ref, chip_ref)


def pack(background, conductivity, perturbation):
    shape = jax.ShapeDtypeStruct
    anywhere = pl.BlockSpec(memory_space=pl.ANY)
    return pl.pallas_call(
        pack_kernel,
        out_shape=(
            shape((16, 144, LANES), jnp.float32),
            shape((16, 72, LANES), jnp.float32),
            shape((16, 72, LANES), jnp.float32),
        ),
        in_specs=[anywhere] * 3,
        scratch_shapes=[
            pltpu.VMEM((2048, LANES), jnp.float32),
            pltpu.VMEM((16, 8, LANES), jnp.float32),
            pltpu.VMEM((16, 8, LANES), jnp.float32),
            pltpu.SemaphoreType.DMA((3,)),
        ],
        compiler_params=pltpu.CompilerParams(vmem_limit_bytes=16 * MB),
        name="pack_y",
    )(background, conductivity, perturbation)


def edge_layout():
    table, at = [], 0
    for dx in range(1, HALO + 1):
        table.append((dx, 16 - dx, at))
        at += (16 - 2 * dx) * F + 32
    return table, at


EDGE, EDGE_ROWS = edge_layout()


def pack_x_kernel(own_ref, core_ref, chip_ref, a_ref, b_ref, sems):
    odd_x = odd("gx")

    def send(left_ref, right_ref):
        pairs = []
        for out, up in ((a_ref, jnp.logical_not(odd_x)), (b_ref, odd_x)):
            for y0, y1, at in EDGE:
                x = jnp.where(up, 16 - y0, y0 - 1)
                pieces = []
                if y0 < 4:
                    pieces.append((left_ref, y0 * F, 64))
                pieces.append((own_ref, 0, 128))
                if y1 > 12:
                    pieces.append((right_ref, 0, (y1 - 12) * F))
                pieces += [(own_ref, 128, 144), (left_ref, 64, 72), (right_ref, 64, 72)]
                for ref, a, b in pieces:
                    pairs.append((ref.at[x, pl.ds(a, b - a)], out.at[pl.ds(at, b - a)]))
                    at += b - a
        wait_all(run_copies(pairs, sems))

    @pl.when(odd("gy"))
    def _():
        send(core_ref, chip_ref)

    @pl.when(jnp.logical_not(odd("gy")))
    def _():
        send(chip_ref, core_ref)


def pack_x(own, core, chip):
    shape = jax.ShapeDtypeStruct((EDGE_ROWS, LANES), jnp.float32)
    anywhere = pl.BlockSpec(memory_space=pl.ANY)
    return pl.pallas_call(
        pack_x_kernel,
        out_shape=(shape, shape),
        in_specs=[anywhere] * 3,
        out_specs=(anywhere, anywhere),
        scratch_shapes=[pltpu.SemaphoreType.DMA((44,))],
        compiler_params=pltpu.CompilerParams(vmem_limit_bytes=2 * MB),
        name="pack_x",
    )(own, core, chip)


def lane_ids(rows):
    return lax.broadcasted_iota(jnp.int32, (rows, LANES), 1)


def own_copies(own_ref, core_ref, chip_ref, bext, ranges):
    odd_y = odd("gy")
    core_at = pl.multiple_of(jnp.where(odd_y, 0, 192), 8)
    chip_at = pl.multiple_of(jnp.where(odd_y, 192, 0), 8)
    core_c = pl.multiple_of(jnp.where(odd_y, 272, 280), 8)
    chip_c = pl.multiple_of(jnp.where(odd_y, 280, 272), 8)
    pairs = []
    for first, count, place in ranges:
        src, dst = pl.ds(first, count), pl.ds(place, count)
        pairs += [
            (own_ref.at[src, pl.ds(128, 16)], bext.at[dst, pl.ds(256, 16)]),
            (core_ref.at[src, pl.ds(64, 8)], bext.at[dst, pl.ds(core_c, 8)]),
            (chip_ref.at[src, pl.ds(64, 8)], bext.at[dst, pl.ds(chip_c, 8)]),
            (own_ref.at[src, pl.ds(0, 128)], bext.at[dst, pl.ds(64, 128)]),
            (core_ref.at[src, pl.ds(0, 64)], bext.at[dst, pl.ds(core_at, 64)]),
            (chip_ref.at[src, pl.ds(0, 64)], bext.at[dst, pl.ds(chip_at, 64)]),
        ]
    return pairs


def faces(bext, planes, ccoef, pcoef):
    lane = lane_ids(16)
    last = lane == LANES - 1
    edge = (lane == 0) | last

    def cells(x):
        own, left, right = bext[x, 256:272, :], bext[x, 272:280, :], bext[x, 280:288, :]
        return (
            jnp.concatenate([left[0:4], own[0:8], right[0:4]], axis=0),
            jnp.concatenate([left[4:8], own[8:16], right[4:8]], axis=0),
        )

    def plane(x):
        now, then = cells(x), cells(x + 1)
        for coef, c, n, half, base in (
            (ccoef, now[0], then[0], 0.5, 0.05 - SHIFT),
            (pcoef, now[1], then[1], -0.5, 0.0),
        ):
            fx, fy, fu, fd, dd = coef
            fx[x] = half * (c + n)
            fy[x] = half * (c + pltpu.roll(c, 15, 0))
            up = jnp.where(last, 0.0, half * (c + pltpu.roll(c, LANES - 1, 1)))
            fu[x] = up
            fd[x] = pltpu.roll(up, 1, 1)
            dd[x] = base + jnp.where(edge, half * c, 0.0)

    for x in planes:
        plane(x)


def stencil_plane(src, coeffs, x, y0, y1, mask_x, mask_y, emit):
    fx, fy, fu, fd, dd = coeffs
    q = src[x, tile_at(y0), :]
    flux = fy[x, y0 - 1 : y0, :] * (q - src[x, tile_at(y0 - 1), :])
    for y in range(y0, y1):
        nxt = src[x, tile_at(y + 1), :]
        row = slice(y, y + 1)
        later = fy[x, row, :] * (nxt - q)
        out = dd[x, row, :] * q + (flux - later)
        out = out + fx[x - 1, row, :] * (q - src[x - 1, tile_at(y), :])
        out = out - fx[x, row, :] * (src[x + 1, tile_at(y), :] - q)
        out = out + fd[x, row, :] * (q - pltpu.roll(q, 1, 1))
        out = out - fu[x, row, :] * (pltpu.roll(q, LANES - 1, 1) - q)
        mask = mask_x
        if y < 4:
            mask = mask_y[0] if mask is None else mask * mask_y[0]
        elif y >= 12:
            mask = mask_y[1] if mask is None else mask * mask_y[1]
        if mask is not None:
            out = out * mask
        emit(y, out)
        flux, q = later, nxt


def put_split(s_ref, i, row, y, value, exact=False):
    lanes = slice((y - 3) * LANES, (y - 2) * LANES)
    hi = value.astype(jnp.bfloat16)
    s_ref[i, row : row + F, lanes] = hi
    if not exact:
        lo = (value - hi.astype(jnp.float32)).astype(jnp.bfloat16)
        s_ref[i, row + F : row + 2 * F, lanes] = lo


def electrode_ids(elec_ref):
    sub = lax.broadcasted_iota(jnp.int32, (F, LANES), 0)
    ids = jnp.zeros((F, LANES), jnp.int32)
    for e in range(F):
        ids = jnp.where(sub == e, elec_ref[e], ids)
    return ids - lane_ids(F)


def grid_masks():
    one, zero = jnp.float32(1), jnp.float32(0)
    masks = []
    for axis in ("gx", "gy"):
        i = lax.axis_index(axis)
        low, high = i > 0, i < lax.axis_size(axis) - 1
        masks.append((jnp.where(low, one, zero), jnp.where(high, one, zero)))
    return masks


def unit_plane(ids, at_x, e0, i, s_ref, s_at, y_kept):
    size_x, size_y = 16 * lax.axis_size("gx"), 8 * lax.axis_size("gy")
    good_x = (at_x >= 0) & (at_x < size_x)
    for y in range(2, 14):
        at_y = lax.axis_index("gy") * 8 + y - 4
        good = good_x & (at_y >= 0) & (at_y < size_y)
        here = jnp.where(good, (at_x * size_y + at_y) * LANES, -(2**20))
        value = jnp.where(ids == here, 1.0, 0.0)
        e0[i, tile_at(y), :] = value
        if y_kept[0] <= y < y_kept[1]:
            put_split(s_ref, s_at, E0, y, value, exact=True)


def gram_of(s_ref, i):
    return lax.dot_general(
        s_ref[i, 0:KEPT, LANES : 9 * LANES],
        s_ref[i, :, LANES : 9 * LANES],
        (((1,), (1,)), ((), ())),
        preferred_element_type=jnp.float32,
    )


def inner_kernel(
    elec_ref, own_ref, core_ref, chip_ref, s_hbm, band_hbm, gram_ref,
    bext, v0, v1, v2, e0, e1, s_ref, cx, cy, cu, cd, cr, px, py, pu, pd, pr, sems, out_sems,
):
    copies = run_copies(own_copies(own_ref, core_ref, chip_ref, bext, [(0, 16, 0)]), sems)
    gx = lax.axis_index("gx")
    _, mask_y = grid_masks()
    ids = electrode_ids(elec_ref)

    def units(x, carry):
        unit_plane(ids, gx * 16 + x, e0, x, s_ref, x, (3, 13))
        return carry

    lax.fori_loop(2, 14, units, 0)
    wait_all(copies[:3])
    ccoef, pcoef = (cx, cy, cu, cd, cr), (px, py, pu, pd, pr)
    faces(bext, range(15), ccoef, pcoef)
    wait_all(copies[3:])

    def sweep(src, dst, coeffs, first, reach, row, keep):
        def plane(x, carry):
            def emit(y, out):
                if dst is not None:
                    dst[x, tile_at(y), :] = out
                if keep[0] <= y < keep[1]:
                    put_split(s_ref, x, row, y, out)

            stencil_plane(src, coeffs, x, 4 - reach, 12 + reach, None, mask_y, emit)
            return carry

        lax.fori_loop(first, 16 - first, plane, 0, unroll=2)

    def save(first, row, rows, at):
        count = 16 - 2 * first
        pair = (
            s_ref.at[pl.ds(first, count), pl.ds(row, rows)],
            s_hbm.at[pl.ds(first + 1, count), pl.ds(row, rows)],
        )
        return run_copies([pair], out_sems, at)

    def save_band(src, first, at):
        pairs = [
            (src.at[pl.ds(x, 2)], band_hbm.at[pl.ds(2 * at + 2 * k, 2)])
            for k, x in enumerate((first, 14 - first))
        ]
        return run_copies(pairs, out_sems, 4 + at)

    sweep(bext, v0, pcoef, 1, 3, V0, (3, 13))
    outs = save(1, V0, 32, 0) + save_band(v0, 1, 0)
    sweep(v0, v1, ccoef, 2, 2, V1, (3, 13))
    outs += save(2, V1, 32, 1) + save_band(v1, 2, 2)
    sweep(v1, v2, ccoef, 3, 1, V2, (3, 13))
    outs += save(3, V2, 32, 2) + save_band(v2, 3, 4)
    sweep(e0, e1, ccoef, 3, 1, E1, (3, 13))
    outs += save(4, E0, 48, 3)
    sweep(v2, None, ccoef, 4, 0, V3, (4, 12))
    sweep(e1, None, ccoef, 4, 0, E2, (4, 12))

    gram_ref[...] = gram_of(s_ref, 4)

    def gram_step(x, carry):
        gram_ref[...] += gram_of(s_ref, x)
        return carry

    lax.fori_loop(5, 12, gram_step, 0)
    wait_all(outs)


def inner(electrodes, own, core, chip):
    anywhere = pl.BlockSpec(memory_space=pl.ANY)
    vmem = pl.BlockSpec(memory_space=pltpu.VMEM)
    field = pltpu.VMEM((16, 256, LANES), jnp.float32)
    coeff = pltpu.VMEM((16, 16, LANES), jnp.float32)
    return pl.pallas_call(
        inner_kernel,
        out_shape=(
            jax.ShapeDtypeStruct((18, KEPT, WIDE), jnp.bfloat16),
            jax.ShapeDtypeStruct((12, 256, LANES), jnp.float32),
            jax.ShapeDtypeStruct((KEPT, ALL_ROWS), jnp.float32),
        ),
        in_specs=[pl.BlockSpec(memory_space=pltpu.SMEM)] + [anywhere] * 3,
        out_specs=(anywhere, anywhere, vmem),
        scratch_shapes=[pltpu.VMEM((16, 288, LANES), jnp.float32)]
        + [field] * 5
        + [pltpu.VMEM((16, ALL_ROWS, WIDE), jnp.bfloat16)]
        + [coeff] * 10
        + [pltpu.SemaphoreType.DMA((6,)), pltpu.SemaphoreType.DMA((10,))],
        compiler_params=pltpu.CompilerParams(vmem_limit_bytes=32 * MB),
        cost_estimate=pl.CostEstimate(
            flops=4 * 10**9, bytes_accessed=16 * 10**6, transcendentals=0
        ),
        name="inner",
    )(electrodes, own, core, chip)


def edge_kernel(
    elec_ref, own_ref, core_ref, chip_ref, a_ref, b_ref, band_ref, first_gram, s_in,
    s_hbm, pay_ref,
    bext, v0, v1, v2, e0, e1, s_ref, gram, cx, cy, cu, cd, cr, px, py, pu, pd, pr, sems, out_sems,
):
    odd_x = odd("gx")
    pairs = own_copies(own_ref, core_ref, chip_ref, bext, [(0, 6, 4), (10, 6, 10)])
    coef_pairs, field_pairs = pairs[0:3] + pairs[6:9], pairs[3:6] + pairs[9:12]
    for ref, high in ((a_ref, jnp.logical_not(odd_x)), (b_ref, odd_x)):
        for y0, y1, at in EDGE:
            count = (y1 - y0) * F
            to = jnp.where(high, 15 + y0, 4 - y0)
            coef_pairs.append((ref.at[pl.ds(at + count, 32)], bext.at[to, pl.ds(256, 32)]))
            field_pairs.append((ref.at[pl.ds(at, count)], bext.at[to, pl.ds(y0 * F, count)]))
    band_pairs = [
        (band_ref.at[pl.ds(2 * k, 2)], dst.at[pl.ds(to, 2)])
        for k, (dst, to) in enumerate(((v0, 5), (v0, 13), (v1, 6), (v1, 12), (v2, 7), (v2, 11)))
    ]
    s_pairs = []
    for row, count in ((V0, 3), (V1, 2), (V2, 1)):
        rows = pl.ds(row, 32)
        for src, to in ((5 - count, 5 - count), (13, 5)):
            s_pairs.append(
                (s_in.at[pl.ds(src, count), rows], s_ref.at[pl.ds(to, count), rows])
            )
    coef_copies = run_copies(coef_pairs, sems)
    at = len(coef_pairs)
    field_copies = run_copies(field_pairs, sems, at)
    at += len(field_pairs)
    band_copies = run_copies(band_pairs, sems, at)
    at += len(band_pairs)
    s_copies = run_copies(s_pairs, sems, at)

    gx = lax.axis_index("gx")
    mask_x, mask_y = grid_masks()
    ids = electrode_ids(elec_ref)

    def x_of(l):
        return l - 4 if l < 10 else l

    def keep_of(l):
        x = x_of(l)
        i = x + 1 if l < 10 else x - 7
        if x in (-1, 16):
            return i, (4, 12)
        if -1 < x < 4 or 11 < x < 16:
            return i, (3, 13)
        return 0, (99, 99)

    for l in list(range(2, 10)) + list(range(10, 18)):
        i, keep = keep_of(l)
        unit_plane(ids, gx * 16 + x_of(l), e0, l, s_ref, i, keep)
    wait_all(coef_copies)
    ccoef, pcoef = (cx, cy, cu, cd, cr), (px, py, pu, pd, pr)
    faces(bext, list(range(9)) + list(range(10, 19)), ccoef, pcoef)
    wait_all(field_copies)

    def sweep(src, dst, coeffs, reach, planes, row, rows_kept=None):
        for l in planes:
            x = x_of(l)
            out_by = max(0, -x, x - 15)
            mask = mask_x[0] if x < 0 else mask_x[1] if x > 15 else None
            i, keep = keep_of(l)
            keep = rows_kept or keep

            def emit(y, out, l=l, i=i, keep=keep):
                if dst is not None:
                    dst[l, tile_at(y), :] = out
                if keep[0] <= y < keep[1]:
                    put_split(s_ref, i, row, y, out)

            near = reach - out_by
            stencil_plane(src, coeffs, l, 4 - near, 12 + near, mask, mask_y, emit)

    def sides(low, count):
        return [x + 4 for x in range(low, low + count)] + [15 - x for x in range(low, low + count)]

    def save(row, rows, count, at):
        pairs = [
            (s_ref.at[pl.ds(i, count), pl.ds(row, rows)], s_hbm.at[pl.ds(o, count), pl.ds(row, rows)])
            for i, o in ((0, 0), (10 - count, 18 - count))
        ]
        return run_copies(pairs, out_sems, at)

    sweep(bext, v0, pcoef, 3, sides(-3, 4), V0)
    outs = save(V0, 32, 2, 0)
    wait_all(band_copies)
    sweep(v0, v1, ccoef, 2, sides(-2, 4), V1)
    outs += save(V1, 32, 3, 2)
    sweep(v1, v2, ccoef, 1, sides(-1, 4), V2)
    outs += save(V2, 32, 4, 4)
    sweep(e0, e1, ccoef, 1, sides(-1, 6), E1)
    outs += save(E0, 48, 5, 6)
    sweep(v2, None, ccoef, 0, sides(0, 4), V3, (4, 12))
    sweep(e1, None, ccoef, 0, sides(0, 4), E2, (4, 12))
    wait_all(s_copies)

    gram[...] = first_gram[...]

    def gram_step(i, carry):
        gram[...] += gram_of(s_ref, i)
        return carry

    lax.fori_loop(1, 9, gram_step, 0)

    def rows_of(row):
        if row == E0:
            return gram[row : row + F, :]
        return gram[row : row + F, :] + gram[row + F : row + 2 * F, :]

    summed = {row: rows_of(row) for row in (V0, V1, V2, E0, E1)}

    def block(row, col):
        rows = summed[row]
        if col == E0:
            return rows[:, col : col + F]
        return rows[:, col : col + F] + rows[:, col + F : col + 2 * F]

    order = [
        (V0, V0), (V0, V1), (V1, V1), (V1, V2), (V2, V2), (V2, V3), (V0, E0), (V1, E0),
        (V2, E0), (E0, V3), (E1, V3), (E0, E0), (E0, E1), (E1, E1), (E1, E2),
    ]
    blocks = [block(r, c) for r, c in order] + [jnp.zeros((F, F), jnp.float32)]
    pay_ref[0:16, :] = jnp.concatenate(blocks[:8], axis=1)
    pay_ref[16:32, :] = jnp.concatenate(blocks[8:], axis=1)
    wait_all(outs)


def edge(electrodes, own, core, chip, a, b, band, gram, s):
    anywhere = pl.BlockSpec(memory_space=pl.ANY)
    vmem = pl.BlockSpec(memory_space=pltpu.VMEM)
    field = pltpu.VMEM((20, 256, LANES), jnp.float32)
    coeff = pltpu.VMEM((20, 16, LANES), jnp.float32)
    return pl.pallas_call(
        edge_kernel,
        out_shape=(
            jax.ShapeDtypeStruct((18, KEPT, WIDE), jnp.bfloat16),
            jax.ShapeDtypeStruct((32, LANES), jnp.float32),
        ),
        in_specs=[pl.BlockSpec(memory_space=pltpu.SMEM)] + [anywhere] * 6 + [vmem, anywhere],
        out_specs=(anywhere, vmem),
        scratch_shapes=[pltpu.VMEM((20, 288, LANES), jnp.float32)]
        + [field] * 5
        + [
            pltpu.VMEM((10, ALL_ROWS, WIDE), jnp.bfloat16),
            pltpu.VMEM((KEPT, ALL_ROWS), jnp.float32),
        ]
        + [coeff] * 10
        + [pltpu.SemaphoreType.DMA((40,)), pltpu.SemaphoreType.DMA((8,))],
        input_output_aliases={8: 0},
        compiler_params=pltpu.CompilerParams(vmem_limit_bytes=32 * MB),
        name="edge",
    )(electrodes, own, core, chip, a, b, band, gram, s)


def matmul(a, b, dims=((1,), (0,))):
    return lax.dot_general(
        a, b, (dims, ((), ())), precision=HIGHEST, preferred_element_type=jnp.float32
    )


def galerkin(m0, m1, m2, m3):
    a12 = m2 + SHIFT * m1
    work = jnp.concatenate(
        [
            jnp.concatenate([m1 + SHIFT * m0, a12, m0], axis=1),
            jnp.concatenate([a12, m3 + SHIFT * m2, m1], axis=1),
        ],
        axis=0,
    )
    sub = lax.broadcasted_iota(jnp.int32, work.shape, 0)
    for k in range(2 * F):
        row = work[k : k + 1, :]
        row = row / row[:, k : k + 1]
        work = jnp.where(sub == k, row, work - work[:, k : k + 1] * row)
    return work[:, 2 * F :]


def final_kernel(
    pattern_ref, parts_ref, own_ref, core_ref, chip_ref, a_ref, b_ref, s_hbm,
    out_ref, sens_ref, bg, adj, s_ref, sems, *, damping,
):
    odd_x, odd_y = odd("gx"), odd("gy")

    def y_rows(is_left):
        src = pl.multiple_of(jnp.where(is_left, 48, 0), 8)
        dst = pl.multiple_of(jnp.where(is_left, 0, 144), 8)
        return pl.ds(src, 16), pl.ds(dst, 16)

    planes = pl.ds(1, 16)
    core_src, core_dst = y_rows(odd_y)
    chip_src, chip_dst = y_rows(jnp.logical_not(odd_y))
    near = pl.ds(3 * F, 128)
    pairs = [
        (s_hbm, s_ref),
        (own_ref.at[:, pl.ds(0, 128)], bg.at[planes, pl.ds(16, 128)]),
        (core_ref.at[:, core_src], bg.at[planes, core_dst]),
        (chip_ref.at[:, chip_src], bg.at[planes, chip_dst]),
        (a_ref.at[near], bg.at[jnp.where(odd_x, 0, 17), pl.ds(16, 128)]),
        (b_ref.at[near], bg.at[jnp.where(odd_x, 17, 0), pl.ds(16, 128)]),
    ]
    copies = run_copies(pairs, sems)

    total = jnp.sum(parts_ref[...], axis=0)

    def part(k):
        r, c = (k // 8) * F, (k % 8) * F
        return total[r : r + F, c : c + F]

    m = [part(k) for k in range(6)]
    p = [part(6), part(7), part(8), part(9).T, part(10).T]
    e = [part(k) for k in range(11, 15)]
    y = galerkin(*m[:4])
    y0, y1 = y[0:F], y[F:]
    probe = matmul(y0, p[0], ((0,), (0,))) + matmul(y1, p[1], ((0,), (0,)))
    lane = lax.broadcasted_iota(jnp.int32, (F, F), 1)
    sub = lax.broadcasted_iota(jnp.int32, (F, F), 0)
    first, second = jnp.zeros((F, F), jnp.int32), jnp.zeros((F, F), jnp.int32)
    for i in range(F):
        first = jnp.where(sub == i, pattern_ref[i, 0], first)
        second = jnp.where(sub == i, pattern_ref[i, 1], second)
    pairing = jnp.where(lane == first, 1.0, 0.0) - jnp.where(lane == second, 1.0, 0.0)
    measured = matmul(probe, pairing, ((1,), (1,)))
    weight = 8.0 * matmul(measured, pairing)
    z = jnp.concatenate([damping * y0, damping * y1, weight.T], axis=0)
    rows = []
    for k in range(4):
        rows.append(jnp.concatenate([m[k], m[k + 1], p[k]], axis=1))
        rows.append(jnp.concatenate([m[k + 1], m[k + 2], p[k + 1]], axis=1))
        rows.append(jnp.concatenate([p[k].T, p[k + 1].T, e[k]], axis=1))
    nz = matmul(jnp.concatenate(rows, axis=0), z)
    moments = [matmul(z, nz[48 * k : 48 * (k + 1)], ((0,), (0,))) for k in range(4)]
    q = galerkin(*moments)
    z0, z1 = matmul(z, q[0:F]), matmul(z, q[F:])
    none = jnp.zeros((F, F), jnp.float32)
    mix = [
        jnp.concatenate([y0, z0[0:F]], axis=1),
        jnp.concatenate([y1, z0[F : 2 * F] + z1[0:F]], axis=1),
        jnp.concatenate([none, z1[F : 2 * F]], axis=1),
        jnp.concatenate([none, z0[2 * F :]], axis=1),
        jnp.concatenate([none, z1[2 * F :]], axis=1),
    ]
    mix = [mix[i] for i in (0, 0, 1, 1, 2, 2, 3, 4, 4)]
    mix = jnp.concatenate(mix, axis=0).T
    hi = mix.astype(jnp.bfloat16)
    lo = (mix - hi.astype(jnp.float32)).astype(jnp.bfloat16)
    both = jnp.concatenate([hi, lo], axis=0)
    wait_all(copies)

    def combine(x, lanes):
        out = jnp.dot(both, s_ref[x, :, lanes], preferred_element_type=jnp.float32)
        return out[0:32] + out[32:64]

    def plane(x, carry):
        out = combine(x, slice(0, WIDE))
        for k in range(10):
            cols = slice(k * LANES, (k + 1) * LANES)
            if 0 < k < 9:
                out_ref[pl.ds(x * 8 + k - 9, F, stride=128), :] = out[0:F, cols]
            adj[x, tile_at(k), :] = out[F:, cols]
        return carry

    lax.fori_loop(1, 17, plane, 0)
    for x in (0, 17):
        out = combine(x, slice(LANES, 9 * LANES))
        for k in range(8):
            adj[x, tile_at(k + 1), :] = out[F:, k * LANES : (k + 1) * LANES]

    lane = lane_ids(F)

    def sens_plane(x, carry):
        b, a = bg[x, tile_at(1), :], adj[x, tile_at(1), :]
        before = (b - bg[x, tile_at(0), :]) * (a - adj[x, tile_at(0), :])
        for k in range(1, 9):
            bn, an = bg[x, tile_at(k + 1), :], adj[x, tile_at(k + 1), :]
            after = (bn - b) * (an - a)
            total = before + after
            for s in (x - 1, x + 1):
                total = total + (bg[s, tile_at(k), :] - b) * (adj[s, tile_at(k), :] - a)
            bu = jnp.where(lane == LANES - 1, 0.0, pltpu.roll(b, LANES - 1, 1))
            au = jnp.where(lane == LANES - 1, 0.0, pltpu.roll(a, LANES - 1, 1))
            bd = jnp.where(lane == 0, 0.0, pltpu.roll(b, 1, 1))
            ad = jnp.where(lane == 0, 0.0, pltpu.roll(a, 1, 1))
            total = total + (bu - b) * (au - a) + (bd - b) * (ad - a)
            sens_ref[x - 1, k - 1 : k, :] = -0.5 * jnp.sum(total, axis=0, keepdims=True)
            before, b, a = after, bn, an
        return carry

    lax.fori_loop(1, 17, sens_plane, 0, unroll=2)


def final(pattern, parts, own, core, chip, a, b, s, damping):
    anywhere = pl.BlockSpec(memory_space=pl.ANY)
    vmem = pl.BlockSpec(memory_space=pltpu.VMEM)

    def kernel(*refs):
        final_kernel(*refs, damping=damping)

    return pl.pallas_call(
        kernel,
        out_shape=(
            jax.ShapeDtypeStruct((2048, LANES), jnp.float32),
            jax.ShapeDtypeStruct((16, 8, LANES), jnp.float32),
        ),
        in_specs=[pl.BlockSpec(memory_space=pltpu.SMEM), vmem] + [anywhere] * 6,
        scratch_shapes=[
            pltpu.VMEM((18, 160, LANES), jnp.float32),
            pltpu.VMEM((18, 160, LANES), jnp.float32),
            pltpu.VMEM((18, KEPT, WIDE), jnp.bfloat16),
            pltpu.SemaphoreType.DMA((6,)),
        ],
        compiler_params=pltpu.CompilerParams(vmem_limit_bytes=56 * MB),
        name="final",
    )(pattern, parts, own, core, chip, a, b, s)


def spread(block, axis, count, groups=None):
    copies = jnp.broadcast_to(block[None], (count,) + block.shape)
    return lax.all_to_all(copies, axis, 0, 0, axis_index_groups=groups)


def swaps(first, count):
    lows = range(first, count - 1, 2)
    return [(i, i + 1) for i in lows] + [(i + 1, i) for i in lows]


def on_device(background, conductivity, perturbation, electrodes, pattern):
    size_x, size_y, size_z = conductivity.shape
    count_x, count_y = lax.axis_size("gx"), lax.axis_size("gy")
    flat = background.reshape(-1, size_z)
    own, core, chip = pack(flat, conductivity, perturbation)
    chip = lax.ppermute(chip, "gy", swaps(1, count_y))
    core = lax.ppermute(core, "gy", swaps(0, count_y))
    a, b = pack_x(own, core, chip)
    a = lax.ppermute(a, "gx", swaps(0, count_x))
    b = lax.ppermute(b, "gx", swaps(1, count_x))
    s, band, gram = inner(electrodes, own, core, chip)
    s, pay = edge(electrodes, own, core, chip, a, b, band, gram, s)
    pay = pay + lax.ppermute(pay, "gy", swaps(0, count_y))
    pay = jnp.sum(spread(pay, "gx", count_x), axis=0)
    chips = count_y // 2
    groups = [[2 * i + c for i in range(chips)] for c in range(2)]
    parts = spread(pay, "gy", chips, groups)
    cells = size_x * size_y * size_z * count_x * count_y
    damping = 80.0 / math.sqrt(cells)
    tangent, sens = final(pattern, parts, own, core, chip, a, b, s, damping)
    return tangent.reshape(background.shape), sens


def solution(mesh):
    in_specs = (P(None, "gx", "gy", None), P("gx", "gy", None), P("gx", "gy", None), P(), P())
    out_specs = (P(None, "gx", "gy", None), P("gx", "gy", None))
    return jax.shard_map(
        on_device, mesh=mesh, in_specs=in_specs, out_specs=out_specs, check_vma=False
    )
```

```python
import math

import jax
import jax.numpy as jnp
from jax import lax
from jax.experimental import pallas as pl
from jax.experimental.pallas import tpu as pltpu
from jax.sharding import PartitionSpec as P

SHIFT = 12.0
F = 16
LANES = 128
HALO = 4
HIGHEST = lax.Precision.HIGHEST
V0, V1, V2, E0, E1, V3, E2 = 0, 32, 64, 96, 112, 144, 176
KEPT, ALL_ROWS = 144, 208
WIDE = 10 * LANES
MB = 2**20


def tile_at(y):
    return slice(y * F, (y + 1) * F)


def run_copies(pairs, sems, first=0):
    copies = [
        pltpu.make_async_copy(s, d, sems.at[first + i]) for i, (s, d) in enumerate(pairs)
    ]
    for c in copies:
        c.start()
    return copies


def wait_all(copies):
    for c in copies:
        c.wait()


def odd(axis):
    return lax.rem(lax.axis_index(axis), 2) == 1


PARTS = 4


def pack_kernel(
    bg_hbm, cond_hbm, pert_hbm, own_ref, core_ref, chip_ref, a_ref, b_ref,
    bg, cond_v, pert_v, sems,
):
    size_x, size_y = cond_v.shape[0], cond_v.shape[1]
    each = size_x // PARTS
    pairs = [(cond_hbm, cond_v), (pert_hbm, pert_v)]
    for i in range(PARTS):
        planes = pl.ds(i * each, each)
        pairs.append((bg_hbm.at[:, planes], bg.at[:, planes]))
    copies = run_copies(pairs, sems)

    def fill(top_ref, bottom_ref):
        wait_all(copies[:2])

        def plane(x, carry):
            for y in range(size_y):
                tile = bg[:, x, y, :]
                own_ref[x, tile_at(y), :] = tile
                if y >= size_y - HALO:
                    top_ref[x, tile_at(y - size_y + HALO), :] = tile
                if y < HALO:
                    bottom_ref[x, tile_at(y), :] = tile
            cond, pert = cond_v[x], pert_v[x]
            own_ref[x, 128:136, :] = cond
            own_ref[x, 136:144, :] = pert
            top_ref[x, 64:72, :] = jnp.concatenate([cond[4:8], pert[4:8]], axis=0)
            bottom_ref[x, 64:72, :] = jnp.concatenate([cond[0:4], pert[0:4]], axis=0)
            return carry

        for i in range(PARTS):
            copies[2 + i].wait()
            lax.fori_loop(i * each, (i + 1) * each, plane, 0, unroll=each)

    @pl.when(odd("gy"))
    def _():
        fill(chip_ref, core_ref)

    @pl.when(jnp.logical_not(odd("gy")))
    def _():
        fill(core_ref, chip_ref)

    for out, up in ((a_ref, jnp.logical_not(odd("gx"))), (b_ref, odd("gx"))):
        for dx in range(1, HALO + 1):
            out[dx - 1] = own_ref[jnp.where(up, size_x - dx, dx - 1)]


def pack(background, conductivity, perturbation):
    shape = jax.ShapeDtypeStruct
    inputs = [
        pltpu.with_memory_space_constraint(v, pltpu.HBM)
        for v in (background, conductivity, perturbation)
    ]
    return pl.pallas_call(
        pack_kernel,
        out_shape=(
            shape((16, 144, LANES), jnp.float32),
            shape((16, 72, LANES), jnp.float32),
            shape((16, 72, LANES), jnp.float32),
            shape((HALO, 144, LANES), jnp.float32),
            shape((HALO, 144, LANES), jnp.float32),
        ),
        in_specs=[pl.BlockSpec(memory_space=pltpu.HBM)] * 3,
        scratch_shapes=[
            pltpu.VMEM((16, 16, 8, LANES), jnp.float32),
            pltpu.VMEM((16, 8, LANES), jnp.float32),
            pltpu.VMEM((16, 8, LANES), jnp.float32),
            pltpu.SemaphoreType.DMA((2 + PARTS,)),
        ],
        compiler_params=pltpu.CompilerParams(vmem_limit_bytes=16 * MB),
        name="pack_y",
    )(*inputs)


def corner_layout():
    table, at = [], 0
    for dx in range(1, HALO):
        rows = (HALO - dx) * F
        table.append((dx, rows, at))
        at += 2 * rows + 16
    return table, at


CORNERS, CORNER_ROWS = corner_layout()


def pack_x_kernel(core_ref, chip_ref, a_ref, b_ref):
    def send(left_ref, right_ref):
        for out, up in ((a_ref, jnp.logical_not(odd("gx"))), (b_ref, odd("gx"))):
            for dx, rows, at in CORNERS:
                x = jnp.where(up, left_ref.shape[0] - dx, dx - 1)
                out[at : at + rows, :] = left_ref[x, 64 - rows : 64, :]
                out[at + rows : at + 2 * rows, :] = right_ref[x, 0:rows, :]
                at += 2 * rows
                out[at : at + 8, :] = left_ref[x, 64:72, :]
                out[at + 8 : at + 16, :] = right_ref[x, 64:72, :]

    @pl.when(odd("gy"))
    def _():
        send(core_ref, chip_ref)

    @pl.when(jnp.logical_not(odd("gy")))
    def _():
        send(chip_ref, core_ref)


def pack_x(core, chip):
    shape = jax.ShapeDtypeStruct((CORNER_ROWS, LANES), jnp.float32)
    return pl.pallas_call(
        pack_x_kernel,
        out_shape=(shape, shape),
        compiler_params=pltpu.CompilerParams(vmem_limit_bytes=16 * MB),
        name="pack_x",
    )(core, chip)


def lane_ids(rows):
    return lax.broadcasted_iota(jnp.int32, (rows, LANES), 1)


def own_copies(own_ref, core_ref, chip_ref, bext):
    odd_y = odd("gy")
    core_at = pl.multiple_of(jnp.where(odd_y, 0, 192), 8)
    chip_at = pl.multiple_of(jnp.where(odd_y, 192, 0), 8)
    core_c = pl.multiple_of(jnp.where(odd_y, 272, 280), 8)
    chip_c = pl.multiple_of(jnp.where(odd_y, 280, 272), 8)
    return [
        (own_ref.at[:, pl.ds(128, 16)], bext.at[:, pl.ds(256, 16)]),
        (core_ref.at[:, pl.ds(64, 8)], bext.at[:, pl.ds(core_c, 8)]),
        (chip_ref.at[:, pl.ds(64, 8)], bext.at[:, pl.ds(chip_c, 8)]),
        (own_ref.at[:, pl.ds(0, 128)], bext.at[:, pl.ds(64, 128)]),
        (core_ref.at[:, pl.ds(0, 64)], bext.at[:, pl.ds(core_at, 64)]),
        (chip_ref.at[:, pl.ds(0, 64)], bext.at[:, pl.ds(chip_at, 64)]),
    ]


def faces(rows_of, planes, ccoef, pcoef):
    lane = lane_ids(16)
    last = lane == LANES - 1
    edge = (lane == 0) | last

    def cells(x):
        own, left, right = rows_of(x)
        return (
            jnp.concatenate([left[0:4], own[0:8], right[0:4]], axis=0),
            jnp.concatenate([left[4:8], own[8:16], right[4:8]], axis=0),
        )

    for x in planes:
        now, then = cells(x), cells(x + 1)
        for coef, c, n, half, base in (
            (ccoef, now[0], then[0], 0.5, 0.05 - SHIFT),
            (pcoef, now[1], then[1], -0.5, 0.0),
        ):
            fx, fy, fu, fd, dd = coef
            fx[x] = half * (c + n)
            fy[x] = half * (c + pltpu.roll(c, 15, 0))
            up = jnp.where(last, 0.0, half * (c + pltpu.roll(c, LANES - 1, 1)))
            fu[x] = up
            fd[x] = pltpu.roll(up, 1, 1)
            dd[x] = base + jnp.where(edge, half * c, 0.0)


def stencil_plane(get, coeffs, x, y0, y1, mask_x, mask_y, emit):
    fx, fy, fu, fd, dd = coeffs
    q = get(x, y0)
    flux = fy[x, y0 - 1 : y0, :] * (q - get(x, y0 - 1))
    for y in range(y0, y1):
        nxt = get(x, y + 1)
        row = slice(y, y + 1)
        later = fy[x, row, :] * (nxt - q)
        out = dd[x, row, :] * q + (flux - later)
        out = out + fx[x - 1, row, :] * (q - get(x - 1, y))
        out = out - fx[x, row, :] * (get(x + 1, y) - q)
        out = out + fd[x, row, :] * (q - pltpu.roll(q, 1, 1))
        out = out - fu[x, row, :] * (pltpu.roll(q, LANES - 1, 1) - q)
        mask = mask_x
        if y < 4:
            mask = mask_y[0] if mask is None else mask * mask_y[0]
        elif y >= 12:
            mask = mask_y[1] if mask is None else mask * mask_y[1]
        if mask is not None:
            out = out * mask
        emit(y, out)
        flux, q = later, nxt


def tiles(ref):
    return lambda x, y: ref[x, tile_at(y), :]


def put_split(s_ref, i, row, y, value, exact=False):
    lanes = slice((y - 3) * LANES, (y - 2) * LANES)
    hi = value.astype(jnp.bfloat16)
    s_ref[i, row : row + F, lanes] = hi
    if not exact:
        lo = (value - hi.astype(jnp.float32)).astype(jnp.bfloat16)
        s_ref[i, row + F : row + 2 * F, lanes] = lo


def electrode_ids(elec_ref):
    sub = lax.broadcasted_iota(jnp.int32, (F, LANES), 0)
    ids = jnp.zeros((F, LANES), jnp.int32)
    for e in range(F):
        ids = jnp.where(sub == e, elec_ref[e], ids)
    return ids - lane_ids(F)


def grid_masks():
    one, zero = jnp.float32(1), jnp.float32(0)
    masks = []
    for axis in ("gx", "gy"):
        i = lax.axis_index(axis)
        low, high = i > 0, i < lax.axis_size(axis) - 1
        masks.append((jnp.where(low, one, zero), jnp.where(high, one, zero)))
    return masks


def unit_plane(ids, at_x, e0, i, s_ref, s_at, y_kept):
    size_x, size_y = 16 * lax.axis_size("gx"), 8 * lax.axis_size("gy")
    good_x = (at_x >= 0) & (at_x < size_x)
    for y in range(2, 14):
        at_y = lax.axis_index("gy") * 8 + y - 4
        good = good_x & (at_y >= 0) & (at_y < size_y)
        here = jnp.where(good, (at_x * size_y + at_y) * LANES, -(2**20))
        value = jnp.where(ids == here, 1.0, 0.0)
        e0[i, tile_at(y), :] = value
        if y_kept[0] <= y < y_kept[1]:
            put_split(s_ref, s_at, E0, y, value, exact=True)


def gram_of(s_ref, i):
    return lax.dot_general(
        s_ref[i, 0:KEPT, LANES : 9 * LANES],
        s_ref[i, :, LANES : 9 * LANES],
        (((1,), (1,)), ((), ())),
        preferred_element_type=jnp.float32,
    )


def inner_kernel(
    elec_ref, own_ref, core_ref, chip_ref, s_hbm, wide_ref, band_ref, side_ref, gram_ref,
    bext, v0, v1, v2, e0, e1, s_ref, cx, cy, cu, cd, cr, px, py, pu, pd, pr, sems, out_sems,
):
    copies = run_copies(own_copies(own_ref, core_ref, chip_ref, bext), sems)
    gx = lax.axis_index("gx")
    _, mask_y = grid_masks()
    ids = electrode_ids(elec_ref)

    def units(x, carry):
        unit_plane(ids, gx * 16 + x, e0, x, s_ref, x, (3, 13))
        return carry

    lax.fori_loop(2, 14, units, 0)
    wait_all(copies[:3])
    ccoef, pcoef = (cx, cy, cu, cd, cr), (px, py, pu, pd, pr)
    faces(
        lambda x: (bext[x, 256:272, :], bext[x, 272:280, :], bext[x, 280:288, :]),
        range(15), ccoef, pcoef,
    )
    wait_all(copies[3:])
    outs = []

    def hand_on(src, dst):
        outs.extend(run_copies([(src, dst)], out_sems, len(outs)))

    def sweep(src, dst, coeffs, first, reach, row, keep):
        def plane(x, carry):
            def emit(y, out):
                if dst is not None:
                    dst[x, tile_at(y), :] = out
                if keep[0] <= y < keep[1]:
                    put_split(s_ref, x, row, y, out)

            stencil_plane(tiles(src), coeffs, x, 4 - reach, 12 + reach, None, mask_y, emit)
            return carry

        lax.fori_loop(first, 16 - first, plane, 0, unroll=2)

    def hand_band(src, first, at):
        for k, x in enumerate((first, 14 - first)):
            hand_on(src.at[pl.ds(x, 2)], band_ref.at[pl.ds(at + 2 * k, 2)])

    hand_on(bext.at[pl.ds(0, 6)], wide_ref.at[pl.ds(0, 6)])
    hand_on(bext.at[pl.ds(10, 6)], wide_ref.at[pl.ds(6, 6)])
    sweep(bext, v0, pcoef, 1, 3, V0, (3, 13))
    hand_band(v0, 1, 0)
    sweep(v0, v1, ccoef, 2, 2, V1, (3, 13))
    hand_band(v1, 2, 4)
    sweep(v1, v2, ccoef, 3, 1, V2, (3, 13))
    hand_band(v2, 3, 8)
    hand_on(s_ref.at[pl.ds(1, 3), pl.ds(0, 96)], side_ref.at[pl.ds(0, 3)])
    hand_on(s_ref.at[pl.ds(12, 3), pl.ds(0, 96)], side_ref.at[pl.ds(3, 3)])
    sweep(e0, e1, ccoef, 3, 1, E1, (3, 13))
    hand_on(s_ref.at[pl.ds(4, 8), pl.ds(0, KEPT)], s_hbm)
    sweep(v2, None, ccoef, 4, 0, V3, (4, 12))
    sweep(e1, None, ccoef, 4, 0, E2, (4, 12))

    gram_ref[...] = gram_of(s_ref, 4)

    def gram_step(x, carry):
        gram_ref[...] += gram_of(s_ref, x)
        return carry

    lax.fori_loop(5, 12, gram_step, 0, unroll=7)
    wait_all(outs)


def inner(electrodes, own, core, chip):
    anywhere = pl.BlockSpec(memory_space=pl.ANY)
    vmem = pl.BlockSpec(memory_space=pltpu.VMEM)
    field = pltpu.VMEM((16, 256, LANES), jnp.float32)
    coeff = pltpu.VMEM((16, 16, LANES), jnp.float32)
    shape = jax.ShapeDtypeStruct
    return pl.pallas_call(
        inner_kernel,
        out_shape=(
            pltpu.HBM((8, KEPT, WIDE), jnp.bfloat16),
            shape((12, 288, LANES), jnp.float32),
            shape((12, 256, LANES), jnp.float32),
            shape((6, 96, WIDE), jnp.bfloat16),
            shape((KEPT, ALL_ROWS), jnp.float32),
        ),
        in_specs=[pl.BlockSpec(memory_space=pltpu.SMEM)] + [anywhere] * 3,
        out_specs=(pl.BlockSpec(memory_space=pltpu.HBM), vmem, vmem, vmem, vmem),
        scratch_shapes=[pltpu.VMEM((16, 288, LANES), jnp.float32)]
        + [field] * 5
        + [pltpu.VMEM((16, ALL_ROWS, WIDE), jnp.bfloat16)]
        + [coeff] * 10
        + [pltpu.SemaphoreType.DMA((6,)), pltpu.SemaphoreType.DMA((11,))],
        compiler_params=pltpu.CompilerParams(vmem_limit_bytes=36 * MB),
        cost_estimate=pl.CostEstimate(
            flops=4 * 10**9, bytes_accessed=16 * 10**6, transcendentals=0
        ),
        name="inner",
    )(electrodes, own, core, chip)


def edge_kernel(
    elec_ref, a_ref, b_ref, a_corner, b_corner, wide_ref, band_ref, side_ref, first_gram,
    s_hbm, pay_ref, halo, v0, v1, v2, e0, e1, s_ref, gram, cx, cy, cu, cd, cr, px, py, pu, pd, pr, out_sems,
):
    gx = lax.axis_index("gx")
    mask_x, mask_y = grid_masks()
    ids = electrode_ids(elec_ref)

    def x_of(l):
        return l - 4 if l < 10 else l

    def place(ref, corner, first):
        for dx in range(1, HALO + 1):
            k = first + dx - 1
            halo[k, 64:192, :] = ref[dx - 1, 0:128, :]
            halo[k, 256:272, :] = ref[dx - 1, 128:144, :]
        for dx, rows, at in CORNERS:
            k = first + dx - 1
            halo[k, 64 - rows : 64, :] = corner[at : at + rows, :]
            halo[k, 192 : 192 + rows, :] = corner[at + rows : at + 2 * rows, :]
            halo[k, 272:288, :] = corner[at + 2 * rows : at + 2 * rows + 16, :]

    @pl.when(odd("gx"))
    def _():
        place(a_ref, a_corner, 0)
        place(b_ref, b_corner, HALO)

    @pl.when(jnp.logical_not(odd("gx")))
    def _():
        place(b_ref, b_corner, 0)
        place(a_ref, a_corner, HALO)

    def plane_of(l):
        x = x_of(l)
        if 0 <= x < 16:
            return wide_ref, x if x < 6 else x - 4
        return halo, (-x - 1 if x < 0 else HALO + x - 16)

    def coeff_rows(l):
        ref, k = plane_of(l)
        return tuple(ref[k, a:b, :] for a, b in ((256, 272), (272, 280), (280, 288)))

    def background(l, y):
        ref, k = plane_of(l)
        return ref[k, tile_at(y), :]

    def banded(ref, first, at):
        def get(l, y):
            x = x_of(l)
            for k, start in enumerate((first, 14 - first)):
                if x in (start, start + 1):
                    return band_ref[at + 2 * k + x - start, tile_at(y), :]
            return ref[l, tile_at(y), :]

        return get

    def keep_of(l):
        x = x_of(l)
        i = x + 1 if l < 10 else x - 7
        if x in (-1, 16):
            return i, (4, 12)
        if -1 < x < 4 or 11 < x < 16:
            return i, (3, 13)
        return 0, (99, 99)

    for i in range(3):
        rows = 96 - 32 * (2 - i)
        s_ref[2 + i, 0:rows, :] = side_ref[i, 0:rows, :]
        s_ref[7 - i, 0:rows, :] = side_ref[5 - i, 0:rows, :]
    for l in list(range(2, 10)) + list(range(10, 18)):
        i, keep = keep_of(l)
        unit_plane(ids, gx * 16 + x_of(l), e0, l, s_ref, i, keep)
    ccoef, pcoef = (cx, cy, cu, cd, cr), (px, py, pu, pd, pr)
    faces(coeff_rows, list(range(9)) + list(range(10, 19)), ccoef, pcoef)

    def sweep(get, dst, coeffs, reach, planes, row, rows_kept=None):
        for l in planes:
            x = x_of(l)
            out_by = max(0, -x, x - 15)
            mask = mask_x[0] if x < 0 else mask_x[1] if x > 15 else None
            i, keep = keep_of(l)
            keep = rows_kept or keep

            def emit(y, out, l=l, i=i, keep=keep):
                if dst is not None:
                    dst[l, tile_at(y), :] = out
                if keep[0] <= y < keep[1]:
                    put_split(s_ref, i, row, y, out)

            near = reach - out_by
            stencil_plane(get, coeffs, l, 4 - near, 12 + near, mask, mask_y, emit)

    def sides(low, count):
        return [x + 4 for x in range(low, low + count)] + [15 - x for x in range(low, low + count)]

    sweep(background, v0, pcoef, 3, sides(-3, 4), V0)
    sweep(banded(v0, 1, 0), v1, ccoef, 2, sides(-2, 4), V1)
    sweep(banded(v1, 2, 4), v2, ccoef, 1, sides(-1, 4), V2)
    sweep(tiles(e0), e1, ccoef, 1, sides(-1, 6), E1)
    outs = run_copies([(s_ref.at[:, pl.ds(0, KEPT)], s_hbm)], out_sems)
    sweep(banded(v2, 3, 8), None, ccoef, 0, sides(0, 4), V3, (4, 12))
    sweep(tiles(e1), None, ccoef, 0, sides(0, 4), E2, (4, 12))

    gram[...] = first_gram[...]

    def gram_step(i, carry):
        gram[...] += gram_of(s_ref, i)
        return carry

    lax.fori_loop(1, 9, gram_step, 0, unroll=8)

    def rows_of(row):
        if row == E0:
            return gram[row : row + F, :]
        return gram[row : row + F, :] + gram[row + F : row + 2 * F, :]

    summed = {row: rows_of(row) for row in (V0, V1, V2, E0, E1)}

    def block(row, col):
        rows = summed[row]
        if col == E0:
            return rows[:, col : col + F]
        return rows[:, col : col + F] + rows[:, col + F : col + 2 * F]

    order = [
        (V0, V0), (V0, V1), (V1, V1), (V1, V2), (V2, V2), (V2, V3), (V0, E0), (V1, E0),
        (V2, E0), (E0, V3), (E1, V3), (E0, E0), (E0, E1), (E1, E1), (E1, E2),
    ]
    blocks = [block(r, c) for r, c in order] + [jnp.zeros((F, F), jnp.float32)]
    pay_ref[0:16, :] = jnp.concatenate(blocks[:8], axis=1)
    pay_ref[16:32, :] = jnp.concatenate(blocks[8:], axis=1)
    wait_all(outs)


def edge(electrodes, a, b, a_corner, b_corner, wide, band, side, gram):
    vmem = pl.BlockSpec(memory_space=pltpu.VMEM)
    field = pltpu.VMEM((20, 256, LANES), jnp.float32)
    coeff = pltpu.VMEM((20, 16, LANES), jnp.float32)
    return pl.pallas_call(
        edge_kernel,
        out_shape=(
            pltpu.HBM((10, KEPT, WIDE), jnp.bfloat16),
            jax.ShapeDtypeStruct((32, LANES), jnp.float32),
        ),
        in_specs=[pl.BlockSpec(memory_space=pltpu.SMEM)] + [vmem] * 8,
        out_specs=(pl.BlockSpec(memory_space=pltpu.HBM), vmem),
        scratch_shapes=[pltpu.VMEM((2 * HALO, 288, LANES), jnp.float32)]
        + [field] * 5
        + [
            pltpu.VMEM((10, ALL_ROWS, WIDE), jnp.bfloat16),
            pltpu.VMEM((KEPT, ALL_ROWS), jnp.float32),
        ]
        + [coeff] * 10
        + [pltpu.SemaphoreType.DMA((1,))],
        compiler_params=pltpu.CompilerParams(vmem_limit_bytes=36 * MB),
        name="edge",
    )(electrodes, a, b, a_corner, b_corner, wide, band, side, gram)


def matmul(a, b, dims=((1,), (0,))):
    return lax.dot_general(
        a, b, (dims, ((), ())), precision=HIGHEST, preferred_element_type=jnp.float32
    )


def galerkin(m0, m1, m2, m3):
    a12 = m2 + SHIFT * m1
    work = jnp.concatenate(
        [
            jnp.concatenate([m1 + SHIFT * m0, a12, m0], axis=1),
            jnp.concatenate([a12, m3 + SHIFT * m2, m1], axis=1),
        ],
        axis=0,
    )
    work = jnp.concatenate([work, jnp.zeros((2 * F, LANES - 3 * F), jnp.float32)], axis=1)
    return eliminate(work)[:, 2 * F : 3 * F]


def eliminate(work, size=8):
    count = work.shape[0]
    sub = lax.broadcasted_iota(jnp.int32, work.shape, 0)

    def column(k):
        return jnp.take_along_axis(work, jnp.full(work.shape, k, jnp.int32), axis=1)

    def row(v, k):
        return jnp.broadcast_to(v[k : k + 1, :], (8, LANES))

    def tall(v):
        return jnp.concatenate([v] * (count // 8), axis=0)

    for k in range(0, count, size):
        cols = [column(k + j) for j in range(size)]
        rows = [row(work, k + i) for i in range(size)]
        p = [[row(cols[j], k + i) for j in range(size)] for i in range(size)]
        for s in range(0, size, 2):
            a, b, c, d = p[s][s], p[s][s + 1], p[s + 1][s], p[s + 1][s + 1]
            inverse = 1.0 / (a * d - b * c)
            a, b, c, d = d * inverse, -(b * inverse), -(c * inverse), a * inverse
            rows[s], rows[s + 1] = a * rows[s] + b * rows[s + 1], c * rows[s] + d * rows[s + 1]
            for j in range(s + 2, size):
                u, v = p[s][j], p[s + 1][j]
                p[s][j], p[s + 1][j] = a * u + b * v, c * u + d * v
            for i in range(size):
                if i in (s, s + 1):
                    continue
                u, v = p[i][s], p[i][s + 1]
                rows[i] = rows[i] - u * rows[s] - v * rows[s + 1]
                for j in range(s + 2, size):
                    p[i][j] = p[i][j] - u * p[s][j] - v * p[s + 1][j]
        for j in range(size):
            work = work - cols[j] * tall(rows[j])
        for j in range(size):
            work = jnp.where(sub == k + j, tall(rows[j]), work)
    return work


def final_kernel(
    pattern_ref, parts_ref, own_ref, core_ref, chip_ref, a_ref, b_ref, mid_hbm, edge_hbm,
    out_ref, sens_ref, bg, adj, s_ref, mix_ref, sems, *, damping,
):
    odd_y = odd("gy")

    def y_rows(is_left):
        src = pl.multiple_of(jnp.where(is_left, 48, 0), 8)
        dst = pl.multiple_of(jnp.where(is_left, 0, 144), 8)
        return pl.ds(src, 16), pl.ds(dst, 16)

    planes = pl.ds(1, 16)
    core_src, core_dst = y_rows(odd_y)
    chip_src, chip_dst = y_rows(jnp.logical_not(odd_y))
    near = pl.ds(0, 128)
    odd_x = odd("gx")
    pairs = [
        (edge_hbm.at[pl.ds(0, 5)], s_ref.at[pl.ds(0, 5)]),
        (mid_hbm, s_ref.at[pl.ds(5, 8)]),
        (edge_hbm.at[pl.ds(5, 5)], s_ref.at[pl.ds(13, 5)]),
        (own_ref.at[:, pl.ds(0, 128)], bg.at[planes, pl.ds(16, 128)]),
        (core_ref.at[:, core_src], bg.at[planes, core_dst]),
        (chip_ref.at[:, chip_src], bg.at[planes, chip_dst]),
        (a_ref.at[0, near], bg.at[jnp.where(odd_x, 0, 17), pl.ds(16, 128)]),
        (b_ref.at[0, near], bg.at[jnp.where(odd_x, 17, 0), pl.ds(16, 128)]),
    ]
    copies = [pltpu.make_async_copy(s, d, sems.at[i]) for i, (s, d) in enumerate(pairs)]

    @pl.when(lax.axis_index("gx") >= 0)
    def _():
        for c in copies:
            c.start()

    total = jnp.sum(parts_ref[...], axis=0)

    def part(k):
        r, c = (k // 8) * F, (k % 8) * F
        return total[r : r + F, c : c + F]

    m = [part(k) for k in range(6)]
    p = [part(6), part(7), part(8), part(9).T, part(10).T]
    e = [part(k) for k in range(11, 15)]
    y = galerkin(*m[:4])

    lane = lax.broadcasted_iota(jnp.int32, (F, F), 1)
    sub = lax.broadcasted_iota(jnp.int32, (F, F), 0)
    first, second = jnp.zeros((F, F), jnp.int32), jnp.zeros((F, F), jnp.int32)
    for i in range(F):
        first = jnp.where(sub == i, pattern_ref[i, 0], first)
        second = jnp.where(sub == i, pattern_ref[i, 1], second)
    pairing = jnp.where(lane == first, 1.0, 0.0) - jnp.where(lane == second, 1.0, 0.0)
    w = matmul(8.0 * matmul(pairing, pairing, ((0,), (0,))), jnp.concatenate(p[:2], axis=0), ((1,), (1,)))
    forms = []
    for k in range(4):
        inside = jnp.concatenate(
            [
                jnp.concatenate([m[k], m[k + 1]], axis=1),
                jnp.concatenate([m[k + 1], m[k + 2]], axis=1),
            ],
            axis=0,
        )
        across = matmul(jnp.concatenate([p[k], p[k + 1]], axis=0), w)
        local = matmul(w, matmul(e[k], w), ((0,), (0,)))
        forms.append(damping * (damping * inside + across + across.T) + local)
    hy = matmul(jnp.concatenate(forms, axis=0), y)
    moments = [matmul(y, hy[32 * k : 32 * (k + 1)], ((0,), (0,))) for k in range(4)]
    z = jnp.concatenate([damping * y, matmul(w, y)], axis=0)
    q = galerkin(*moments)
    z0, z1 = matmul(z, q[0:F]), matmul(z, q[F:])
    none = jnp.zeros((F, F), jnp.float32)
    mix = [
        jnp.concatenate([y[0:F], z0[0:F]], axis=1),
        jnp.concatenate([y[F:], z0[F : 2 * F] + z1[0:F]], axis=1),
        jnp.concatenate([none, z1[F : 2 * F]], axis=1),
        jnp.concatenate([none, z0[2 * F :]], axis=1),
        jnp.concatenate([none, z1[2 * F :]], axis=1),
    ]
    mix = [mix[i] for i in (0, 0, 1, 1, 2, 2, 3, 4, 4)]
    mix = jnp.concatenate(mix, axis=0).T
    hi = mix.astype(jnp.bfloat16)
    mix_ref[0:32, :] = hi
    mix_ref[32:64, :] = (mix - hi.astype(jnp.float32)).astype(jnp.bfloat16)
    wait_all(copies)
    both = mix_ref[...]

    def combine(x, lanes):
        out = jnp.dot(both, s_ref[x, :, lanes], preferred_element_type=jnp.float32)
        return out[0:32] + out[32:64]

    def store(x, out):
        for k in range(10):
            cols = slice(k * LANES, (k + 1) * LANES)
            if 0 < k < 9:
                out_ref[pl.ds(x * 8 + k - 9, F, stride=128), :] = out[0:F, cols]
            adj[x, tile_at(k), :] = out[F:, cols]

    def store_end(x, out):
        for k in range(8):
            adj[x, tile_at(k + 1), :] = out[F:, k * LANES : (k + 1) * LANES]

    lane = lane_ids(F)

    def sens_plane(x):
        b, a = bg[x, tile_at(1), :], adj[x, tile_at(1), :]
        before = (b - bg[x, tile_at(0), :]) * (a - adj[x, tile_at(0), :])
        for k in range(1, 9):
            bn, an = bg[x, tile_at(k + 1), :], adj[x, tile_at(k + 1), :]
            after = (bn - b) * (an - a)
            total = before + after
            for s in (x - 1, x + 1):
                total = total + (bg[s, tile_at(k), :] - b) * (adj[s, tile_at(k), :] - a)
            bu = jnp.where(lane == LANES - 1, 0.0, pltpu.roll(b, LANES - 1, 1))
            au = jnp.where(lane == LANES - 1, 0.0, pltpu.roll(a, LANES - 1, 1))
            bd = jnp.where(lane == 0, 0.0, pltpu.roll(b, 1, 1))
            ad = jnp.where(lane == 0, 0.0, pltpu.roll(a, 1, 1))
            total = total + (bu - b) * (au - a) + (bd - b) * (ad - a)
            sens_ref[x - 1, k - 1 : k, :] = -0.5 * jnp.sum(total, axis=0, keepdims=True)
            before, b, a = after, bn, an

    ends = slice(LANES, 9 * LANES)
    store_end(0, combine(0, ends))
    store(1, combine(1, slice(0, WIDE)))
    store(2, combine(2, slice(0, WIDE)))

    def plane(x, carry):
        out = combine(x + 2, slice(0, WIDE))
        sens_plane(x)
        store(x + 2, out)
        return carry

    lax.fori_loop(1, 15, plane, 0, unroll=2)
    out = combine(17, ends)
    sens_plane(15)
    store_end(17, out)
    sens_plane(16)


def final(pattern, parts, own, core, chip, a, b, mid, edges, damping):
    anywhere = pl.BlockSpec(memory_space=pl.ANY)
    vmem = pl.BlockSpec(memory_space=pltpu.VMEM)
    hbm = pl.BlockSpec(memory_space=pltpu.HBM)

    def kernel(*refs):
        final_kernel(*refs, damping=damping)

    return pl.pallas_call(
        kernel,
        out_shape=(
            jax.ShapeDtypeStruct((2048, LANES), jnp.float32),
            jax.ShapeDtypeStruct((16, 8, LANES), jnp.float32),
        ),
        in_specs=[pl.BlockSpec(memory_space=pltpu.SMEM), vmem] + [anywhere] * 5 + [hbm] * 2,
        scratch_shapes=[
            pltpu.VMEM((18, 160, LANES), jnp.float32),
            pltpu.VMEM((18, 160, LANES), jnp.float32),
            pltpu.VMEM((18, KEPT, WIDE), jnp.bfloat16),
            pltpu.VMEM((64, KEPT), jnp.bfloat16),
            pltpu.SemaphoreType.DMA((8,)),
        ],
        compiler_params=pltpu.CompilerParams(vmem_limit_bytes=56 * MB),
        name="final",
    )(pattern, parts, own, core, chip, a, b, mid, edges)


def spread(block, axis, count, groups=None):
    copies = jnp.broadcast_to(block[None], (count,) + block.shape)
    return lax.all_to_all(copies, axis, 0, 0, axis_index_groups=groups)


def swaps(first, count):
    lows = range(first, count - 1, 2)
    return [(i, i + 1) for i in lows] + [(i + 1, i) for i in lows]


def on_device(background, conductivity, perturbation, electrodes, pattern):
    size_x, size_y, size_z = conductivity.shape
    count_x, count_y = lax.axis_size("gx"), lax.axis_size("gy")
    own, core, chip, a, b = pack(background, conductivity, perturbation)
    a = lax.ppermute(a, "gx", swaps(0, count_x))
    b = lax.ppermute(b, "gx", swaps(1, count_x))
    chip = lax.ppermute(chip, "gy", swaps(1, count_y))
    core = lax.ppermute(core, "gy", swaps(0, count_y))
    a_corner, b_corner = pack_x(core, chip)
    a_corner = lax.ppermute(a_corner, "gx", swaps(0, count_x))
    b_corner = lax.ppermute(b_corner, "gx", swaps(1, count_x))
    mid, wide, band, side, gram = inner(electrodes, own, core, chip)
    edges, pay = edge(electrodes, a, b, a_corner, b_corner, wide, band, side, gram)
    pay = pay + lax.ppermute(pay, "gy", swaps(0, count_y))
    pay = jnp.sum(spread(pay, "gx", count_x), axis=0)
    chips = count_y // 2
    groups = [[2 * i + c for i in range(chips)] for c in range(2)]
    parts = spread(pay, "gy", chips, groups)
    cells = size_x * size_y * size_z * count_x * count_y
    damping = 80.0 / math.sqrt(cells)
    tangent, sens = final(pattern, parts, own, core, chip, a, b, mid, edges, damping)
    return tangent.reshape(background.shape), sens


def solution(mesh):
    in_specs = (P(None, "gx", "gy", None), P("gx", "gy", None), P("gx", "gy", None), P(), P())
    out_specs = (P(None, "gx", "gy", None), P("gx", "gy", None))
    return jax.shard_map(
        on_device, mesh=mesh, in_specs=in_specs, out_specs=out_specs, check_vma=False
    )
```

```python
import math

import jax
import jax.numpy as jnp
from jax import lax
from jax.experimental import pallas as pl
from jax.experimental.pallas import tpu as pltpu
from jax.sharding import PartitionSpec as P

SHIFT = 12.0
F = 16
LANES = 128
HALO = 4
HIGHEST = lax.Precision.HIGHEST
V0, V1, V2, E0, E1, V3, E2 = 0, 32, 64, 96, 112, 144, 176
KEPT, ALL_ROWS = 144, 208
WIDE = 10 * LANES
MB = 2**20


def tile_at(y):
    return slice(y * F, (y + 1) * F)


def run_copies(pairs, sems, first=0):
    copies = [
        pltpu.make_async_copy(s, d, sems.at[first + i]) for i, (s, d) in enumerate(pairs)
    ]
    for c in copies:
        c.start()
    return copies


def wait_all(copies):
    for c in copies:
        c.wait()


def odd(axis):
    return lax.rem(lax.axis_index(axis), 2) == 1


PARTS = 4


def pack_kernel(
    bg_hbm, cond_hbm, pert_hbm, elec_hbm, wide_ref, core_ref, chip_ref, a_ref, b_ref, ids_ref,
    bg, cond_v, pert_v, elec, sems,
):
    size_x, size_y = cond_v.shape[0], cond_v.shape[1]
    each = size_x // PARTS
    pairs = [(cond_hbm, cond_v), (pert_hbm, pert_v), (elec_hbm, elec)]
    for i in range(PARTS):
        planes = pl.ds(i * each, each)
        pairs.append((bg_hbm.at[:, planes], bg.at[:, planes]))
    copies = run_copies(pairs, sems)

    def fill(top_ref, bottom_ref):
        wait_all(copies[:3])

        def plane(x, carry):
            for y in range(size_y):
                tile = bg[:, x, y, :]
                wide_ref[x + HALO, tile_at(y + HALO), :] = tile
                if y >= size_y - HALO:
                    top_ref[x, tile_at(y - size_y + HALO), :] = tile
                if y < HALO:
                    bottom_ref[x, tile_at(y), :] = tile
            cond, pert = cond_v[x], pert_v[x]
            wide_ref[x + HALO, 256:264, :] = cond
            wide_ref[x + HALO, 264:272, :] = pert
            top_ref[x, 64:72, :] = jnp.concatenate([cond[4:8], pert[4:8]], axis=0)
            bottom_ref[x, 64:72, :] = jnp.concatenate([cond[0:4], pert[0:4]], axis=0)
            return carry

        for i in range(PARTS):
            copies[3 + i].wait()
            lax.fori_loop(i * each, (i + 1) * each, plane, 0, unroll=each)

    @pl.when(odd("gy"))
    def _():
        fill(chip_ref, core_ref)

    @pl.when(jnp.logical_not(odd("gy")))
    def _():
        fill(core_ref, chip_ref)

    sub = lax.broadcasted_iota(jnp.int32, (F, LANES), 0)
    ids = jnp.zeros((F, LANES), jnp.int32)
    for e in range(F):
        ids = jnp.where(sub == e, elec[e], ids)
    ids_ref[...] = ids - lane_ids(F)

    for out, up in ((a_ref, jnp.logical_not(odd("gx"))), (b_ref, odd("gx"))):
        for dx in range(1, HALO + 1):
            x = HALO + jnp.where(up, size_x - dx, dx - 1)
            out[dx - 1, 0:128, :] = wide_ref[x, 64:192, :]
            out[dx - 1, 128:144, :] = wide_ref[x, 256:272, :]


def pack(background, conductivity, perturbation, electrodes):
    shape = jax.ShapeDtypeStruct
    inputs = [
        pltpu.with_memory_space_constraint(v, pltpu.HBM)
        for v in (background, conductivity, perturbation, electrodes)
    ]
    return pl.pallas_call(
        pack_kernel,
        out_shape=(
            shape((24, 288, LANES), jnp.float32),
            shape((16, 72, LANES), jnp.float32),
            shape((16, 72, LANES), jnp.float32),
            shape((HALO, 144, LANES), jnp.float32),
            shape((HALO, 144, LANES), jnp.float32),
            shape((F, LANES), jnp.int32),
        ),
        in_specs=[pl.BlockSpec(memory_space=pltpu.HBM)] * 4,
        scratch_shapes=[
            pltpu.VMEM((16, 16, 8, LANES), jnp.float32),
            pltpu.VMEM((16, 8, LANES), jnp.float32),
            pltpu.VMEM((16, 8, LANES), jnp.float32),
            pltpu.SMEM((F,), jnp.int32),
            pltpu.SemaphoreType.DMA((3 + PARTS,)),
        ],
        compiler_params=pltpu.CompilerParams(vmem_limit_bytes=16 * MB),
        name="pack_y",
    )(*inputs)


def corner_layout():
    table, at = [], 0
    for dx in range(1, HALO):
        rows = (HALO - dx) * F
        table.append((dx, rows, at))
        at += 2 * rows + 16
    return table, at


CORNERS, CORNER_ROWS = corner_layout()


def pack_corners_kernel(core_ref, chip_ref, a_ref, b_ref):
    def send(left_ref, right_ref):
        for out, up in ((a_ref, jnp.logical_not(odd("gx"))), (b_ref, odd("gx"))):
            for dx, rows, at in CORNERS:
                x = jnp.where(up, left_ref.shape[0] - dx, dx - 1)
                out[at : at + rows, :] = left_ref[x, 64 - rows : 64, :]
                out[at + rows : at + 2 * rows, :] = right_ref[x, 0:rows, :]
                at += 2 * rows
                out[at : at + 8, :] = left_ref[x, 64:72, :]
                out[at + 8 : at + 16, :] = right_ref[x, 64:72, :]

    @pl.when(odd("gy"))
    def _():
        send(core_ref, chip_ref)

    @pl.when(jnp.logical_not(odd("gy")))
    def _():
        send(chip_ref, core_ref)


def pack_corners(core, chip):
    shape = jax.ShapeDtypeStruct((CORNER_ROWS, LANES), jnp.float32)
    return pl.pallas_call(
        pack_corners_kernel,
        out_shape=(shape, shape),
        compiler_params=pltpu.CompilerParams(vmem_limit_bytes=16 * MB),
        name="pack_corners",
    )(core, chip)


def lane_ids(rows):
    return lax.broadcasted_iota(jnp.int32, (rows, LANES), 1)


def faces(wide, x, ccoef, pcoef):
    lane = lane_ids(16)
    last = lane == LANES - 1
    edge = (lane == 0) | last

    def cells(x):
        own, left, right = wide[x, 256:272, :], wide[x, 272:280, :], wide[x, 280:288, :]
        return (
            jnp.concatenate([left[0:4], own[0:8], right[0:4]], axis=0),
            jnp.concatenate([left[4:8], own[8:16], right[4:8]], axis=0),
        )

    before, now, then = cells(jnp.maximum(x - 1, 0)), cells(x), cells(x + 1)
    for which, coef, half in ((0, ccoef, 0.5), (1, pcoef, -0.5)):
        c, n = now[which], then[which]
        fx, fy, fu, fd, dd = coef
        east = half * (c + n)
        south = half * (c + pltpu.roll(c, 15, 0))
        up = jnp.where(last, 0.0, half * (c + pltpu.roll(c, LANES - 1, 1)))
        down = pltpu.roll(up, 1, 1)
        rest = jnp.where(edge, half * c, 0.0)
        if which == 0:
            west = half * (c + before[0])
            sides = (east + west) + (south + pltpu.roll(south, 1, 0)) + (up + down)
            rest = (0.05 - SHIFT) + rest + sides
        fx[x], fy[x], fu[x], fd[x], dd[x] = east, south, up, down, rest


def source_plane(get, coeffs, x, y0, y1, mask_x, mask_y, emit):
    fx, fy, fu, fd, dd = coeffs
    q = get(x, y0)
    flux = fy[x, y0 - 1 : y0, :] * (q - get(x, y0 - 1))
    for y in range(y0, y1):
        nxt = get(x, y + 1)
        row = slice(y, y + 1)
        later = fy[x, row, :] * (nxt - q)
        out = dd[x, row, :] * q + (flux - later)
        out = out + fx[x - 1, row, :] * (q - get(x - 1, y))
        out = out - fx[x, row, :] * (get(x + 1, y) - q)
        out = out + fd[x, row, :] * (q - pltpu.roll(q, 1, 1))
        out = out - fu[x, row, :] * (pltpu.roll(q, LANES - 1, 1) - q)
        emit(y, masked(out, y, mask_x, mask_y))
        flux, q = later, nxt


def operator_plane(get, coeffs, x, y0, y1, mask_x, mask_y, emit):
    fx, fy, fu, fd, dd = coeffs
    before, q = get(x, y0 - 1), get(x, y0)
    north = fy[x, y0 - 1 : y0, :]
    for y in range(y0, y1):
        nxt = get(x, y + 1)
        row = slice(y, y + 1)
        south = fy[x, row, :]
        out = dd[x, row, :] * q - north * before - south * nxt
        across = fx[x - 1, row, :] * get(x - 1, y) + fx[x, row, :] * get(x + 1, y)
        depth = fd[x, row, :] * pltpu.roll(q, 1, 1) + fu[x, row, :] * pltpu.roll(q, LANES - 1, 1)
        emit(y, masked(out - (across + depth), y, mask_x, mask_y))
        before, q, north = q, nxt, south


def masked(out, y, mask_x, mask_y):
    mask = mask_x
    if y < 4:
        mask = mask_y[0] if mask is None else mask * mask_y[0]
    elif y >= 12:
        mask = mask_y[1] if mask is None else mask * mask_y[1]
    return out if mask is None else out * mask


def tiles(ref):
    return lambda x, y: ref[x, tile_at(y), :]


def put_split(s_ref, i, row, y, value, exact=False):
    lanes = slice((y - 3) * LANES, (y - 2) * LANES)
    hi = value.astype(jnp.bfloat16)
    s_ref[i, row : row + F, lanes] = hi
    if not exact:
        lo = (value - hi.astype(jnp.float32)).astype(jnp.bfloat16)
        s_ref[i, row + F : row + 2 * F, lanes] = lo


def grid_masks():
    one, zero = jnp.float32(1), jnp.float32(0)
    masks = []
    for axis in ("gx", "gy"):
        i = lax.axis_index(axis)
        low, high = i > 0, i < lax.axis_size(axis) - 1
        masks.append((jnp.where(low, one, zero), jnp.where(high, one, zero)))
    return masks


def unit_plane(ids, at_x, e0, i, s_ref, s_at):
    size_x, size_y = 16 * lax.axis_size("gx"), 8 * lax.axis_size("gy")
    good_x = (at_x >= 0) & (at_x < size_x)
    for y in range(2, 14):
        at_y = lax.axis_index("gy") * 8 + y - 4
        good = good_x & (at_y >= 0) & (at_y < size_y)
        here = jnp.where(good, (at_x * size_y + at_y) * LANES, -(2**20))
        value = jnp.where(ids == here, 1.0, 0.0)
        e0[i, tile_at(y), :] = value
        if 3 <= y < 13:
            put_split(s_ref, s_at, E0, y, value, exact=True)


def gram_of(s_ref, i):
    return lax.dot_general(
        s_ref[i, 0:KEPT, LANES : 9 * LANES],
        s_ref[i, :, LANES : 9 * LANES],
        (((1,), (1,)), ((), ())),
        preferred_element_type=jnp.float32,
    )


def inner_kernel(
    ids_ref, wide_in, core_ref, chip_ref,
    wide, v0, v1, v2, side_ref, gram_ref, s_hbm,
    e0, e1, s_ref, cx, cy, cu, cd, cr, px, py, pu, pd, pr, out_sems,
):
    del wide_in

    def fill(left_ref, right_ref):
        def plane(x, carry):
            wide[x + HALO, 0:64, :] = left_ref[x, 0:64, :]
            wide[x + HALO, 192:256, :] = right_ref[x, 0:64, :]
            wide[x + HALO, 272:280, :] = left_ref[x, 64:72, :]
            wide[x + HALO, 280:288, :] = right_ref[x, 64:72, :]
            return carry

        lax.fori_loop(0, 16, plane, 0, unroll=4)

    @pl.when(odd("gy"))
    def _():
        fill(core_ref, chip_ref)

    @pl.when(jnp.logical_not(odd("gy")))
    def _():
        fill(chip_ref, core_ref)

    gx = lax.axis_index("gx")
    _, mask_y = grid_masks()
    ids = ids_ref[...]
    ccoef, pcoef = (cx, cy, cu, cd, cr), (px, py, pu, pd, pr)

    def prepare(x, carry):
        faces(wide, x, ccoef, pcoef)
        return carry

    lax.fori_loop(4, 19, prepare, 0, unroll=3)

    def units(x, carry):
        unit_plane(ids, gx * 16 + x - HALO, e0, x, s_ref, x - HALO)
        return carry

    lax.fori_loop(6, 18, units, 0, unroll=2)
    outs = []

    def hand_on(src, dst):
        outs.extend(run_copies([(src, dst)], out_sems, len(outs)))

    def sweep(stencil, src, dst, coeffs, first, reach, row, keep):
        def plane(x, carry):
            def emit(y, out):
                if dst is not None:
                    dst[x, tile_at(y), :] = out
                if keep[0] <= y < keep[1]:
                    put_split(s_ref, x - HALO, row, y, out)

            stencil(tiles(src), coeffs, x, 4 - reach, 12 + reach, None, mask_y, emit)
            return carry

        lax.fori_loop(HALO + first, HALO + 16 - first, plane, 0, unroll=2)

    sweep(source_plane, wide, v0, pcoef, 1, 3, V0, (3, 13))
    sweep(operator_plane, v0, v1, ccoef, 2, 2, V1, (3, 13))
    sweep(operator_plane, v1, v2, ccoef, 3, 1, V2, (3, 13))
    hand_on(s_ref.at[pl.ds(1, 3), pl.ds(0, 96)], side_ref.at[pl.ds(0, 3)])
    hand_on(s_ref.at[pl.ds(12, 3), pl.ds(0, 96)], side_ref.at[pl.ds(3, 3)])
    sweep(operator_plane, e0, e1, ccoef, 3, 1, E1, (3, 13))
    hand_on(s_ref.at[pl.ds(4, 8), pl.ds(0, KEPT)], s_hbm)
    sweep(operator_plane, v2, None, ccoef, 4, 0, V3, (4, 12))
    sweep(operator_plane, e1, None, ccoef, 4, 0, E2, (4, 12))

    gram_ref[...] = gram_of(s_ref, 4)

    def gram_step(x, carry):
        gram_ref[...] += gram_of(s_ref, x)
        return carry

    lax.fori_loop(5, 12, gram_step, 0, unroll=7)
    wait_all(outs)


FIELD = (24, 256, LANES)
COEFF = (24, 16, LANES)


def inner(ids, wide, core, chip):
    vmem = pl.BlockSpec(memory_space=pltpu.VMEM)
    shape = jax.ShapeDtypeStruct
    field = shape(FIELD, jnp.float32)
    return pl.pallas_call(
        inner_kernel,
        out_shape=(
            shape((24, 288, LANES), jnp.float32),
            field, field, field,
            shape((6, 96, WIDE), jnp.bfloat16),
            shape((KEPT, ALL_ROWS), jnp.float32),
            pltpu.HBM((8, KEPT, WIDE), jnp.bfloat16),
        ),
        in_specs=[vmem] * 4,
        out_specs=(vmem,) * 6 + (pl.BlockSpec(memory_space=pltpu.HBM),),
        scratch_shapes=[pltpu.VMEM(FIELD, jnp.float32)] * 2
        + [pltpu.VMEM((16, ALL_ROWS, WIDE), jnp.bfloat16)]
        + [pltpu.VMEM(COEFF, jnp.float32)] * 10
        + [pltpu.SemaphoreType.DMA((3,))],
        input_output_aliases={1: 0},
        compiler_params=pltpu.CompilerParams(vmem_limit_bytes=VMEM_INNER * MB),
        cost_estimate=pl.CostEstimate(
            flops=4 * 10**9, bytes_accessed=16 * 10**6, transcendentals=0
        ),
        name="inner",
    )(ids, wide, core, chip)


VMEM_INNER = 36
VMEM_EDGE = 36


def edge_kernel(
    ids_ref, a_ref, b_ref, a_corner, b_corner, wide_in, v0_in, v1_in, v2_in, side_ref, first_gram,
    wide, v0, v1, v2, pay_ref, s_hbm, bg_hbm,
    e0, e1, s_ref, gram, cx, cy, cu, cd, cr, px, py, pu, pd, pr, out_sems,
):
    del wide_in, v0_in, v1_in, v2_in
    gx = lax.axis_index("gx")
    mask_x, mask_y = grid_masks()
    ids = ids_ref[...]

    def halo_plane(high, dx):
        return jnp.where(high, 19 + dx, HALO - dx)

    sides = ((a_ref, a_corner, jnp.logical_not(odd("gx"))), (b_ref, b_corner, odd("gx")))
    for ref, corner, high in sides:
        for dx in range(1, HALO + 1):
            x = halo_plane(high, dx)
            wide[x, 64:192, :] = ref[dx - 1, 0:128, :]
            wide[x, 256:272, :] = ref[dx - 1, 128:144, :]
        for dx, rows, at in CORNERS:
            x = halo_plane(high, dx)
            wide[x, 64 - rows : 64, :] = corner[at : at + rows, :]
            wide[x, 192 : 192 + rows, :] = corner[at + rows : at + 2 * rows, :]
            wide[x, 272:288, :] = corner[at + 2 * rows : at + 2 * rows + 16, :]

    outs = run_copies([(wide.at[pl.ds(3, 18), pl.ds(48, 160)], bg_hbm)], out_sems)

    for i in range(3):
        rows = 96 - 32 * (2 - i)
        s_ref[2 + i, 0:rows, :] = side_ref[i, 0:rows, :]
        s_ref[7 - i, 0:rows, :] = side_ref[5 - i, 0:rows, :]

    ccoef, pcoef = (cx, cy, cu, cd, cr), (px, py, pu, pd, pr)

    def prepare(i, carry):
        faces(wide, jnp.where(i < 9, i, i + 5), ccoef, pcoef)
        return carry

    lax.fori_loop(0, 18, prepare, 0, unroll=3)

    def mirrored(low, count, body):
        for x in range(low, low + count):
            inside = -1 <= x <= 3
            body(HALO + x, x + 1 if inside else 10, mask_x[0])
            body(19 - x, 8 - x if inside else 10, mask_x[1])

    mirrored(-2, 8, lambda at, s_at, _: unit_plane(ids, gx * 16 + at - HALO, e0, at, s_ref, s_at))

    def sweep(stencil, src, dst, coeffs, row, low, count, near, keep):
        def body(at, s_at, mask):
            def emit(y, out):
                if dst is not None:
                    dst[at, tile_at(y), :] = out
                if keep[0] <= y < keep[1]:
                    put_split(s_ref, s_at, row, y, out)

            mask = mask if low < 0 else None
            stencil(tiles(src), coeffs, at, 4 - near, 12 + near, mask, mask_y, emit)

        mirrored(low, count, body)

    def save(row, rows):
        pair = (s_ref.at[pl.ds(0, 10), pl.ds(row, rows)], s_hbm.at[:, pl.ds(row, rows)])
        outs.extend(run_copies([pair], out_sems, len(outs)))

    none, block, both = (99, 99), (4, 12), (3, 13)
    sweep(operator_plane, e0, e1, ccoef, E1, -1, 1, 0, block)
    sweep(operator_plane, e0, e1, ccoef, E1, 0, 5, 1, both)
    save(E0, 48)
    sweep(source_plane, wide, v0, pcoef, V0, -3, 1, 0, none)
    sweep(source_plane, wide, v0, pcoef, V0, -2, 1, 1, none)
    sweep(source_plane, wide, v0, pcoef, V0, -1, 1, 2, both)
    sweep(source_plane, wide, v0, pcoef, V0, 0, 1, 3, both)
    save(V0, 32)
    sweep(operator_plane, v0, v1, ccoef, V1, -2, 1, 0, none)
    sweep(operator_plane, v0, v1, ccoef, V1, -1, 1, 1, both)
    sweep(operator_plane, v0, v1, ccoef, V1, 0, 2, 2, both)
    save(V1, 32)
    sweep(operator_plane, v1, v2, ccoef, V2, -1, 1, 0, block)
    sweep(operator_plane, v1, v2, ccoef, V2, 0, 3, 1, both)
    save(V2, 32)
    sweep(operator_plane, v2, None, ccoef, V3, 0, 4, 0, block)
    sweep(operator_plane, e1, None, ccoef, E2, 0, 4, 0, block)

    gram[...] = first_gram[...]

    def gram_step(i, carry):
        gram[...] += gram_of(s_ref, i)
        return carry

    lax.fori_loop(1, 9, gram_step, 0, unroll=8)

    def rows_of(row):
        if row == E0:
            return gram[row : row + F, :]
        return gram[row : row + F, :] + gram[row + F : row + 2 * F, :]

    summed = {row: rows_of(row) for row in (V0, V1, V2, E0, E1)}

    def block_of(row, col):
        rows = summed[row]
        if col == E0:
            return rows[:, col : col + F]
        return rows[:, col : col + F] + rows[:, col + F : col + 2 * F]

    order = [
        (V0, V0), (V0, V1), (V1, V1), (V1, V2), (V2, V2), (V2, V3), (V0, E0), (V1, E0),
        (V2, E0), (E0, V3), (E1, V3), (E0, E0), (E0, E1), (E1, E1), (E1, E2),
    ]
    blocks = [block_of(r, c) for r, c in order] + [jnp.zeros((F, F), jnp.float32)]
    pay_ref[0:16, :] = jnp.concatenate(blocks[:8], axis=1)
    pay_ref[16:32, :] = jnp.concatenate(blocks[8:], axis=1)
    wait_all(outs)


def edge(ids, a, b, a_corner, b_corner, wide, v0, v1, v2, side, gram):
    vmem = pl.BlockSpec(memory_space=pltpu.VMEM)
    hbm = pl.BlockSpec(memory_space=pltpu.HBM)
    shape = jax.ShapeDtypeStruct
    field = shape(FIELD, jnp.float32)
    outs = pl.pallas_call(
        edge_kernel,
        out_shape=(
            shape((24, 288, LANES), jnp.float32),
            field, field, field,
            shape((32, LANES), jnp.float32),
            pltpu.HBM((10, KEPT, WIDE), jnp.bfloat16),
            pltpu.HBM((18, 160, LANES), jnp.float32),
        ),
        in_specs=[vmem] * 11,
        out_specs=(vmem,) * 5 + (hbm,) * 2,
        scratch_shapes=[pltpu.VMEM(FIELD, jnp.float32)] * 2
        + [
            pltpu.VMEM((11, ALL_ROWS, WIDE), jnp.bfloat16),
            pltpu.VMEM((KEPT, ALL_ROWS), jnp.float32),
        ]
        + [pltpu.VMEM(COEFF, jnp.float32)] * 10
        + [pltpu.SemaphoreType.DMA((5,))],
        input_output_aliases={5: 0, 6: 1, 7: 2, 8: 3},
        compiler_params=pltpu.CompilerParams(vmem_limit_bytes=VMEM_EDGE * MB),
        name="edge",
    )(ids, a, b, a_corner, b_corner, wide, v0, v1, v2, side, gram)
    return outs[4:]


def matmul(a, b, dims=((1,), (0,))):
    return lax.dot_general(
        a, b, (dims, ((), ())), precision=HIGHEST, preferred_element_type=jnp.float32
    )


def galerkin(m0, m1, m2, m3):
    a12 = m2 + SHIFT * m1
    work = jnp.concatenate(
        [
            jnp.concatenate([m1 + SHIFT * m0, a12, m0], axis=1),
            jnp.concatenate([a12, m3 + SHIFT * m2, m1], axis=1),
        ],
        axis=0,
    )
    work = jnp.concatenate([work, jnp.zeros((2 * F, LANES - 3 * F), jnp.float32)], axis=1)
    return eliminate(work)[:, 2 * F : 3 * F]


def eliminate(work, size=8):
    count = work.shape[0]
    sub = lax.broadcasted_iota(jnp.int32, work.shape, 0)

    def column(k):
        return jnp.take_along_axis(work, jnp.full(work.shape, k, jnp.int32), axis=1)

    def row(v, k):
        return jnp.broadcast_to(v[k : k + 1, :], (8, LANES))

    def tall(v):
        return jnp.concatenate([v] * (count // 8), axis=0)

    for k in range(0, count, size):
        cols = [column(k + j) for j in range(size)]
        rows = [row(work, k + i) for i in range(size)]
        p = [[row(cols[j], k + i) for j in range(size)] for i in range(size)]
        for s in range(0, size, 2):
            a, b, c, d = p[s][s], p[s][s + 1], p[s + 1][s], p[s + 1][s + 1]
            inverse = 1.0 / (a * d - b * c)
            a, b, c, d = d * inverse, -(b * inverse), -(c * inverse), a * inverse
            rows[s], rows[s + 1] = a * rows[s] + b * rows[s + 1], c * rows[s] + d * rows[s + 1]
            for j in range(s + 2, size):
                u, v = p[s][j], p[s + 1][j]
                p[s][j], p[s + 1][j] = a * u + b * v, c * u + d * v
            for i in range(size):
                if i in (s, s + 1):
                    continue
                u, v = p[i][s], p[i][s + 1]
                rows[i] = rows[i] - u * rows[s] - v * rows[s + 1]
                for j in range(s + 2, size):
                    p[i][j] = p[i][j] - u * p[s][j] - v * p[s + 1][j]
        for j in range(size):
            work = work - cols[j] * tall(rows[j])
        for j in range(size):
            work = jnp.where(sub == k + j, tall(rows[j]), work)
    return work


def final_kernel(
    pattern_ref, parts_ref, bg_hbm, mid_hbm, edge_hbm,
    out_ref, sens_ref, bg, adj, s_ref, mix_ref, sems, *, damping,
):
    pairs = [
        (edge_hbm.at[pl.ds(0, 5)], s_ref.at[pl.ds(0, 5)]),
        (mid_hbm, s_ref.at[pl.ds(5, 8)]),
        (edge_hbm.at[pl.ds(5, 5)], s_ref.at[pl.ds(13, 5)]),
        (bg_hbm, bg),
    ]
    copies = [pltpu.make_async_copy(s, d, sems.at[i]) for i, (s, d) in enumerate(pairs)]

    @pl.when(lax.axis_index("gx") >= 0)
    def _():
        for c in copies:
            c.start()

    total = jnp.sum(parts_ref[...], axis=0)

    def part(k):
        r, c = (k // 8) * F, (k % 8) * F
        return total[r : r + F, c : c + F]

    m = [part(k) for k in range(6)]
    p = [part(6), part(7), part(8), part(9).T, part(10).T]
    e = [part(k) for k in range(11, 15)]
    y = galerkin(*m[:4])

    lane = lax.broadcasted_iota(jnp.int32, (F, F), 1)
    sub = lax.broadcasted_iota(jnp.int32, (F, F), 0)
    first, second = jnp.zeros((F, F), jnp.int32), jnp.zeros((F, F), jnp.int32)
    for i in range(F):
        first = jnp.where(sub == i, pattern_ref[i, 0], first)
        second = jnp.where(sub == i, pattern_ref[i, 1], second)
    pairing = jnp.where(lane == first, 1.0, 0.0) - jnp.where(lane == second, 1.0, 0.0)
    w = matmul(8.0 * matmul(pairing, pairing, ((0,), (0,))), jnp.concatenate(p[:2], axis=0), ((1,), (1,)))
    forms = []
    for k in range(4):
        inside = jnp.concatenate(
            [
                jnp.concatenate([m[k], m[k + 1]], axis=1),
                jnp.concatenate([m[k + 1], m[k + 2]], axis=1),
            ],
            axis=0,
        )
        across = matmul(jnp.concatenate([p[k], p[k + 1]], axis=0), w)
        local = matmul(w, matmul(e[k], w), ((0,), (0,)))
        forms.append(damping * (damping * inside + across + across.T) + local)
    hy = matmul(jnp.concatenate(forms, axis=0), y)
    moments = [matmul(y, hy[32 * k : 32 * (k + 1)], ((0,), (0,))) for k in range(4)]
    z = jnp.concatenate([damping * y, matmul(w, y)], axis=0)
    q = galerkin(*moments)
    z0, z1 = matmul(z, q[0:F]), matmul(z, q[F:])
    none = jnp.zeros((F, F), jnp.float32)
    mix = [
        jnp.concatenate([y[0:F], z0[0:F]], axis=1),
        jnp.concatenate([y[F:], z0[F : 2 * F] + z1[0:F]], axis=1),
        jnp.concatenate([none, z1[F : 2 * F]], axis=1),
        jnp.concatenate([none, z0[2 * F :]], axis=1),
        jnp.concatenate([none, z1[2 * F :]], axis=1),
    ]
    mix = [mix[i] for i in (0, 0, 1, 1, 2, 2, 3, 4, 4)]
    mix = jnp.concatenate(mix, axis=0).T
    hi = mix.astype(jnp.bfloat16)
    mix_ref[0:32, :] = hi
    mix_ref[32:64, :] = (mix - hi.astype(jnp.float32)).astype(jnp.bfloat16)
    wait_all(copies)
    both = mix_ref[...]

    def combine(x, lanes):
        out = jnp.dot(both, s_ref[x, :, lanes], preferred_element_type=jnp.float32)
        return out[0:32] + out[32:64]

    def store(x, out):
        for k in range(10):
            cols = slice(k * LANES, (k + 1) * LANES)
            if 0 < k < 9:
                out_ref[pl.ds(x * 8 + k - 9, F, stride=128), :] = out[0:F, cols]
            adj[x, tile_at(k), :] = out[F:, cols]

    def store_end(x, out):
        for k in range(8):
            adj[x, tile_at(k + 1), :] = out[F:, k * LANES : (k + 1) * LANES]

    lane = lane_ids(F)

    def sens_plane(x):
        b, a = bg[x, tile_at(1), :], adj[x, tile_at(1), :]
        before = (b - bg[x, tile_at(0), :]) * (a - adj[x, tile_at(0), :])
        for k in range(1, 9):
            bn, an = bg[x, tile_at(k + 1), :], adj[x, tile_at(k + 1), :]
            after = (bn - b) * (an - a)
            total = before + after
            for s in (x - 1, x + 1):
                total = total + (bg[s, tile_at(k), :] - b) * (adj[s, tile_at(k), :] - a)
            bu = jnp.where(lane == LANES - 1, 0.0, pltpu.roll(b, LANES - 1, 1))
            au = jnp.where(lane == LANES - 1, 0.0, pltpu.roll(a, LANES - 1, 1))
            bd = jnp.where(lane == 0, 0.0, pltpu.roll(b, 1, 1))
            ad = jnp.where(lane == 0, 0.0, pltpu.roll(a, 1, 1))
            total = total + (bu - b) * (au - a) + (bd - b) * (ad - a)
            sens_ref[x - 1, k - 1 : k, :] = -0.5 * jnp.sum(total, axis=0, keepdims=True)
            before, b, a = after, bn, an

    ends = slice(LANES, 9 * LANES)
    store_end(0, combine(0, ends))
    store(1, combine(1, slice(0, WIDE)))
    store(2, combine(2, slice(0, WIDE)))

    def plane(x, carry):
        out = combine(x + 2, slice(0, WIDE))
        sens_plane(x)
        store(x + 2, out)
        return carry

    lax.fori_loop(1, 15, plane, 0, unroll=7)
    out = combine(17, ends)
    sens_plane(15)
    store_end(17, out)
    sens_plane(16)


def final(pattern, parts, bg, mid, edges, damping):
    vmem = pl.BlockSpec(memory_space=pltpu.VMEM)
    hbm = pl.BlockSpec(memory_space=pltpu.HBM)

    def kernel(*refs):
        final_kernel(*refs, damping=damping)

    return pl.pallas_call(
        kernel,
        out_shape=(
            jax.ShapeDtypeStruct((2048, LANES), jnp.float32),
            jax.ShapeDtypeStruct((16, 8, LANES), jnp.float32),
        ),
        in_specs=[pl.BlockSpec(memory_space=pltpu.SMEM), vmem] + [hbm] * 3,
        scratch_shapes=[
            pltpu.VMEM((18, 160, LANES), jnp.float32),
            pltpu.VMEM((18, 160, LANES), jnp.float32),
            pltpu.VMEM((18, KEPT, WIDE), jnp.bfloat16),
            pltpu.VMEM((64, KEPT), jnp.bfloat16),
            pltpu.SemaphoreType.DMA((4,)),
        ],
        compiler_params=pltpu.CompilerParams(vmem_limit_bytes=56 * MB),
        name="final",
    )(pattern, parts, bg, mid, edges)


def spread(block, axis, count, groups=None):
    copies = jnp.broadcast_to(block[None], (count,) + block.shape)
    return lax.all_to_all(copies, axis, 0, 0, axis_index_groups=groups)


def swaps(first, count):
    lows = range(first, count - 1, 2)
    return [(i, i + 1) for i in lows] + [(i + 1, i) for i in lows]


def on_device(background, conductivity, perturbation, electrodes, pattern):
    size_x, size_y, size_z = conductivity.shape
    count_x, count_y = lax.axis_size("gx"), lax.axis_size("gy")
    wide, core, chip, a, b, ids = pack(background, conductivity, perturbation, electrodes)
    a = lax.ppermute(a, "gx", swaps(0, count_x))
    b = lax.ppermute(b, "gx", swaps(1, count_x))
    chip = lax.ppermute(chip, "gy", swaps(1, count_y))
    core = lax.ppermute(core, "gy", swaps(0, count_y))
    a_corner, b_corner = pack_corners(core, chip)
    a_corner = lax.ppermute(a_corner, "gx", swaps(0, count_x))
    b_corner = lax.ppermute(b_corner, "gx", swaps(1, count_x))
    wide, v0, v1, v2, side, gram, mid = inner(ids, wide, core, chip)
    pay, edges, bg = edge(
        ids, a, b, a_corner, b_corner, wide, v0, v1, v2, side, gram
    )
    pay = pay + lax.ppermute(pay, "gy", swaps(0, count_y))
    pay = jnp.sum(spread(pay, "gx", count_x), axis=0)
    chips = count_y // 2
    groups = [[2 * i + c for i in range(chips)] for c in range(2)]
    parts = spread(pay, "gy", chips, groups)
    cells = size_x * size_y * size_z * count_x * count_y
    damping = 80.0 / math.sqrt(cells)
    tangent, sens = final(pattern, parts, bg, mid, edges, damping)
    return tangent.reshape(background.shape), sens


def solution(mesh):
    in_specs = (P(None, "gx", "gy", None), P("gx", "gy", None), P("gx", "gy", None), P(), P())
    out_specs = (P(None, "gx", "gy", None), P("gx", "gy", None))
    return jax.shard_map(
        on_device, mesh=mesh, in_specs=in_specs, out_specs=out_specs, check_vma=False
    )
```

```python
import math

import jax
import jax.numpy as jnp
from jax import lax
from jax.experimental import pallas as pl
from jax.experimental.pallas import tpu as pltpu
from jax.sharding import PartitionSpec as P

SHIFT = 12.0
F = 16
LANES = 128
HALO = 4
HIGHEST = lax.Precision.HIGHEST
V0, V1, V2, E0, E1, V3, E2 = 0, 32, 64, 96, 112, 144, 176
KEPT, ALL_ROWS = 144, 208
WIDE = 10 * LANES
MB = 2**20
FIELD = (24, 256, LANES)
COEFF = (24, 16, LANES)


def tile_at(y):
    return slice(y * F, (y + 1) * F)


def run_copies(pairs, sems, first=0):
    copies = [
        pltpu.make_async_copy(s, d, sems.at[first + i]) for i, (s, d) in enumerate(pairs)
    ]
    for c in copies:
        c.start()
    return copies


def wait_all(copies):
    for c in copies:
        c.wait()


def odd(axis):
    return lax.rem(lax.axis_index(axis), 2) == 1


PARTS = 4


def pack_kernel(
    bg_hbm, cond_hbm, pert_hbm, elec_hbm, pattern_hbm,
    wide_ref, core_ref, chip_ref, a_ref, b_ref, ids_ref, pairing_ref,
    bg, cond_v, pert_v, elec, pattern, pairing, sems,
):
    size_x, size_y = cond_v.shape[0], cond_v.shape[1]
    each = size_x // PARTS
    pairs = [(cond_hbm, cond_v), (pert_hbm, pert_v), (elec_hbm, elec), (pattern_hbm, pattern)]
    for i in range(PARTS):
        planes = pl.ds(i * each, each)
        pairs.append((bg_hbm.at[:, planes], bg.at[:, planes]))
    copies = run_copies(pairs, sems)

    wait_all(copies[:4])
    sub = lax.broadcasted_iota(jnp.int32, (F, LANES), 0)
    ids = jnp.zeros((F, LANES), jnp.int32)
    for e in range(F):
        ids = jnp.where(sub == e, elec[e], ids)
    ids_ref[...] = ids - lane_ids(F)
    sub = lax.broadcasted_iota(jnp.int32, (F, F), 0)
    first = jnp.where(sub == pattern[0:1, :], 1.0, 0.0)
    pairing[:, 0:F] = first - jnp.where(sub == pattern[1:2, :], 1.0, 0.0)
    outs = run_copies([(pairing, pairing_ref)], sems, 4 + PARTS)

    def fill(top_ref, bottom_ref):
        def plane(x, carry):
            for y in range(size_y):
                tile = bg[:, x, y, :]
                wide_ref[x + HALO, tile_at(y + HALO), :] = tile
                if y >= size_y - HALO:
                    top_ref[x, tile_at(y - size_y + HALO), :] = tile
                if y < HALO:
                    bottom_ref[x, tile_at(y), :] = tile
            cond, pert = cond_v[x], pert_v[x]
            wide_ref[x + HALO, 256:264, :] = cond
            wide_ref[x + HALO, 264:272, :] = pert
            top_ref[x, 64:72, :] = jnp.concatenate([cond[4:8], pert[4:8]], axis=0)
            bottom_ref[x, 64:72, :] = jnp.concatenate([cond[0:4], pert[0:4]], axis=0)
            return carry

        for i in range(PARTS):
            copies[4 + i].wait()
            lax.fori_loop(i * each, (i + 1) * each, plane, 0, unroll=each)

    @pl.when(odd("gy"))
    def _():
        fill(chip_ref, core_ref)

    @pl.when(jnp.logical_not(odd("gy")))
    def _():
        fill(core_ref, chip_ref)

    for out, up in ((a_ref, jnp.logical_not(odd("gx"))), (b_ref, odd("gx"))):
        for dx in range(1, HALO + 1):
            x = HALO + jnp.where(up, size_x - dx, dx - 1)
            out[dx - 1, 0:128, :] = wide_ref[x, 64:192, :]
            out[dx - 1, 128:144, :] = wide_ref[x, 256:272, :]
    wait_all(outs)


def pack(background, conductivity, perturbation, electrodes, pattern):
    shape = jax.ShapeDtypeStruct
    inputs = [
        pltpu.with_memory_space_constraint(v, pltpu.HBM)
        for v in (background, conductivity, perturbation, electrodes, pattern.T)
    ]
    return pl.pallas_call(
        pack_kernel,
        out_shape=(
            shape((24, 288, LANES), jnp.float32),
            shape((16, 72, LANES), jnp.float32),
            shape((16, 72, LANES), jnp.float32),
            shape((HALO, 144, LANES), jnp.float32),
            shape((HALO, 144, LANES), jnp.float32),
            shape((F, LANES), jnp.int32),
            pltpu.HBM((F, LANES), jnp.float32),
        ),
        in_specs=[pl.BlockSpec(memory_space=pltpu.HBM)] * 5,
        out_specs=(pl.BlockSpec(memory_space=pltpu.VMEM),) * 6
        + (pl.BlockSpec(memory_space=pltpu.HBM),),
        scratch_shapes=[
            pltpu.VMEM((16, 16, 8, LANES), jnp.float32),
            pltpu.VMEM((16, 8, LANES), jnp.float32),
            pltpu.VMEM((16, 8, LANES), jnp.float32),
            pltpu.SMEM((F,), jnp.int32),
            pltpu.VMEM((2, F), jnp.int32),
            pltpu.VMEM((F, LANES), jnp.float32),
            pltpu.SemaphoreType.DMA((5 + PARTS,)),
        ],
        compiler_params=pltpu.CompilerParams(vmem_limit_bytes=16 * MB),
        name="pack_y",
    )(*inputs)


def corner_layout():
    table, at = [], 0
    for dx in range(1, HALO):
        rows = (HALO - dx) * F
        table.append((dx, rows, at))
        at += 2 * rows + 16
    return table, at


CORNERS, CORNER_ROWS = corner_layout()


def pack_corners_kernel(core_ref, chip_ref, a_ref, b_ref):
    def send(left_ref, right_ref):
        for out, up in ((a_ref, jnp.logical_not(odd("gx"))), (b_ref, odd("gx"))):
            for dx, rows, at in CORNERS:
                x = jnp.where(up, left_ref.shape[0] - dx, dx - 1)
                out[at : at + rows, :] = left_ref[x, 64 - rows : 64, :]
                out[at + rows : at + 2 * rows, :] = right_ref[x, 0:rows, :]
                at += 2 * rows
                out[at : at + 8, :] = left_ref[x, 64:72, :]
                out[at + 8 : at + 16, :] = right_ref[x, 64:72, :]

    @pl.when(odd("gy"))
    def _():
        send(core_ref, chip_ref)

    @pl.when(jnp.logical_not(odd("gy")))
    def _():
        send(chip_ref, core_ref)


def pack_corners(core, chip):
    shape = jax.ShapeDtypeStruct((CORNER_ROWS, LANES), jnp.float32)
    return pl.pallas_call(
        pack_corners_kernel,
        out_shape=(shape, shape),
        compiler_params=pltpu.CompilerParams(vmem_limit_bytes=16 * MB),
        name="pack_corners",
    )(core, chip)


def lane_ids(rows):
    return lax.broadcasted_iota(jnp.int32, (rows, LANES), 1)


def faces(wide, x, ccoef, pcoef):
    lane = lane_ids(16)
    last = lane == LANES - 1
    edge = (lane == 0) | last

    def cells(x):
        own, left, right = wide[x, 256:272, :], wide[x, 272:280, :], wide[x, 280:288, :]
        return (
            jnp.concatenate([left[0:4], own[0:8], right[0:4]], axis=0),
            jnp.concatenate([left[4:8], own[8:16], right[4:8]], axis=0),
        )

    before, now, then = cells(jnp.maximum(x - 1, 0)), cells(x), cells(x + 1)
    for which, coef, half in ((0, ccoef, 0.5), (1, pcoef, -0.5)):
        c, n = now[which], then[which]
        fx, fy, fu, fd, dd = coef
        east = half * (c + n)
        south = half * (c + pltpu.roll(c, 15, 0))
        up = jnp.where(last, 0.0, half * (c + pltpu.roll(c, LANES - 1, 1)))
        down = pltpu.roll(up, 1, 1)
        rest = jnp.where(edge, half * c, 0.0)
        if which == 0:
            west = half * (c + before[0])
            sides = (east + west) + (south + pltpu.roll(south, 1, 0)) + (up + down)
            rest = (0.05 - SHIFT) + rest + sides
        fx[x], fy[x], fu[x], fd[x], dd[x] = east, south, up, down, rest


def source_plane(get, coeffs, x, y0, y1, mask_x, mask_y, emit):
    fx, fy, fu, fd, dd = coeffs
    q = get(x, y0)
    flux = fy[x, y0 - 1 : y0, :] * (q - get(x, y0 - 1))
    for y in range(y0, y1):
        nxt = get(x, y + 1)
        row = slice(y, y + 1)
        later = fy[x, row, :] * (nxt - q)
        out = dd[x, row, :] * q + (flux - later)
        out = out + fx[x - 1, row, :] * (q - get(x - 1, y))
        out = out - fx[x, row, :] * (get(x + 1, y) - q)
        out = out + fd[x, row, :] * (q - pltpu.roll(q, 1, 1))
        out = out - fu[x, row, :] * (pltpu.roll(q, LANES - 1, 1) - q)
        emit(y, masked(out, y, mask_x, mask_y))
        flux, q = later, nxt


def operator_plane(get, coeffs, x, y0, y1, mask_x, mask_y, emit):
    fx, fy, fu, fd, dd = coeffs
    before, q = get(x, y0 - 1), get(x, y0)
    north = fy[x, y0 - 1 : y0, :]
    for y in range(y0, y1):
        nxt = get(x, y + 1)
        row = slice(y, y + 1)
        south = fy[x, row, :]
        out = dd[x, row, :] * q - north * before - south * nxt
        across = fx[x - 1, row, :] * get(x - 1, y) + fx[x, row, :] * get(x + 1, y)
        depth = fd[x, row, :] * pltpu.roll(q, 1, 1) + fu[x, row, :] * pltpu.roll(q, LANES - 1, 1)
        emit(y, masked(out - (across + depth), y, mask_x, mask_y))
        before, q, north = q, nxt, south


def masked(out, y, mask_x, mask_y):
    mask = mask_x
    if y < 4:
        mask = mask_y[0] if mask is None else mask * mask_y[0]
    elif y >= 12:
        mask = mask_y[1] if mask is None else mask * mask_y[1]
    return out if mask is None else out * mask


def tiles(ref):
    return lambda x, y: ref[x, tile_at(y), :]


def put_split(s_ref, i, row, y, value, exact=False):
    lanes = slice((y - 3) * LANES, (y - 2) * LANES)
    hi = value.astype(jnp.bfloat16)
    s_ref[i, row : row + F, lanes] = hi
    if not exact:
        lo = (value - hi.astype(jnp.float32)).astype(jnp.bfloat16)
        s_ref[i, row + F : row + 2 * F, lanes] = lo


def grid_masks():
    one, zero = jnp.float32(1), jnp.float32(0)
    masks = []
    for axis in ("gx", "gy"):
        i = lax.axis_index(axis)
        low, high = i > 0, i < lax.axis_size(axis) - 1
        masks.append((jnp.where(low, one, zero), jnp.where(high, one, zero)))
    return masks


def unit_plane(ids, at_x, e0, i, s_ref, s_at):
    size_x, size_y = 16 * lax.axis_size("gx"), 8 * lax.axis_size("gy")
    good_x = (at_x >= 0) & (at_x < size_x)
    for y in range(2, 14):
        at_y = lax.axis_index("gy") * 8 + y - 4
        good = good_x & (at_y >= 0) & (at_y < size_y)
        here = jnp.where(good, (at_x * size_y + at_y) * LANES, -(2**20))
        value = jnp.where(ids == here, 1.0, 0.0)
        e0[i, tile_at(y), :] = value
        if 3 <= y < 13:
            put_split(s_ref, s_at, E0, y, value, exact=True)


def gram_of(s_ref, i):
    return lax.dot_general(
        s_ref[i, 0:KEPT, LANES : 9 * LANES],
        s_ref[i, :, LANES : 9 * LANES],
        (((1,), (1,)), ((), ())),
        preferred_element_type=jnp.float32,
    )


def prepare_planes(wide, ccoef, pcoef):
    def prepare(x, carry):
        faces(wide, x, ccoef, pcoef)
        return carry

    lax.fori_loop(HALO, HALO + 15, prepare, 0, unroll=3)


def sweep_planes(stencil, src, dst, coeffs, first, ranges, mask_y, s_ref, row, keep, unroll=2):
    def plane(x, carry):
        def emit(y, out):
            if dst is not None:
                dst[x, tile_at(y), :] = out
            if keep[0] <= y < keep[1]:
                put_split(s_ref, x - HALO, row, y, out)

        for y0, y1 in ranges:
            stencil(tiles(src), coeffs, x, y0, y1, None, mask_y, emit)
        return carry

    lax.fori_loop(HALO + first, HALO + 16 - first, plane, 0, unroll=unroll)


BLOCK, BOTH = (4, 12), (3, 13)


def early_kernel(
    ids_ref, wide, v0, v1, v2, e0, e1, s_ref, cx, cy, cu, cd, cr, px, py, pu, pd, pr
):
    gx = lax.axis_index("gx")
    ids = ids_ref[...]
    ccoef, pcoef = (cx, cy, cu, cd, cr), (px, py, pu, pd, pr)
    prepare_planes(wide, ccoef, pcoef)

    def units(x, carry):
        unit_plane(ids, gx * 16 + x - HALO, e0, x, s_ref, x - HALO)
        return carry

    lax.fori_loop(6, 18, units, 0, unroll=2)

    def sweep(stencil, src, dst, coeffs, first, rows, row):
        sweep_planes(stencil, src, dst, coeffs, first, [rows], None, s_ref, row, rows)

    sweep(source_plane, wide, v0, pcoef, 1, (5, 11), V0)
    sweep(operator_plane, v0, v1, ccoef, 2, (6, 10), V1)
    sweep(operator_plane, v1, v2, ccoef, 3, (7, 9), V2)
    sweep(operator_plane, e0, e1, ccoef, 3, (5, 11), E1)
    sweep(operator_plane, e1, None, ccoef, 4, (6, 10), E2)


def early(ids, wide):
    vmem = pl.BlockSpec(memory_space=pltpu.VMEM)
    field = jax.ShapeDtypeStruct(FIELD, jnp.float32)
    return pl.pallas_call(
        early_kernel,
        out_shape=(field,) * 5 + (jax.ShapeDtypeStruct((16, ALL_ROWS, WIDE), jnp.bfloat16),),
        in_specs=[vmem] * 2,
        out_specs=(vmem,) * 6,
        scratch_shapes=[pltpu.VMEM(COEFF, jnp.float32)] * 10,
        compiler_params=pltpu.CompilerParams(vmem_limit_bytes=10 * MB),
        cost_estimate=pl.CostEstimate(
            flops=10**9, bytes_accessed=8 * 10**6, transcendentals=0
        ),
        name="early",
    )(ids, wide)


def inner_kernel(
    wide_in, v0_in, v1_in, v2_in, e0_in, e1_in, s_in, core_ref, chip_ref,
    wide, v0, v1, v2, e0, e1, s_ref, side_ref, gram_ref, s_hbm,
    cx, cy, cu, cd, cr, px, py, pu, pd, pr, out_sems,
):
    del wide_in, v0_in, v1_in, v2_in, e0_in, e1_in, s_in

    def fill(left_ref, right_ref):
        def plane(x, carry):
            wide[x + HALO, 0:64, :] = left_ref[x, 0:64, :]
            wide[x + HALO, 192:256, :] = right_ref[x, 0:64, :]
            wide[x + HALO, 272:280, :] = left_ref[x, 64:72, :]
            wide[x + HALO, 280:288, :] = right_ref[x, 64:72, :]
            return carry

        lax.fori_loop(0, 16, plane, 0, unroll=4)

    @pl.when(odd("gy"))
    def _():
        fill(core_ref, chip_ref)

    @pl.when(jnp.logical_not(odd("gy")))
    def _():
        fill(chip_ref, core_ref)

    _, mask_y = grid_masks()
    ccoef, pcoef = (cx, cy, cu, cd, cr), (px, py, pu, pd, pr)
    prepare_planes(wide, ccoef, pcoef)
    outs = []

    def hand_on(src, dst):
        outs.extend(run_copies([(src, dst)], out_sems, len(outs)))

    def sweep(stencil, src, dst, coeffs, first, reach, done, row, keep):
        y0, y1 = 4 - reach, 12 + reach
        ranges = [(y0, done[0]), (done[1], y1)] if done else [(y0, y1)]
        sweep_planes(stencil, src, dst, coeffs, first, ranges, mask_y, s_ref, row, keep)

    sweep(source_plane, wide, v0, pcoef, 1, 3, (5, 11), V0, BOTH)
    sweep(operator_plane, v0, v1, ccoef, 2, 2, (6, 10), V1, BOTH)
    sweep(operator_plane, v1, v2, ccoef, 3, 1, (7, 9), V2, BOTH)
    hand_on(s_ref.at[pl.ds(1, 3), pl.ds(0, 96)], side_ref.at[pl.ds(0, 3)])
    hand_on(s_ref.at[pl.ds(12, 3), pl.ds(0, 96)], side_ref.at[pl.ds(3, 3)])
    sweep(operator_plane, e0, e1, ccoef, 3, 1, (5, 11), E1, BOTH)
    hand_on(s_ref.at[pl.ds(4, 8), pl.ds(0, KEPT)], s_hbm)
    sweep(operator_plane, v2, None, ccoef, 4, 0, None, V3, BLOCK)
    sweep(operator_plane, e1, None, ccoef, 4, 0, (6, 10), E2, BLOCK)

    gram_ref[...] = gram_of(s_ref, 4)

    def gram_step(x, carry):
        gram_ref[...] += gram_of(s_ref, x)
        return carry

    lax.fori_loop(5, 12, gram_step, 0, unroll=7)
    wait_all(outs)


def inner(wide, fields, core, chip):
    vmem = pl.BlockSpec(memory_space=pltpu.VMEM)
    shape = jax.ShapeDtypeStruct
    field = shape(FIELD, jnp.float32)
    return pl.pallas_call(
        inner_kernel,
        out_shape=(
            shape((24, 288, LANES), jnp.float32),
            field, field, field, field, field,
            shape((16, ALL_ROWS, WIDE), jnp.bfloat16),
            shape((6, 96, WIDE), jnp.bfloat16),
            shape((KEPT, ALL_ROWS), jnp.float32),
            pltpu.HBM((8, KEPT, WIDE), jnp.bfloat16),
        )
        + (shape(COEFF, jnp.float32),) * 10,
        in_specs=[vmem] * 9,
        out_specs=(vmem,) * 9 + (pl.BlockSpec(memory_space=pltpu.HBM),) + (vmem,) * 10,
        scratch_shapes=[pltpu.SemaphoreType.DMA((3,))],
        input_output_aliases={i: i for i in range(7)},
        compiler_params=pltpu.CompilerParams(vmem_limit_bytes=10 * MB),
        cost_estimate=pl.CostEstimate(
            flops=4 * 10**9, bytes_accessed=16 * 10**6, transcendentals=0
        ),
        name="inner",
    )(wide, *fields, core, chip)


def edge_kernel(
    ids_ref, a_ref, b_ref, a_corner, b_corner, side_ref, first_gram, *refs
):
    wide, v0, v1, v2, *coeffs = refs[14:28]
    pay_ref, s_hbm, bg_hbm, e0, e1, s_ref, gram, out_sems = refs[28:]
    gx = lax.axis_index("gx")
    mask_x, mask_y = grid_masks()
    ids = ids_ref[...]

    def halo_plane(high, dx):
        return jnp.where(high, 19 + dx, HALO - dx)

    sides = ((a_ref, a_corner, jnp.logical_not(odd("gx"))), (b_ref, b_corner, odd("gx")))
    for ref, corner, high in sides:
        for dx in range(1, HALO + 1):
            x = halo_plane(high, dx)
            wide[x, 64:192, :] = ref[dx - 1, 0:128, :]
            wide[x, 256:272, :] = ref[dx - 1, 128:144, :]
        for dx, rows, at in CORNERS:
            x = halo_plane(high, dx)
            wide[x, 64 - rows : 64, :] = corner[at : at + rows, :]
            wide[x, 192 : 192 + rows, :] = corner[at + rows : at + 2 * rows, :]
            wide[x, 272:288, :] = corner[at + 2 * rows : at + 2 * rows + 16, :]

    outs = run_copies([(wide.at[pl.ds(3, 18), pl.ds(48, 160)], bg_hbm)], out_sems)

    for i in range(3):
        rows = 96 - 32 * (2 - i)
        s_ref[2 + i, 0:rows, :] = side_ref[i, 0:rows, :]
        s_ref[7 - i, 0:rows, :] = side_ref[5 - i, 0:rows, :]

    ccoef, pcoef = coeffs[:5], coeffs[5:]

    def prepare(i, carry):
        faces(wide, jnp.where(i < 5, i, i + 14), ccoef, pcoef)
        return carry

    lax.fori_loop(0, 9, prepare, 0, unroll=3)

    def mirrored(low, count, body):
        for x in range(low, low + count):
            inside = -1 <= x <= 3
            body(HALO + x, x + 1 if inside else 10, mask_x[0])
            body(19 - x, 8 - x if inside else 10, mask_x[1])

    mirrored(-2, 8, lambda at, s_at, _: unit_plane(ids, gx * 16 + at - HALO, e0, at, s_ref, s_at))

    def sweep(stencil, src, dst, coeffs, row, low, count, near, keep):
        def body(at, s_at, mask):
            def emit(y, out):
                if dst is not None:
                    dst[at, tile_at(y), :] = out
                if keep[0] <= y < keep[1]:
                    put_split(s_ref, s_at, row, y, out)

            mask = mask if low < 0 else None
            stencil(tiles(src), coeffs, at, 4 - near, 12 + near, mask, mask_y, emit)

        mirrored(low, count, body)

    def save(row, rows):
        pair = (s_ref.at[pl.ds(0, 10), pl.ds(row, rows)], s_hbm.at[:, pl.ds(row, rows)])
        outs.extend(run_copies([pair], out_sems, len(outs)))

    none, block, both = (99, 99), (4, 12), (3, 13)
    sweep(operator_plane, e0, e1, ccoef, E1, -1, 1, 0, block)
    sweep(operator_plane, e0, e1, ccoef, E1, 0, 5, 1, both)
    save(E0, 48)
    sweep(source_plane, wide, v0, pcoef, V0, -3, 1, 0, none)
    sweep(source_plane, wide, v0, pcoef, V0, -2, 1, 1, none)
    sweep(source_plane, wide, v0, pcoef, V0, -1, 1, 2, both)
    sweep(source_plane, wide, v0, pcoef, V0, 0, 1, 3, both)
    save(V0, 32)
    sweep(operator_plane, v0, v1, ccoef, V1, -2, 1, 0, none)
    sweep(operator_plane, v0, v1, ccoef, V1, -1, 1, 1, both)
    sweep(operator_plane, v0, v1, ccoef, V1, 0, 2, 2, both)
    save(V1, 32)
    sweep(operator_plane, v1, v2, ccoef, V2, -1, 1, 0, block)
    sweep(operator_plane, v1, v2, ccoef, V2, 0, 3, 1, both)
    save(V2, 32)
    sweep(operator_plane, v2, None, ccoef, V3, 0, 4, 0, block)
    sweep(operator_plane, e1, None, ccoef, E2, 0, 4, 0, block)

    gram[...] = first_gram[...]

    def gram_step(i, carry):
        gram[...] += gram_of(s_ref, i)
        return carry

    lax.fori_loop(1, 9, gram_step, 0, unroll=8)

    def rows_of(row):
        if row == E0:
            return gram[row : row + F, :]
        return gram[row : row + F, :] + gram[row + F : row + 2 * F, :]

    summed = {row: rows_of(row) for row in (V0, V1, V2, E0, E1)}

    def block_of(row, col):
        rows = summed[row]
        if col == E0:
            return rows[:, col : col + F]
        return rows[:, col : col + F] + rows[:, col + F : col + 2 * F]

    order = [
        (V0, V0), (V0, V1), (V1, V1), (V1, V2), (V2, V2), (V2, V3), (V0, E0), (V1, E0),
        (V2, E0), (E0, V3), (E1, V3), (E0, E0), (E0, E1), (E1, E1), (E1, E2),
    ]
    blocks = [block_of(r, c) for r, c in order] + [jnp.zeros((F, F), jnp.float32)]
    pay_ref[0:16, :] = jnp.concatenate(blocks[:8], axis=1)
    pay_ref[16:32, :] = jnp.concatenate(blocks[8:], axis=1)
    wait_all(outs)


def edge(ids, a, b, a_corner, b_corner, kept, side, gram):
    vmem = pl.BlockSpec(memory_space=pltpu.VMEM)
    hbm = pl.BlockSpec(memory_space=pltpu.HBM)
    shape = jax.ShapeDtypeStruct
    count = len(kept)
    outs = pl.pallas_call(
        edge_kernel,
        out_shape=tuple(shape(v.shape, v.dtype) for v in kept)
        + (
            shape((32, LANES), jnp.float32),
            pltpu.HBM((10, KEPT, WIDE), jnp.bfloat16),
            pltpu.HBM((18, 160, LANES), jnp.float32),
        ),
        in_specs=[vmem] * (7 + count),
        out_specs=(vmem,) * (count + 1) + (hbm,) * 2,
        scratch_shapes=[pltpu.VMEM(FIELD, jnp.float32)] * 2
        + [
            pltpu.VMEM((11, ALL_ROWS, WIDE), jnp.bfloat16),
            pltpu.VMEM((KEPT, ALL_ROWS), jnp.float32),
            pltpu.SemaphoreType.DMA((5,)),
        ],
        input_output_aliases={7 + i: i for i in range(count)},
        compiler_params=pltpu.CompilerParams(vmem_limit_bytes=24 * MB),
        name="edge",
    )(ids, a, b, a_corner, b_corner, side, gram, *kept)
    return outs[count:]


def matmul(a, b, dims=((1,), (0,))):
    return lax.dot_general(
        a, b, (dims, ((), ())), precision=HIGHEST, preferred_element_type=jnp.float32
    )


def galerkin(m0, m1, m2, m3):
    a12 = m2 + SHIFT * m1
    work = jnp.concatenate(
        [
            jnp.concatenate([m1 + SHIFT * m0, a12, m0], axis=1),
            jnp.concatenate([a12, m3 + SHIFT * m2, m1], axis=1),
        ],
        axis=0,
    )
    work = jnp.concatenate([work, jnp.zeros((2 * F, LANES - 3 * F), jnp.float32)], axis=1)
    return eliminate(work)[:, 2 * F : 3 * F]


def eliminate(work, size=8):
    count = work.shape[0]
    sub = lax.broadcasted_iota(jnp.int32, work.shape, 0)

    def column(k):
        return jnp.take_along_axis(work, jnp.full(work.shape, k, jnp.int32), axis=1)

    def row(v, k):
        return jnp.broadcast_to(v[k : k + 1, :], (8, LANES))

    def tall(v):
        return jnp.concatenate([v] * (count // 8), axis=0)

    for k in range(0, count, size):
        cols = [column(k + j) for j in range(size)]
        rows = [row(work, k + i) for i in range(size)]
        p = [[row(cols[j], k + i) for j in range(size)] for i in range(size)]
        for s in range(0, size, 2):
            a, b, c, d = p[s][s], p[s][s + 1], p[s + 1][s], p[s + 1][s + 1]
            inverse = 1.0 / (a * d - b * c)
            a, b, c, d = d * inverse, -(b * inverse), -(c * inverse), a * inverse
            rows[s], rows[s + 1] = a * rows[s] + b * rows[s + 1], c * rows[s] + d * rows[s + 1]
            for j in range(s + 2, size):
                u, v = p[s][j], p[s + 1][j]
                p[s][j], p[s + 1][j] = a * u + b * v, c * u + d * v
            for i in range(size):
                if i in (s, s + 1):
                    continue
                u, v = p[i][s], p[i][s + 1]
                rows[i] = rows[i] - u * rows[s] - v * rows[s + 1]
                for j in range(s + 2, size):
                    p[i][j] = p[i][j] - u * p[s][j] - v * p[s + 1][j]
        for j in range(size):
            work = work - cols[j] * tall(rows[j])
        for j in range(size):
            work = jnp.where(sub == k + j, tall(rows[j]), work)
    return work


def final_kernel(
    pairing_hbm, parts_hbm, bg_hbm, mid_hbm, edge_hbm,
    out_ref, sens_ref, pairing_ref, parts_ref, bg, adj, s_ref, mix_ref, sems, *, damping,
):
    pairs = [
        (parts_hbm, parts_ref),
        (pairing_hbm, pairing_ref),
        (edge_hbm.at[pl.ds(0, 5)], s_ref.at[pl.ds(0, 5)]),
        (mid_hbm, s_ref.at[pl.ds(5, 8)]),
        (edge_hbm.at[pl.ds(5, 5)], s_ref.at[pl.ds(13, 5)]),
        (bg_hbm, bg),
    ]
    copies = [pltpu.make_async_copy(s, d, sems.at[i]) for i, (s, d) in enumerate(pairs)]

    @pl.when(lax.axis_index("gx") >= 0)
    def _():
        for c in copies:
            c.start()
        wait_all(copies[:2])

    total = jnp.sum(parts_ref[...], axis=0)

    def part(k):
        r, c = (k // 8) * F, (k % 8) * F
        return total[r : r + F, c : c + F]

    m = [part(k) for k in range(6)]
    p = [part(6), part(7), part(8), part(9).T, part(10).T]
    e = [part(k) for k in range(11, 15)]
    y = galerkin(*m[:4])

    pairing = pairing_ref[:, 0:F]
    w = matmul(8.0 * matmul(pairing, pairing, ((1,), (1,))), jnp.concatenate(p[:2], axis=0), ((1,), (1,)))
    forms = []
    for k in range(4):
        inside = jnp.concatenate(
            [
                jnp.concatenate([m[k], m[k + 1]], axis=1),
                jnp.concatenate([m[k + 1], m[k + 2]], axis=1),
            ],
            axis=0,
        )
        across = matmul(jnp.concatenate([p[k], p[k + 1]], axis=0), w)
        local = matmul(w, matmul(e[k], w), ((0,), (0,)))
        forms.append(damping * (damping * inside + across + across.T) + local)
    hy = matmul(jnp.concatenate(forms, axis=0), y)
    moments = [matmul(y, hy[32 * k : 32 * (k + 1)], ((0,), (0,))) for k in range(4)]
    z = jnp.concatenate([damping * y, matmul(w, y)], axis=0)
    q = galerkin(*moments)
    z0, z1 = matmul(z, q[0:F]), matmul(z, q[F:])
    none = jnp.zeros((F, F), jnp.float32)
    mix = [
        jnp.concatenate([y[0:F], z0[0:F]], axis=1),
        jnp.concatenate([y[F:], z0[F : 2 * F] + z1[0:F]], axis=1),
        jnp.concatenate([none, z1[F : 2 * F]], axis=1),
        jnp.concatenate([none, z0[2 * F :]], axis=1),
        jnp.concatenate([none, z1[2 * F :]], axis=1),
    ]
    mix = [mix[i] for i in (0, 0, 1, 1, 2, 2, 3, 4, 4)]
    mix = jnp.concatenate(mix, axis=0).T
    hi = mix.astype(jnp.bfloat16)
    mix_ref[0:32, :] = hi
    mix_ref[32:64, :] = (mix - hi.astype(jnp.float32)).astype(jnp.bfloat16)
    wait_all(copies[2:])
    both = mix_ref[...]

    def combine(x, lanes):
        out = jnp.dot(both, s_ref[x, :, lanes], preferred_element_type=jnp.float32)
        return out[0:32] + out[32:64]

    def store(x, out):
        for k in range(10):
            cols = slice(k * LANES, (k + 1) * LANES)
            if 0 < k < 9:
                out_ref[pl.ds(x * 8 + k - 9, F, stride=128), :] = out[0:F, cols]
            adj[x, tile_at(k), :] = out[F:, cols]

    def store_end(x, out):
        for k in range(8):
            adj[x, tile_at(k + 1), :] = out[F:, k * LANES : (k + 1) * LANES]

    lane = lane_ids(F)

    def sens_plane(x):
        b, a = bg[x, tile_at(1), :], adj[x, tile_at(1), :]
        before = (b - bg[x, tile_at(0), :]) * (a - adj[x, tile_at(0), :])
        for k in range(1, 9):
            bn, an = bg[x, tile_at(k + 1), :], adj[x, tile_at(k + 1), :]
            after = (bn - b) * (an - a)
            total = before + after
            for s in (x - 1, x + 1):
                total = total + (bg[s, tile_at(k), :] - b) * (adj[s, tile_at(k), :] - a)
            bu = jnp.where(lane == LANES - 1, 0.0, pltpu.roll(b, LANES - 1, 1))
            au = jnp.where(lane == LANES - 1, 0.0, pltpu.roll(a, LANES - 1, 1))
            bd = jnp.where(lane == 0, 0.0, pltpu.roll(b, 1, 1))
            ad = jnp.where(lane == 0, 0.0, pltpu.roll(a, 1, 1))
            total = total + (bu - b) * (au - a) + (bd - b) * (ad - a)
            sens_ref[x - 1, k - 1 : k, :] = -0.5 * jnp.sum(total, axis=0, keepdims=True)
            before, b, a = after, bn, an

    ends = slice(LANES, 9 * LANES)
    store_end(0, combine(0, ends))
    store(1, combine(1, slice(0, WIDE)))
    store(2, combine(2, slice(0, WIDE)))

    def plane(x, carry):
        out = combine(x + 2, slice(0, WIDE))
        sens_plane(x)
        store(x + 2, out)
        return carry

    lax.fori_loop(1, 15, plane, 0, unroll=7)
    out = combine(17, ends)
    sens_plane(15)
    store_end(17, out)
    sens_plane(16)


def final(pairing, parts, bg, mid, edges, damping):
    vmem = pl.BlockSpec(memory_space=pltpu.VMEM)
    hbm = pl.BlockSpec(memory_space=pltpu.HBM)

    def kernel(*refs):
        final_kernel(*refs, damping=damping)

    return pl.pallas_call(
        kernel,
        out_shape=(
            jax.ShapeDtypeStruct((2048, LANES), jnp.float32),
            jax.ShapeDtypeStruct((16, 8, LANES), jnp.float32),
        ),
        in_specs=[hbm] * 5,
        scratch_shapes=[
            pltpu.VMEM((F, LANES), jnp.float32),
            pltpu.VMEM((F, 32, LANES), jnp.float32),
            pltpu.VMEM((18, 160, LANES), jnp.float32),
            pltpu.VMEM((18, 160, LANES), jnp.float32),
            pltpu.VMEM((18, KEPT, WIDE), jnp.bfloat16),
            pltpu.VMEM((64, KEPT), jnp.bfloat16),
            pltpu.SemaphoreType.DMA((6,)),
        ],
        compiler_params=pltpu.CompilerParams(vmem_limit_bytes=56 * MB),
        name="final",
    )(pairing, pltpu.with_memory_space_constraint(parts, pltpu.HBM), bg, mid, edges)


def spread(block, axis, count, groups=None):
    copies = jnp.broadcast_to(block[None], (count,) + block.shape)
    return lax.all_to_all(copies, axis, 0, 0, axis_index_groups=groups)


def swaps(first, count):
    lows = range(first, count - 1, 2)
    return [(i, i + 1) for i in lows] + [(i + 1, i) for i in lows]


def on_device(background, conductivity, perturbation, electrodes, pattern):
    size_x, size_y, size_z = conductivity.shape
    count_x, count_y = lax.axis_size("gx"), lax.axis_size("gy")
    wide, core, chip, a, b, ids, pairing = pack(
        background, conductivity, perturbation, electrodes, pattern
    )
    a = lax.ppermute(a, "gx", swaps(0, count_x))
    b = lax.ppermute(b, "gx", swaps(1, count_x))
    chip = lax.ppermute(chip, "gy", swaps(1, count_y))
    core = lax.ppermute(core, "gy", swaps(0, count_y))
    fields = early(ids, wide)
    a_corner, b_corner = pack_corners(core, chip)
    a_corner = lax.ppermute(a_corner, "gx", swaps(0, count_x))
    b_corner = lax.ppermute(b_corner, "gx", swaps(1, count_x))
    wide, v0, v1, v2, _, _, _, side, gram, mid, *coeffs = inner(wide, fields, core, chip)
    pay, edges, bg = edge(
        ids, a, b, a_corner, b_corner, [wide, v0, v1, v2, *coeffs], side, gram
    )
    pay = pay + lax.ppermute(pay, "gy", swaps(0, count_y))
    pay = jnp.sum(spread(pay, "gx", count_x), axis=0)
    chips = count_y // 2
    groups = [[2 * i + c for i in range(chips)] for c in range(2)]
    parts = spread(pay, "gy", chips, groups)
    cells = size_x * size_y * size_z * count_x * count_y
    damping = 80.0 / math.sqrt(cells)
    tangent, sens = final(pairing, parts, bg, mid, edges, damping)
    return tangent.reshape(background.shape), sens


def solution(mesh):
    in_specs = (P(None, "gx", "gy", None), P("gx", "gy", None), P("gx", "gy", None), P(), P())
    out_specs = (P(None, "gx", "gy", None), P("gx", "gy", None))
    return jax.shard_map(
        on_device, mesh=mesh, in_specs=in_specs, out_specs=out_specs, check_vma=False
    )
```

```python
import math

import jax
import jax.numpy as jnp
from jax import lax
from jax.experimental import pallas as pl
from jax.experimental.pallas import tpu as pltpu
from jax.sharding import PartitionSpec as P

SHIFT = 12.0
F = 16
LANES = 128
HALO = 4
HIGHEST = lax.Precision.HIGHEST
V0, V1, V2, E0, E1, V3, E2 = 0, 32, 64, 96, 112, 144, 176
KEPT, ALL_ROWS = 144, 208
WIDE = 10 * LANES
MB = 2**20
FIELD = (24, 256, LANES)
COEFF = (24, 16, LANES)


def tile_at(y):
    return slice(y * F, (y + 1) * F)


def run_copies(pairs, sems, first=0):
    copies = [
        pltpu.make_async_copy(s, d, sems.at[first + i]) for i, (s, d) in enumerate(pairs)
    ]
    for c in copies:
        c.start()
    return copies


def wait_all(copies):
    for c in copies:
        c.wait()


def odd(axis):
    return lax.rem(lax.axis_index(axis), 2) == 1


PARTS = 4


def pack_kernel(
    bg_hbm, cond_hbm, pert_hbm, elec_hbm, pattern_hbm,
    wide_ref, core_ref, chip_ref, a_ref, b_ref, ids_ref, pairing_ref,
    bg, cond_v, pert_v, elec, pattern, pairing, sems,
):
    size_x, size_y = cond_v.shape[0], cond_v.shape[1]
    each = size_x // PARTS
    pairs = [(cond_hbm, cond_v), (pert_hbm, pert_v), (elec_hbm, elec), (pattern_hbm, pattern)]
    for i in range(PARTS):
        planes = pl.ds(i * each, each)
        pairs.append((bg_hbm.at[:, planes], bg.at[:, planes]))
    copies = run_copies(pairs, sems)

    wait_all(copies[:4])
    sub = lax.broadcasted_iota(jnp.int32, (F, LANES), 0)
    ids = jnp.zeros((F, LANES), jnp.int32)
    for e in range(F):
        ids = jnp.where(sub == e, elec[e], ids)
    ids_ref[...] = ids - lane_ids(F)
    sub = lax.broadcasted_iota(jnp.int32, (F, F), 0)
    first = jnp.where(sub == pattern[0:1, :], 1.0, 0.0)
    pairing[:, 0:F] = first - jnp.where(sub == pattern[1:2, :], 1.0, 0.0)
    outs = run_copies([(pairing, pairing_ref)], sems, 4 + PARTS)

    def fill(top_ref, bottom_ref):
        def plane(x, carry):
            for y in range(size_y):
                tile = bg[:, x, y, :]
                wide_ref[x + HALO, tile_at(y + HALO), :] = tile
                if y >= size_y - HALO:
                    top_ref[x, tile_at(y - size_y + HALO), :] = tile
                if y < HALO:
                    bottom_ref[x, tile_at(y), :] = tile
            cond, pert = cond_v[x], pert_v[x]
            wide_ref[x + HALO, 256:264, :] = cond
            wide_ref[x + HALO, 264:272, :] = pert
            top_ref[x, 64:72, :] = jnp.concatenate([cond[4:8], pert[4:8]], axis=0)
            bottom_ref[x, 64:72, :] = jnp.concatenate([cond[0:4], pert[0:4]], axis=0)
            return carry

        for i in range(PARTS):
            copies[4 + i].wait()
            lax.fori_loop(i * each, (i + 1) * each, plane, 0, unroll=each)

    @pl.when(odd("gy"))
    def _():
        fill(chip_ref, core_ref)

    @pl.when(jnp.logical_not(odd("gy")))
    def _():
        fill(core_ref, chip_ref)

    for out, up in ((a_ref, jnp.logical_not(odd("gx"))), (b_ref, odd("gx"))):
        for dx in range(1, HALO + 1):
            x = HALO + jnp.where(up, size_x - dx, dx - 1)
            out[dx - 1, 0:128, :] = wide_ref[x, 64:192, :]
            out[dx - 1, 128:144, :] = wide_ref[x, 256:272, :]
    wait_all(outs)


def pack(background, conductivity, perturbation, electrodes, pattern):
    shape = jax.ShapeDtypeStruct
    inputs = [
        pltpu.with_memory_space_constraint(v, pltpu.HBM)
        for v in (background, conductivity, perturbation, electrodes, pattern.T)
    ]
    return pl.pallas_call(
        pack_kernel,
        out_shape=(
            shape((24, 288, LANES), jnp.float32),
            shape((16, 72, LANES), jnp.float32),
            shape((16, 72, LANES), jnp.float32),
            shape((HALO, 144, LANES), jnp.float32),
            shape((HALO, 144, LANES), jnp.float32),
            shape((F, LANES), jnp.int32),
            pltpu.HBM((F, LANES), jnp.float32),
        ),
        in_specs=[pl.BlockSpec(memory_space=pltpu.HBM)] * 5,
        out_specs=(pl.BlockSpec(memory_space=pltpu.VMEM),) * 6
        + (pl.BlockSpec(memory_space=pltpu.HBM),),
        scratch_shapes=[
            pltpu.VMEM((16, 16, 8, LANES), jnp.float32),
            pltpu.VMEM((16, 8, LANES), jnp.float32),
            pltpu.VMEM((16, 8, LANES), jnp.float32),
            pltpu.SMEM((F,), jnp.int32),
            pltpu.VMEM((2, F), jnp.int32),
            pltpu.VMEM((F, LANES), jnp.float32),
            pltpu.SemaphoreType.DMA((5 + PARTS,)),
        ],
        compiler_params=pltpu.CompilerParams(vmem_limit_bytes=16 * MB),
        name="pack_y",
    )(*inputs)


def corner_layout():
    table, at = [], 0
    for dx in range(1, HALO):
        rows = (HALO - dx) * F
        table.append((dx, rows, at))
        at += 2 * rows + 16
    return table, at


CORNERS, CORNER_ROWS = corner_layout()


def pack_corners_kernel(core_ref, chip_ref, a_ref, b_ref):
    def send(left_ref, right_ref):
        for out, up in ((a_ref, jnp.logical_not(odd("gx"))), (b_ref, odd("gx"))):
            for dx, rows, at in CORNERS:
                x = jnp.where(up, left_ref.shape[0] - dx, dx - 1)
                out[at : at + rows, :] = left_ref[x, 64 - rows : 64, :]
                out[at + rows : at + 2 * rows, :] = right_ref[x, 0:rows, :]
                at += 2 * rows
                out[at : at + 8, :] = left_ref[x, 64:72, :]
                out[at + 8 : at + 16, :] = right_ref[x, 64:72, :]

    @pl.when(odd("gy"))
    def _():
        send(core_ref, chip_ref)

    @pl.when(jnp.logical_not(odd("gy")))
    def _():
        send(chip_ref, core_ref)


def pack_corners(core, chip):
    shape = jax.ShapeDtypeStruct((CORNER_ROWS, LANES), jnp.float32)
    return pl.pallas_call(
        pack_corners_kernel,
        out_shape=(shape, shape),
        compiler_params=pltpu.CompilerParams(vmem_limit_bytes=16 * MB),
        name="pack_corners",
    )(core, chip)


def lane_ids(rows):
    return lax.broadcasted_iota(jnp.int32, (rows, LANES), 1)


def faces(wide, x, ccoef, pcoef):
    lane = lane_ids(16)
    last = lane == LANES - 1
    edge = (lane == 0) | last

    def cells(x):
        own, left, right = wide[x, 256:272, :], wide[x, 272:280, :], wide[x, 280:288, :]
        return (
            jnp.concatenate([left[0:4], own[0:8], right[0:4]], axis=0),
            jnp.concatenate([left[4:8], own[8:16], right[4:8]], axis=0),
        )

    before, now, then = cells(jnp.maximum(x - 1, 0)), cells(x), cells(x + 1)
    for which, coef, half in ((0, ccoef, 0.5), (1, pcoef, -0.5)):
        c, n = now[which], then[which]
        fx, fy, fu, fd, dd = coef
        east = half * (c + n)
        south = half * (c + pltpu.roll(c, 15, 0))
        up = jnp.where(last, 0.0, half * (c + pltpu.roll(c, LANES - 1, 1)))
        down = pltpu.roll(up, 1, 1)
        rest = jnp.where(edge, half * c, 0.0)
        if which == 0:
            west = half * (c + before[0])
            sides = (east + west) + (south + pltpu.roll(south, 1, 0)) + (up + down)
            rest = (0.05 - SHIFT) + rest + sides
        fx[x], fy[x], fu[x], fd[x], dd[x] = east, south, up, down, rest


def source_plane(get, coeffs, x, y0, y1, mask_x, mask_y, emit):
    fx, fy, fu, fd, dd = coeffs
    q = get(x, y0)
    flux = fy[x, y0 - 1 : y0, :] * (q - get(x, y0 - 1))
    for y in range(y0, y1):
        nxt = get(x, y + 1)
        row = slice(y, y + 1)
        later = fy[x, row, :] * (nxt - q)
        out = dd[x, row, :] * q + (flux - later)
        out = out + fx[x - 1, row, :] * (q - get(x - 1, y))
        out = out - fx[x, row, :] * (get(x + 1, y) - q)
        out = out + fd[x, row, :] * (q - pltpu.roll(q, 1, 1))
        out = out - fu[x, row, :] * (pltpu.roll(q, LANES - 1, 1) - q)
        emit(y, masked(out, y, mask_x, mask_y))
        flux, q = later, nxt


def operator_plane(get, coeffs, x, y0, y1, mask_x, mask_y, emit):
    fx, fy, fu, fd, dd = coeffs
    before, q = get(x, y0 - 1), get(x, y0)
    north = fy[x, y0 - 1 : y0, :]
    for y in range(y0, y1):
        nxt = get(x, y + 1)
        row = slice(y, y + 1)
        south = fy[x, row, :]
        out = dd[x, row, :] * q - north * before - south * nxt
        across = fx[x - 1, row, :] * get(x - 1, y) + fx[x, row, :] * get(x + 1, y)
        depth = fd[x, row, :] * pltpu.roll(q, 1, 1) + fu[x, row, :] * pltpu.roll(q, LANES - 1, 1)
        emit(y, masked(out - (across + depth), y, mask_x, mask_y))
        before, q, north = q, nxt, south


def masked(out, y, mask_x, mask_y):
    mask = mask_x
    if y < 4:
        mask = mask_y[0] if mask is None else mask * mask_y[0]
    elif y >= 12:
        mask = mask_y[1] if mask is None else mask * mask_y[1]
    return out if mask is None else out * mask


def tiles(ref):
    return lambda x, y: ref[x, tile_at(y), :]


def put_split(s_ref, i, row, y, value, exact=False):
    lanes = slice((y - 3) * LANES, (y - 2) * LANES)
    hi = value.astype(jnp.bfloat16)
    s_ref[i, row : row + F, lanes] = hi
    if not exact:
        lo = (value - hi.astype(jnp.float32)).astype(jnp.bfloat16)
        s_ref[i, row + F : row + 2 * F, lanes] = lo


def grid_masks():
    one, zero = jnp.float32(1), jnp.float32(0)
    masks = []
    for axis in ("gx", "gy"):
        i = lax.axis_index(axis)
        low, high = i > 0, i < lax.axis_size(axis) - 1
        masks.append((jnp.where(low, one, zero), jnp.where(high, one, zero)))
    return masks


def unit_plane(ids, at_x, e0, i, s_ref, s_at):
    size_x, size_y = 16 * lax.axis_size("gx"), 8 * lax.axis_size("gy")
    good_x = (at_x >= 0) & (at_x < size_x)
    for y in range(2, 14):
        at_y = lax.axis_index("gy") * 8 + y - 4
        good = good_x & (at_y >= 0) & (at_y < size_y)
        here = jnp.where(good, (at_x * size_y + at_y) * LANES, -(2**20))
        value = jnp.where(ids == here, 1.0, 0.0)
        e0[i, tile_at(y), :] = value
        if 3 <= y < 13:
            put_split(s_ref, s_at, E0, y, value, exact=True)


def gram_of(s_ref, i):
    return lax.dot_general(
        s_ref[i, 0:KEPT, LANES : 9 * LANES],
        s_ref[i, :, LANES : 9 * LANES],
        (((1,), (1,)), ((), ())),
        preferred_element_type=jnp.float32,
    )


def prepare_planes(wide, ccoef, pcoef):
    def prepare(x, carry):
        faces(wide, x, ccoef, pcoef)
        return carry

    lax.fori_loop(HALO, HALO + 15, prepare, 0, unroll=15)


def sweep_planes(stencil, src, dst, coeffs, first, ranges, mask_y, s_ref, row, keep, unroll):
    def plane(x, carry):
        def emit(y, out):
            if dst is not None:
                dst[x, tile_at(y), :] = out
            if keep[0] <= y < keep[1]:
                put_split(s_ref, x - HALO, row, y, out)

        for y0, y1 in ranges:
            stencil(tiles(src), coeffs, x, y0, y1, None, mask_y, emit)
        return carry

    lax.fori_loop(HALO + first, HALO + 16 - first, plane, 0, unroll=unroll)


BLOCK, BOTH = (4, 12), (3, 13)


def early_kernel(
    ids_ref, wide, v0, v1, v2, e0, e1, s_ref, cx, cy, cu, cd, cr, px, py, pu, pd, pr
):
    gx = lax.axis_index("gx")
    ids = ids_ref[...]
    ccoef, pcoef = (cx, cy, cu, cd, cr), (px, py, pu, pd, pr)
    prepare_planes(wide, ccoef, pcoef)

    def units(x, carry):
        unit_plane(ids, gx * 16 + x - HALO, e0, x, s_ref, x - HALO)
        return carry

    lax.fori_loop(6, 18, units, 0, unroll=2)

    def sweep(stencil, src, dst, coeffs, first, rows, row):
        count = 16 - 2 * first
        sweep_planes(stencil, src, dst, coeffs, first, [rows], None, s_ref, row, rows, count)

    sweep(source_plane, wide, v0, pcoef, 1, (5, 11), V0)
    sweep(operator_plane, v0, v1, ccoef, 2, (6, 10), V1)
    sweep(operator_plane, v1, v2, ccoef, 3, (7, 9), V2)
    sweep(operator_plane, e0, e1, ccoef, 3, (5, 11), E1)
    sweep(operator_plane, e1, None, ccoef, 4, (6, 10), E2)


def early(ids, wide):
    vmem = pl.BlockSpec(memory_space=pltpu.VMEM)
    field = jax.ShapeDtypeStruct(FIELD, jnp.float32)
    return pl.pallas_call(
        early_kernel,
        out_shape=(field,) * 5 + (jax.ShapeDtypeStruct((16, ALL_ROWS, WIDE), jnp.bfloat16),),
        in_specs=[vmem] * 2,
        out_specs=(vmem,) * 6,
        scratch_shapes=[pltpu.VMEM(COEFF, jnp.float32)] * 10,
        compiler_params=pltpu.CompilerParams(vmem_limit_bytes=10 * MB),
        cost_estimate=pl.CostEstimate(
            flops=10**9, bytes_accessed=8 * 10**6, transcendentals=0
        ),
        name="early",
    )(ids, wide)


def inner_kernel(
    wide_in, v0_in, v1_in, v2_in, e0_in, e1_in, s_in, core_ref, chip_ref,
    wide, v0, v1, v2, e0, e1, s_ref, side_ref, gram_ref, s_hbm,
    cx, cy, cu, cd, cr, px, py, pu, pd, pr, out_sems,
):
    del wide_in, v0_in, v1_in, v2_in, e0_in, e1_in, s_in

    def fill(left_ref, right_ref):
        def plane(x, carry):
            wide[x + HALO, 0:64, :] = left_ref[x, 0:64, :]
            wide[x + HALO, 192:256, :] = right_ref[x, 0:64, :]
            wide[x + HALO, 272:280, :] = left_ref[x, 64:72, :]
            wide[x + HALO, 280:288, :] = right_ref[x, 64:72, :]
            return carry

        lax.fori_loop(0, 16, plane, 0, unroll=4)

    @pl.when(odd("gy"))
    def _():
        fill(core_ref, chip_ref)

    @pl.when(jnp.logical_not(odd("gy")))
    def _():
        fill(chip_ref, core_ref)

    _, mask_y = grid_masks()
    ccoef, pcoef = (cx, cy, cu, cd, cr), (px, py, pu, pd, pr)
    prepare_planes(wide, ccoef, pcoef)
    outs = []

    def hand_on(src, dst):
        outs.extend(run_copies([(src, dst)], out_sems, len(outs)))

    def sweep(stencil, src, dst, coeffs, first, reach, done, row, keep):
        y0, y1 = 4 - reach, 12 + reach
        ranges = [(y0, done[0]), (done[1], y1)] if done else [(y0, y1)]
        half = 8 - first
        sweep_planes(stencil, src, dst, coeffs, first, ranges, mask_y, s_ref, row, keep, half)

    sweep(source_plane, wide, v0, pcoef, 1, 3, (5, 11), V0, BOTH)
    sweep(operator_plane, v0, v1, ccoef, 2, 2, (6, 10), V1, BOTH)
    sweep(operator_plane, v1, v2, ccoef, 3, 1, (7, 9), V2, BOTH)
    hand_on(s_ref.at[pl.ds(1, 3), pl.ds(0, 96)], side_ref.at[pl.ds(0, 3)])
    hand_on(s_ref.at[pl.ds(12, 3), pl.ds(0, 96)], side_ref.at[pl.ds(3, 3)])
    sweep(operator_plane, e0, e1, ccoef, 3, 1, (5, 11), E1, BOTH)
    hand_on(s_ref.at[pl.ds(4, 8), pl.ds(0, KEPT)], s_hbm)
    sweep(operator_plane, v2, None, ccoef, 4, 0, None, V3, BLOCK)
    sweep(operator_plane, e1, None, ccoef, 4, 0, (6, 10), E2, BLOCK)

    gram_ref[...] = gram_of(s_ref, 4)

    def gram_step(x, carry):
        gram_ref[...] += gram_of(s_ref, x)
        return carry

    lax.fori_loop(5, 12, gram_step, 0, unroll=7)
    wait_all(outs)


def inner(wide, fields, core, chip):
    vmem = pl.BlockSpec(memory_space=pltpu.VMEM)
    shape = jax.ShapeDtypeStruct
    field = shape(FIELD, jnp.float32)
    return pl.pallas_call(
        inner_kernel,
        out_shape=(
            shape((24, 288, LANES), jnp.float32),
            field, field, field, field, field,
            shape((16, ALL_ROWS, WIDE), jnp.bfloat16),
            shape((6, 96, WIDE), jnp.bfloat16),
            shape((KEPT, ALL_ROWS), jnp.float32),
            pltpu.HBM((8, KEPT, WIDE), jnp.bfloat16),
        )
        + (shape(COEFF, jnp.float32),) * 10,
        in_specs=[vmem] * 9,
        out_specs=(vmem,) * 9 + (pl.BlockSpec(memory_space=pltpu.HBM),) + (vmem,) * 10,
        scratch_shapes=[pltpu.SemaphoreType.DMA((3,))],
        input_output_aliases={i: i for i in range(7)},
        compiler_params=pltpu.CompilerParams(vmem_limit_bytes=10 * MB),
        cost_estimate=pl.CostEstimate(
            flops=4 * 10**9, bytes_accessed=16 * 10**6, transcendentals=0
        ),
        name="inner",
    )(wide, *fields, core, chip)


def edge_kernel(
    ids_ref, a_ref, b_ref, a_corner, b_corner, side_ref, first_gram, *refs
):
    wide, v0, v1, v2, *coeffs = refs[14:28]
    pay_ref, s_hbm, bg_hbm, e0, e1, s_ref, gram, out_sems = refs[28:]
    gx = lax.axis_index("gx")
    mask_x, mask_y = grid_masks()
    ids = ids_ref[...]

    def halo_plane(high, dx):
        return jnp.where(high, 19 + dx, HALO - dx)

    sides = ((a_ref, a_corner, jnp.logical_not(odd("gx"))), (b_ref, b_corner, odd("gx")))
    for ref, corner, high in sides:
        for dx in range(1, HALO + 1):
            x = halo_plane(high, dx)
            wide[x, 64:192, :] = ref[dx - 1, 0:128, :]
            wide[x, 256:272, :] = ref[dx - 1, 128:144, :]
        for dx, rows, at in CORNERS:
            x = halo_plane(high, dx)
            wide[x, 64 - rows : 64, :] = corner[at : at + rows, :]
            wide[x, 192 : 192 + rows, :] = corner[at + rows : at + 2 * rows, :]
            wide[x, 272:288, :] = corner[at + 2 * rows : at + 2 * rows + 16, :]

    outs = run_copies([(wide.at[pl.ds(3, 18), pl.ds(48, 160)], bg_hbm)], out_sems)

    for i in range(3):
        rows = 96 - 32 * (2 - i)
        s_ref[2 + i, 0:rows, :] = side_ref[i, 0:rows, :]
        s_ref[7 - i, 0:rows, :] = side_ref[5 - i, 0:rows, :]

    ccoef, pcoef = coeffs[:5], coeffs[5:]

    def prepare(i, carry):
        faces(wide, jnp.where(i < 5, i, i + 14), ccoef, pcoef)
        return carry

    lax.fori_loop(0, 9, prepare, 0, unroll=9)

    def mirrored(low, count, body):
        for x in range(low, low + count):
            inside = -1 <= x <= 3
            body(HALO + x, x + 1 if inside else 10, mask_x[0])
            body(19 - x, 8 - x if inside else 10, mask_x[1])

    mirrored(-2, 8, lambda at, s_at, _: unit_plane(ids, gx * 16 + at - HALO, e0, at, s_ref, s_at))

    def sweep(stencil, src, dst, coeffs, row, low, count, near, keep):
        def body(at, s_at, mask):
            def emit(y, out):
                if dst is not None:
                    dst[at, tile_at(y), :] = out
                if keep[0] <= y < keep[1]:
                    put_split(s_ref, s_at, row, y, out)

            mask = mask if low < 0 else None
            stencil(tiles(src), coeffs, at, 4 - near, 12 + near, mask, mask_y, emit)

        mirrored(low, count, body)

    def save(row, rows):
        pair = (s_ref.at[pl.ds(0, 10), pl.ds(row, rows)], s_hbm.at[:, pl.ds(row, rows)])
        outs.extend(run_copies([pair], out_sems, len(outs)))

    none, block, both = (99, 99), (4, 12), (3, 13)
    sweep(operator_plane, e0, e1, ccoef, E1, -1, 1, 0, block)
    sweep(operator_plane, e0, e1, ccoef, E1, 0, 5, 1, both)
    save(E0, 48)
    sweep(source_plane, wide, v0, pcoef, V0, -3, 1, 0, none)
    sweep(source_plane, wide, v0, pcoef, V0, -2, 1, 1, none)
    sweep(source_plane, wide, v0, pcoef, V0, -1, 1, 2, both)
    sweep(source_plane, wide, v0, pcoef, V0, 0, 1, 3, both)
    save(V0, 32)
    sweep(operator_plane, v0, v1, ccoef, V1, -2, 1, 0, none)
    sweep(operator_plane, v0, v1, ccoef, V1, -1, 1, 1, both)
    sweep(operator_plane, v0, v1, ccoef, V1, 0, 2, 2, both)
    save(V1, 32)
    sweep(operator_plane, v1, v2, ccoef, V2, -1, 1, 0, block)
    sweep(operator_plane, v1, v2, ccoef, V2, 0, 3, 1, both)
    save(V2, 32)
    sweep(operator_plane, v2, None, ccoef, V3, 0, 4, 0, block)
    sweep(operator_plane, e1, None, ccoef, E2, 0, 4, 0, block)

    gram[...] = first_gram[...]

    def gram_step(i, carry):
        gram[...] += gram_of(s_ref, i)
        return carry

    lax.fori_loop(1, 9, gram_step, 0, unroll=8)

    def rows_of(row):
        if row == E0:
            return gram[row : row + F, :]
        return gram[row : row + F, :] + gram[row + F : row + 2 * F, :]

    summed = {row: rows_of(row) for row in (V0, V1, V2, E0, E1)}

    def block_of(row, col):
        rows = summed[row]
        if col == E0:
            return rows[:, col : col + F]
        return rows[:, col : col + F] + rows[:, col + F : col + 2 * F]

    order = [
        (V0, V0), (V0, V1), (V1, V1), (V1, V2), (V2, V2), (V2, V3), (V0, E0), (V1, E0),
        (V2, E0), (E0, V3), (E1, V3), (E0, E0), (E0, E1), (E1, E1), (E1, E2),
    ]
    blocks = [block_of(r, c) for r, c in order] + [jnp.zeros((F, F), jnp.float32)]
    pay_ref[0:16, :] = jnp.concatenate(blocks[:8], axis=1)
    pay_ref[16:32, :] = jnp.concatenate(blocks[8:], axis=1)
    wait_all(outs)


def edge(ids, a, b, a_corner, b_corner, kept, side, gram):
    vmem = pl.BlockSpec(memory_space=pltpu.VMEM)
    hbm = pl.BlockSpec(memory_space=pltpu.HBM)
    shape = jax.ShapeDtypeStruct
    count = len(kept)
    outs = pl.pallas_call(
        edge_kernel,
        out_shape=tuple(shape(v.shape, v.dtype) for v in kept)
        + (
            shape((32, LANES), jnp.float32),
            pltpu.HBM((10, KEPT, WIDE), jnp.bfloat16),
            pltpu.HBM((18, 160, LANES), jnp.float32),
        ),
        in_specs=[vmem] * (7 + count),
        out_specs=(vmem,) * (count + 1) + (hbm,) * 2,
        scratch_shapes=[pltpu.VMEM(FIELD, jnp.float32)] * 2
        + [
            pltpu.VMEM((11, ALL_ROWS, WIDE), jnp.bfloat16),
            pltpu.VMEM((KEPT, ALL_ROWS), jnp.float32),
            pltpu.SemaphoreType.DMA((5,)),
        ],
        input_output_aliases={7 + i: i for i in range(count)},
        compiler_params=pltpu.CompilerParams(vmem_limit_bytes=24 * MB),
        name="edge",
    )(ids, a, b, a_corner, b_corner, side, gram, *kept)
    return outs[count:]


def matmul(a, b, dims=((1,), (0,))):
    return lax.dot_general(
        a, b, (dims, ((), ())), precision=HIGHEST, preferred_element_type=jnp.float32
    )


def galerkin(m0, m1, m2, m3):
    a12 = m2 + SHIFT * m1
    work = jnp.concatenate(
        [
            jnp.concatenate([m1 + SHIFT * m0, a12, m0], axis=1),
            jnp.concatenate([a12, m3 + SHIFT * m2, m1], axis=1),
        ],
        axis=0,
    )
    work = jnp.concatenate([work, jnp.zeros((2 * F, LANES - 3 * F), jnp.float32)], axis=1)
    return eliminate(work)[:, 2 * F : 3 * F]


def eliminate(work, size=8):
    count = work.shape[0]
    sub = lax.broadcasted_iota(jnp.int32, work.shape, 0)

    def column(k):
        return jnp.take_along_axis(work, jnp.full(work.shape, k, jnp.int32), axis=1)

    def row(v, k):
        return jnp.broadcast_to(v[k : k + 1, :], (8, LANES))

    def tall(v):
        return jnp.concatenate([v] * (count // 8), axis=0)

    for k in range(0, count, size):
        cols = [column(k + j) for j in range(size)]
        rows = [row(work, k + i) for i in range(size)]
        p = [[row(cols[j], k + i) for j in range(size)] for i in range(size)]
        for s in range(0, size, 2):
            a, b, c, d = p[s][s], p[s][s + 1], p[s + 1][s], p[s + 1][s + 1]
            inverse = 1.0 / (a * d - b * c)
            a, b, c, d = d * inverse, -(b * inverse), -(c * inverse), a * inverse
            rows[s], rows[s + 1] = a * rows[s] + b * rows[s + 1], c * rows[s] + d * rows[s + 1]
            for j in range(s + 2, size):
                u, v = p[s][j], p[s + 1][j]
                p[s][j], p[s + 1][j] = a * u + b * v, c * u + d * v
            for i in range(size):
                if i in (s, s + 1):
                    continue
                u, v = p[i][s], p[i][s + 1]
                rows[i] = rows[i] - u * rows[s] - v * rows[s + 1]
                for j in range(s + 2, size):
                    p[i][j] = p[i][j] - u * p[s][j] - v * p[s + 1][j]
        for j in range(size):
            work = work - cols[j] * tall(rows[j])
        for j in range(size):
            work = jnp.where(sub == k + j, tall(rows[j]), work)
    return work


def final_kernel(
    pairing_hbm, parts_hbm, bg_hbm, mid_hbm, edge_hbm,
    out_ref, sens_ref, pairing_ref, parts_ref, bg, adj, s_ref, mix_ref, sems, *, damping,
):
    pairs = [
        (parts_hbm, parts_ref),
        (pairing_hbm, pairing_ref),
        (edge_hbm.at[pl.ds(0, 5)], s_ref.at[pl.ds(0, 5)]),
        (mid_hbm, s_ref.at[pl.ds(5, 8)]),
        (edge_hbm.at[pl.ds(5, 5)], s_ref.at[pl.ds(13, 5)]),
        (bg_hbm, bg),
    ]
    copies = [pltpu.make_async_copy(s, d, sems.at[i]) for i, (s, d) in enumerate(pairs)]

    @pl.when(lax.axis_index("gx") >= 0)
    def _():
        for c in copies:
            c.start()
        wait_all(copies[:2])

    total = jnp.sum(parts_ref[...], axis=0)

    def part(k):
        r, c = (k // 8) * F, (k % 8) * F
        return total[r : r + F, c : c + F]

    m = [part(k) for k in range(6)]
    p = [part(6), part(7), part(8), part(9).T, part(10).T]
    e = [part(k) for k in range(11, 15)]
    y = galerkin(*m[:4])

    pairing = pairing_ref[:, 0:F]
    w = matmul(8.0 * matmul(pairing, pairing, ((1,), (1,))), jnp.concatenate(p[:2], axis=0), ((1,), (1,)))
    forms = []
    for k in range(4):
        inside = jnp.concatenate(
            [
                jnp.concatenate([m[k], m[k + 1]], axis=1),
                jnp.concatenate([m[k + 1], m[k + 2]], axis=1),
            ],
            axis=0,
        )
        across = matmul(jnp.concatenate([p[k], p[k + 1]], axis=0), w)
        local = matmul(w, matmul(e[k], w), ((0,), (0,)))
        forms.append(damping * (damping * inside + across + across.T) + local)
    hy = matmul(jnp.concatenate(forms, axis=0), y)
    moments = [matmul(y, hy[32 * k : 32 * (k + 1)], ((0,), (0,))) for k in range(4)]
    z = jnp.concatenate([damping * y, matmul(w, y)], axis=0)
    q = galerkin(*moments)
    z0, z1 = matmul(z, q[0:F]), matmul(z, q[F:])
    none = jnp.zeros((F, F), jnp.float32)
    mix = [
        jnp.concatenate([y[0:F], z0[0:F]], axis=1),
        jnp.concatenate([y[F:], z0[F : 2 * F] + z1[0:F]], axis=1),
        jnp.concatenate([none, z1[F : 2 * F]], axis=1),
        jnp.concatenate([none, z0[2 * F :]], axis=1),
        jnp.concatenate([none, z1[2 * F :]], axis=1),
    ]
    mix = [mix[i] for i in (0, 0, 1, 1, 2, 2, 3, 4, 4)]
    mix = jnp.concatenate(mix, axis=0).T
    hi = mix.astype(jnp.bfloat16)
    mix_ref[0:32, :] = hi
    mix_ref[32:64, :] = (mix - hi.astype(jnp.float32)).astype(jnp.bfloat16)
    wait_all(copies[2:])
    both = mix_ref[...]

    def combine(x, lanes):
        out = jnp.dot(both, s_ref[x, :, lanes], preferred_element_type=jnp.float32)
        return out[0:32] + out[32:64]

    def store(x, out):
        for k in range(10):
            cols = slice(k * LANES, (k + 1) * LANES)
            if 0 < k < 9:
                out_ref[pl.ds(x * 8 + k - 9, F, stride=128), :] = out[0:F, cols]
            adj[x, tile_at(k), :] = out[F:, cols]

    def store_end(x, out):
        for k in range(8):
            adj[x, tile_at(k + 1), :] = out[F:, k * LANES : (k + 1) * LANES]

    lane = lane_ids(F)

    def sens_plane(x):
        b, a = bg[x, tile_at(1), :], adj[x, tile_at(1), :]
        before = (b - bg[x, tile_at(0), :]) * (a - adj[x, tile_at(0), :])
        for k in range(1, 9):
            bn, an = bg[x, tile_at(k + 1), :], adj[x, tile_at(k + 1), :]
            after = (bn - b) * (an - a)
            total = before + after
            for s in (x - 1, x + 1):
                total = total + (bg[s, tile_at(k), :] - b) * (adj[s, tile_at(k), :] - a)
            bu = jnp.where(lane == LANES - 1, 0.0, pltpu.roll(b, LANES - 1, 1))
            au = jnp.where(lane == LANES - 1, 0.0, pltpu.roll(a, LANES - 1, 1))
            bd = jnp.where(lane == 0, 0.0, pltpu.roll(b, 1, 1))
            ad = jnp.where(lane == 0, 0.0, pltpu.roll(a, 1, 1))
            total = total + (bu - b) * (au - a) + (bd - b) * (ad - a)
            sens_ref[x - 1, k - 1 : k, :] = -0.5 * jnp.sum(total, axis=0, keepdims=True)
            before, b, a = after, bn, an

    ends = slice(LANES, 9 * LANES)
    store_end(0, combine(0, ends))
    store(1, combine(1, slice(0, WIDE)))
    store(2, combine(2, slice(0, WIDE)))

    def plane(x, carry):
        out = combine(x + 2, slice(0, WIDE))
        sens_plane(x)
        store(x + 2, out)
        return carry

    lax.fori_loop(1, 15, plane, 0, unroll=7)
    out = combine(17, ends)
    sens_plane(15)
    store_end(17, out)
    sens_plane(16)


def final(pairing, parts, bg, mid, edges, damping):
    vmem = pl.BlockSpec(memory_space=pltpu.VMEM)
    hbm = pl.BlockSpec(memory_space=pltpu.HBM)

    def kernel(*refs):
        final_kernel(*refs, damping=damping)

    return pl.pallas_call(
        kernel,
        out_shape=(
            jax.ShapeDtypeStruct((2048, LANES), jnp.float32),
            jax.ShapeDtypeStruct((16, 8, LANES), jnp.float32),
        ),
        in_specs=[hbm] * 5,
        scratch_shapes=[
            pltpu.VMEM((F, LANES), jnp.float32),
            pltpu.VMEM((F, 32, LANES), jnp.float32),
            pltpu.VMEM((18, 160, LANES), jnp.float32),
            pltpu.VMEM((18, 160, LANES), jnp.float32),
            pltpu.VMEM((18, KEPT, WIDE), jnp.bfloat16),
            pltpu.VMEM((64, KEPT), jnp.bfloat16),
            pltpu.SemaphoreType.DMA((6,)),
        ],
        compiler_params=pltpu.CompilerParams(vmem_limit_bytes=56 * MB),
        name="final",
    )(pairing, pltpu.with_memory_space_constraint(parts, pltpu.HBM), bg, mid, edges)


def spread(block, axis, count, groups=None):
    copies = jnp.broadcast_to(block[None], (count,) + block.shape)
    return lax.all_to_all(copies, axis, 0, 0, axis_index_groups=groups)


def swaps(first, count):
    lows = range(first, count - 1, 2)
    return [(i, i + 1) for i in lows] + [(i + 1, i) for i in lows]


def on_device(background, conductivity, perturbation, electrodes, pattern):
    size_x, size_y, size_z = conductivity.shape
    count_x, count_y = lax.axis_size("gx"), lax.axis_size("gy")
    wide, core, chip, a, b, ids, pairing = pack(
        background, conductivity, perturbation, electrodes, pattern
    )
    a = lax.ppermute(a, "gx", swaps(0, count_x))
    b = lax.ppermute(b, "gx", swaps(1, count_x))
    chip = lax.ppermute(chip, "gy", swaps(1, count_y))
    core = lax.ppermute(core, "gy", swaps(0, count_y))
    fields = early(ids, wide)
    a_corner, b_corner = pack_corners(core, chip)
    a_corner = lax.ppermute(a_corner, "gx", swaps(0, count_x))
    b_corner = lax.ppermute(b_corner, "gx", swaps(1, count_x))
    wide, v0, v1, v2, _, _, _, side, gram, mid, *coeffs = inner(wide, fields, core, chip)
    pay, edges, bg = edge(
        ids, a, b, a_corner, b_corner, [wide, v0, v1, v2, *coeffs], side, gram
    )
    pay = pay + lax.ppermute(pay, "gy", swaps(0, count_y))
    pay = jnp.sum(spread(pay, "gx", count_x), axis=0)
    chips = count_y // 2
    groups = [[2 * i + c for i in range(chips)] for c in range(2)]
    parts = spread(pay, "gy", chips, groups)
    cells = size_x * size_y * size_z * count_x * count_y
    damping = 80.0 / math.sqrt(cells)
    tangent, sens = final(pairing, parts, bg, mid, edges, damping)
    return tangent.reshape(background.shape), sens


def solution(mesh):
    in_specs = (P(None, "gx", "gy", None), P("gx", "gy", None), P("gx", "gy", None), P(), P())
    out_specs = (P(None, "gx", "gy", None), P("gx", "gy", None))
    return jax.shard_map(
        on_device, mesh=mesh, in_specs=in_specs, out_specs=out_specs, check_vma=False
    )
```

```python
import math

import jax
import jax.numpy as jnp
from jax import lax
from jax.experimental import pallas as pl
from jax.experimental.pallas import tpu as pltpu
from jax.sharding import PartitionSpec as P

SHIFT = 12.0
F = 16
LANES = 128
HALO = 4
HIGHEST = lax.Precision.HIGHEST
V0, V1, V2, E0, E1, V3, E2 = 0, 32, 64, 96, 112, 144, 176
KEPT, ALL_ROWS = 144, 208
WIDE = 10 * LANES
MB = 2**20
FIELD = (24, 256, LANES)
COEFF = (24, 16, LANES)


def tile_at(y):
    return slice(y * F, (y + 1) * F)


def run_copies(pairs, sems, first=0):
    copies = [
        pltpu.make_async_copy(s, d, sems.at[first + i]) for i, (s, d) in enumerate(pairs)
    ]
    for c in copies:
        c.start()
    return copies


def wait_all(copies):
    for c in copies:
        c.wait()


def odd(axis):
    return lax.rem(lax.axis_index(axis), 2) == 1


PARTS = 4


def pack_kernel(
    bg_hbm, cond_hbm, pert_hbm, elec_hbm, pattern_hbm,
    wide_ref, core_ref, chip_ref, a_ref, b_ref, ids_ref, pairing_ref,
    bg, cond_v, pert_v, elec, pattern, pairing, sems,
):
    size_x, size_y = cond_v.shape[0], cond_v.shape[1]
    each = size_x // PARTS
    pairs = [(cond_hbm, cond_v), (pert_hbm, pert_v), (elec_hbm, elec), (pattern_hbm, pattern)]
    for i in range(PARTS):
        planes = pl.ds(i * each, each)
        pairs.append((bg_hbm.at[:, planes], bg.at[:, planes]))
    copies = run_copies(pairs, sems)

    wait_all(copies[:4])
    sub = lax.broadcasted_iota(jnp.int32, (F, LANES), 0)
    ids = jnp.zeros((F, LANES), jnp.int32)
    for e in range(F):
        ids = jnp.where(sub == e, elec[e], ids)
    ids_ref[...] = ids - lane_ids(F)
    sub = lax.broadcasted_iota(jnp.int32, (F, F), 0)
    first = jnp.where(sub == pattern[0:1, :], 1.0, 0.0)
    pairing[:, 0:F] = first - jnp.where(sub == pattern[1:2, :], 1.0, 0.0)
    outs = run_copies([(pairing, pairing_ref)], sems, 4 + PARTS)

    def fill(top_ref, bottom_ref):
        def plane(x, carry):
            for y in range(size_y):
                tile = bg[:, x, y, :]
                wide_ref[x + HALO, tile_at(y + HALO), :] = tile
                if y >= size_y - HALO:
                    top_ref[x, tile_at(y - size_y + HALO), :] = tile
                if y < HALO:
                    bottom_ref[x, tile_at(y), :] = tile
            cond, pert = cond_v[x], pert_v[x]
            wide_ref[x + HALO, 256:264, :] = cond
            wide_ref[x + HALO, 264:272, :] = pert
            top_ref[x, 64:72, :] = jnp.concatenate([cond[4:8], pert[4:8]], axis=0)
            bottom_ref[x, 64:72, :] = jnp.concatenate([cond[0:4], pert[0:4]], axis=0)
            return carry

        for i in range(PARTS):
            copies[4 + i].wait()
            lax.fori_loop(i * each, (i + 1) * each, plane, 0, unroll=each)

    @pl.when(odd("gy"))
    def _():
        fill(chip_ref, core_ref)

    @pl.when(jnp.logical_not(odd("gy")))
    def _():
        fill(core_ref, chip_ref)

    for out, up in ((a_ref, jnp.logical_not(odd("gx"))), (b_ref, odd("gx"))):
        for dx in range(1, HALO + 1):
            x = HALO + jnp.where(up, size_x - dx, dx - 1)
            out[dx - 1, 0:128, :] = wide_ref[x, 64:192, :]
            out[dx - 1, 128:144, :] = wide_ref[x, 256:272, :]
    wait_all(outs)


def pack(background, conductivity, perturbation, electrodes, pattern):
    shape = jax.ShapeDtypeStruct
    inputs = [
        pltpu.with_memory_space_constraint(v, pltpu.HBM)
        for v in (background, conductivity, perturbation, electrodes, pattern.T)
    ]
    return pl.pallas_call(
        pack_kernel,
        out_shape=(
            shape((24, 288, LANES), jnp.float32),
            shape((16, 72, LANES), jnp.float32),
            shape((16, 72, LANES), jnp.float32),
            shape((HALO, 144, LANES), jnp.float32),
            shape((HALO, 144, LANES), jnp.float32),
            shape((F, LANES), jnp.int32),
            pltpu.HBM((F, LANES), jnp.float32),
        ),
        in_specs=[pl.BlockSpec(memory_space=pltpu.HBM)] * 5,
        out_specs=(pl.BlockSpec(memory_space=pltpu.VMEM),) * 6
        + (pl.BlockSpec(memory_space=pltpu.HBM),),
        scratch_shapes=[
            pltpu.VMEM((16, 16, 8, LANES), jnp.float32),
            pltpu.VMEM((16, 8, LANES), jnp.float32),
            pltpu.VMEM((16, 8, LANES), jnp.float32),
            pltpu.SMEM((F,), jnp.int32),
            pltpu.VMEM((2, F), jnp.int32),
            pltpu.VMEM((F, LANES), jnp.float32),
            pltpu.SemaphoreType.DMA((5 + PARTS,)),
        ],
        compiler_params=pltpu.CompilerParams(vmem_limit_bytes=16 * MB),
        name="pack_y",
    )(*inputs)


def corner_layout():
    table, at = [], 0
    for dx in range(1, HALO):
        rows = (HALO - dx) * F
        table.append((dx, rows, at))
        at += 2 * rows + 16
    return table, at


CORNERS, CORNER_ROWS = corner_layout()


def pack_corners_kernel(core_ref, chip_ref, a_ref, b_ref):
    def send(left_ref, right_ref):
        for out, up in ((a_ref, jnp.logical_not(odd("gx"))), (b_ref, odd("gx"))):
            for dx, rows, at in CORNERS:
                x = jnp.where(up, left_ref.shape[0] - dx, dx - 1)
                out[at : at + rows, :] = left_ref[x, 64 - rows : 64, :]
                out[at + rows : at + 2 * rows, :] = right_ref[x, 0:rows, :]
                at += 2 * rows
                out[at : at + 8, :] = left_ref[x, 64:72, :]
                out[at + 8 : at + 16, :] = right_ref[x, 64:72, :]

    @pl.when(odd("gy"))
    def _():
        send(core_ref, chip_ref)

    @pl.when(jnp.logical_not(odd("gy")))
    def _():
        send(chip_ref, core_ref)


def pack_corners(core, chip):
    shape = jax.ShapeDtypeStruct((CORNER_ROWS, LANES), jnp.float32)
    return pl.pallas_call(
        pack_corners_kernel,
        out_shape=(shape, shape),
        compiler_params=pltpu.CompilerParams(vmem_limit_bytes=16 * MB),
        name="pack_corners",
    )(core, chip)


def lane_ids(rows):
    return lax.broadcasted_iota(jnp.int32, (rows, LANES), 1)


def faces(wide, x, ccoef, pcoef):
    lane = lane_ids(16)
    last = lane == LANES - 1
    edge = (lane == 0) | last

    def cells(x):
        own, left, right = wide[x, 256:272, :], wide[x, 272:280, :], wide[x, 280:288, :]
        return (
            jnp.concatenate([left[0:4], own[0:8], right[0:4]], axis=0),
            jnp.concatenate([left[4:8], own[8:16], right[4:8]], axis=0),
        )

    before, now, then = cells(jnp.maximum(x - 1, 0)), cells(x), cells(x + 1)
    for which, coef, half in ((0, ccoef, 0.5), (1, pcoef, -0.5)):
        c, n = now[which], then[which]
        fx, fy, fu, fd, dd = coef
        east = half * (c + n)
        south = half * (c + pltpu.roll(c, 15, 0))
        up = jnp.where(last, 0.0, half * (c + pltpu.roll(c, LANES - 1, 1)))
        down = pltpu.roll(up, 1, 1)
        rest = jnp.where(edge, half * c, 0.0)
        if which == 0:
            west = half * (c + before[0])
            sides = (east + west) + (south + pltpu.roll(south, 1, 0)) + (up + down)
            rest = (0.05 - SHIFT) + rest + sides
        fx[x], fy[x], fu[x], fd[x], dd[x] = east, south, up, down, rest


def source_plane(get, coeffs, x, y0, y1, mask_x, mask_y, emit):
    fx, fy, fu, fd, dd = coeffs
    q = get(x, y0)
    flux = fy[x, y0 - 1 : y0, :] * (q - get(x, y0 - 1))
    for y in range(y0, y1):
        nxt = get(x, y + 1)
        row = slice(y, y + 1)
        later = fy[x, row, :] * (nxt - q)
        out = dd[x, row, :] * q + (flux - later)
        out = out + fx[x - 1, row, :] * (q - get(x - 1, y))
        out = out - fx[x, row, :] * (get(x + 1, y) - q)
        out = out + fd[x, row, :] * (q - pltpu.roll(q, 1, 1))
        out = out - fu[x, row, :] * (pltpu.roll(q, LANES - 1, 1) - q)
        emit(y, masked(out, y, mask_x, mask_y))
        flux, q = later, nxt


def operator_plane(get, coeffs, x, y0, y1, mask_x, mask_y, emit):
    fx, fy, fu, fd, dd = coeffs
    before, q = get(x, y0 - 1), get(x, y0)
    north = fy[x, y0 - 1 : y0, :]
    for y in range(y0, y1):
        nxt = get(x, y + 1)
        row = slice(y, y + 1)
        south = fy[x, row, :]
        out = dd[x, row, :] * q - north * before - south * nxt
        across = fx[x - 1, row, :] * get(x - 1, y) + fx[x, row, :] * get(x + 1, y)
        depth = fd[x, row, :] * pltpu.roll(q, 1, 1) + fu[x, row, :] * pltpu.roll(q, LANES - 1, 1)
        emit(y, masked(out - (across + depth), y, mask_x, mask_y))
        before, q, north = q, nxt, south


def masked(out, y, mask_x, mask_y):
    mask = mask_x
    if y < 4:
        mask = mask_y[0] if mask is None else mask * mask_y[0]
    elif y >= 12:
        mask = mask_y[1] if mask is None else mask * mask_y[1]
    return out if mask is None else out * mask


def tiles(ref):
    return lambda x, y: ref[x, tile_at(y), :]


def put_split(s_ref, i, row, y, value, exact=False):
    lanes = slice((y - 3) * LANES, (y - 2) * LANES)
    hi = value.astype(jnp.bfloat16)
    s_ref[i, row : row + F, lanes] = hi
    if not exact:
        lo = (value - hi.astype(jnp.float32)).astype(jnp.bfloat16)
        s_ref[i, row + F : row + 2 * F, lanes] = lo


def grid_masks():
    one, zero = jnp.float32(1), jnp.float32(0)
    masks = []
    for axis in ("gx", "gy"):
        i = lax.axis_index(axis)
        low, high = i > 0, i < lax.axis_size(axis) - 1
        masks.append((jnp.where(low, one, zero), jnp.where(high, one, zero)))
    return masks


def unit_plane(ids, at_x, e0, i, s_ref, s_at):
    size_x, size_y = 16 * lax.axis_size("gx"), 8 * lax.axis_size("gy")
    good_x = (at_x >= 0) & (at_x < size_x)
    for y in range(2, 14):
        at_y = lax.axis_index("gy") * 8 + y - 4
        good = good_x & (at_y >= 0) & (at_y < size_y)
        here = jnp.where(good, (at_x * size_y + at_y) * LANES, -(2**20))
        value = jnp.where(ids == here, 1.0, 0.0)
        e0[i, tile_at(y), :] = value
        if 3 <= y < 13:
            put_split(s_ref, s_at, E0, y, value, exact=True)


def gram_of(s_ref, i):
    return lax.dot_general(
        s_ref[i, 0:KEPT, LANES : 9 * LANES],
        s_ref[i, :, LANES : 9 * LANES],
        (((1,), (1,)), ((), ())),
        preferred_element_type=jnp.float32,
    )


def prepare_planes(wide, ccoef, pcoef):
    def prepare(x, carry):
        faces(wide, x, ccoef, pcoef)
        return carry

    lax.fori_loop(HALO, HALO + 15, prepare, 0, unroll=15)


def sweep_planes(stencil, src, dst, coeffs, first, ranges, mask_y, s_ref, row, keep, unroll):
    def plane(x, carry):
        def emit(y, out):
            if dst is not None:
                dst[x, tile_at(y), :] = out
            if keep[0] <= y < keep[1]:
                put_split(s_ref, x - HALO, row, y, out)

        for y0, y1 in ranges:
            stencil(tiles(src), coeffs, x, y0, y1, None, mask_y, emit)
        return carry

    lax.fori_loop(HALO + first, HALO + 16 - first, plane, 0, unroll=unroll)


BLOCK, BOTH = (4, 12), (3, 13)


def early_kernel(
    ids_ref, wide, v0, v1, v2, e0, e1, s_ref, cx, cy, cu, cd, cr, px, py, pu, pd, pr
):
    gx = lax.axis_index("gx")
    ids = ids_ref[...]
    ccoef, pcoef = (cx, cy, cu, cd, cr), (px, py, pu, pd, pr)
    prepare_planes(wide, ccoef, pcoef)

    def units(x, carry):
        unit_plane(ids, gx * 16 + x - HALO, e0, x, s_ref, x - HALO)
        return carry

    lax.fori_loop(6, 18, units, 0, unroll=2)

    def sweep(stencil, src, dst, coeffs, first, rows, row):
        count = 16 - 2 * first
        sweep_planes(stencil, src, dst, coeffs, first, [rows], None, s_ref, row, rows, count)

    sweep(source_plane, wide, v0, pcoef, 1, (5, 11), V0)
    sweep(operator_plane, v0, v1, ccoef, 2, (6, 10), V1)
    sweep(operator_plane, v1, v2, ccoef, 3, (7, 9), V2)
    sweep(operator_plane, e0, e1, ccoef, 3, (5, 11), E1)
    sweep(operator_plane, e1, None, ccoef, 4, (6, 10), E2)


def early(ids, wide):
    vmem = pl.BlockSpec(memory_space=pltpu.VMEM)
    field = jax.ShapeDtypeStruct(FIELD, jnp.float32)
    return pl.pallas_call(
        early_kernel,
        out_shape=(field,) * 5 + (jax.ShapeDtypeStruct((16, ALL_ROWS, WIDE), jnp.bfloat16),),
        in_specs=[vmem] * 2,
        out_specs=(vmem,) * 6,
        scratch_shapes=[pltpu.VMEM(COEFF, jnp.float32)] * 10,
        compiler_params=pltpu.CompilerParams(vmem_limit_bytes=10 * MB),
        cost_estimate=pl.CostEstimate(
            flops=10**9, bytes_accessed=8 * 10**6, transcendentals=0
        ),
        name="early",
    )(ids, wide)


def inner_kernel(
    wide_in, v0_in, v1_in, v2_in, e0_in, e1_in, s_in, core_ref, chip_ref,
    wide, v0, v1, v2, e0, e1, s_ref, side_ref, gram_ref, s_hbm,
    cx, cy, cu, cd, cr, px, py, pu, pd, pr, out_sems,
):
    del wide_in, v0_in, v1_in, v2_in, e0_in, e1_in, s_in

    def fill(left_ref, right_ref):
        def plane(x, carry):
            wide[x + HALO, 0:64, :] = left_ref[x, 0:64, :]
            wide[x + HALO, 192:256, :] = right_ref[x, 0:64, :]
            wide[x + HALO, 272:280, :] = left_ref[x, 64:72, :]
            wide[x + HALO, 280:288, :] = right_ref[x, 64:72, :]
            return carry

        lax.fori_loop(0, 16, plane, 0, unroll=4)

    @pl.when(odd("gy"))
    def _():
        fill(core_ref, chip_ref)

    @pl.when(jnp.logical_not(odd("gy")))
    def _():
        fill(chip_ref, core_ref)

    _, mask_y = grid_masks()
    ccoef, pcoef = (cx, cy, cu, cd, cr), (px, py, pu, pd, pr)
    prepare_planes(wide, ccoef, pcoef)
    outs = []

    def hand_on(src, dst):
        outs.extend(run_copies([(src, dst)], out_sems, len(outs)))

    def sweep(stencil, src, dst, coeffs, first, reach, done, row, keep):
        y0, y1 = 4 - reach, 12 + reach
        ranges = [(y0, done[0]), (done[1], y1)] if done else [(y0, y1)]
        half = 8 - first
        sweep_planes(stencil, src, dst, coeffs, first, ranges, mask_y, s_ref, row, keep, half)

    sweep(source_plane, wide, v0, pcoef, 1, 3, (5, 11), V0, BOTH)
    sweep(operator_plane, v0, v1, ccoef, 2, 2, (6, 10), V1, BOTH)
    sweep(operator_plane, v1, v2, ccoef, 3, 1, (7, 9), V2, BOTH)
    hand_on(s_ref.at[pl.ds(1, 3), pl.ds(0, 96)], side_ref.at[pl.ds(0, 3)])
    hand_on(s_ref.at[pl.ds(12, 3), pl.ds(0, 96)], side_ref.at[pl.ds(3, 3)])
    sweep(operator_plane, e0, e1, ccoef, 3, 1, (5, 11), E1, BOTH)
    hand_on(s_ref.at[pl.ds(4, 8), pl.ds(0, KEPT)], s_hbm)
    sweep(operator_plane, v2, None, ccoef, 4, 0, None, V3, BLOCK)
    sweep(operator_plane, e1, None, ccoef, 4, 0, (6, 10), E2, BLOCK)

    gram_ref[...] = gram_of(s_ref, 4)

    def gram_step(x, carry):
        gram_ref[...] += gram_of(s_ref, x)
        return carry

    lax.fori_loop(5, 12, gram_step, 0, unroll=7)
    wait_all(outs)


def inner(wide, fields, core, chip):
    vmem = pl.BlockSpec(memory_space=pltpu.VMEM)
    shape = jax.ShapeDtypeStruct
    field = shape(FIELD, jnp.float32)
    return pl.pallas_call(
        inner_kernel,
        out_shape=(
            shape((24, 288, LANES), jnp.float32),
            field, field, field, field, field,
            shape((16, ALL_ROWS, WIDE), jnp.bfloat16),
            shape((6, 96, WIDE), jnp.bfloat16),
            shape((KEPT, ALL_ROWS), jnp.float32),
            pltpu.HBM((8, KEPT, WIDE), jnp.bfloat16),
        )
        + (shape(COEFF, jnp.float32),) * 10,
        in_specs=[vmem] * 9,
        out_specs=(vmem,) * 9 + (pl.BlockSpec(memory_space=pltpu.HBM),) + (vmem,) * 10,
        scratch_shapes=[pltpu.SemaphoreType.DMA((3,))],
        input_output_aliases={i: i for i in range(7)},
        compiler_params=pltpu.CompilerParams(vmem_limit_bytes=10 * MB),
        cost_estimate=pl.CostEstimate(
            flops=4 * 10**9, bytes_accessed=16 * 10**6, transcendentals=0
        ),
        name="inner",
    )(wide, *fields, core, chip)


def edge_kernel(
    ids_ref, a_ref, b_ref, a_corner, b_corner, side_ref, first_gram, *refs
):
    wide, v0, v1, v2, *coeffs = refs[14:28]
    pay_ref, s_hbm, bg_hbm, e0, e1, s_ref, gram, out_sems = refs[28:]
    gx = lax.axis_index("gx")
    mask_x, mask_y = grid_masks()
    ids = ids_ref[...]

    def halo_plane(high, dx):
        return jnp.where(high, 19 + dx, HALO - dx)

    sides = ((a_ref, a_corner, jnp.logical_not(odd("gx"))), (b_ref, b_corner, odd("gx")))
    for ref, corner, high in sides:
        for dx in range(1, HALO + 1):
            x = halo_plane(high, dx)
            wide[x, 64:192, :] = ref[dx - 1, 0:128, :]
            wide[x, 256:272, :] = ref[dx - 1, 128:144, :]
        for dx, rows, at in CORNERS:
            x = halo_plane(high, dx)
            wide[x, 64 - rows : 64, :] = corner[at : at + rows, :]
            wide[x, 192 : 192 + rows, :] = corner[at + rows : at + 2 * rows, :]
            wide[x, 272:288, :] = corner[at + 2 * rows : at + 2 * rows + 16, :]

    outs = run_copies([(wide.at[pl.ds(3, 18), pl.ds(48, 160)], bg_hbm)], out_sems)

    for i in range(3):
        rows = 96 - 32 * (2 - i)
        s_ref[2 + i, 0:rows, :] = side_ref[i, 0:rows, :]
        s_ref[7 - i, 0:rows, :] = side_ref[5 - i, 0:rows, :]

    ccoef, pcoef = coeffs[:5], coeffs[5:]

    def prepare(i, carry):
        faces(wide, jnp.where(i < 5, i, i + 14), ccoef, pcoef)
        return carry

    lax.fori_loop(0, 9, prepare, 0, unroll=9)

    def mirrored(low, count, body):
        for x in range(low, low + count):
            inside = -1 <= x <= 3
            body(HALO + x, x + 1 if inside else 10, mask_x[0])
            body(19 - x, 8 - x if inside else 10, mask_x[1])

    mirrored(-2, 8, lambda at, s_at, _: unit_plane(ids, gx * 16 + at - HALO, e0, at, s_ref, s_at))

    def sweep(stencil, src, dst, coeffs, row, low, count, near, keep):
        def body(at, s_at, mask):
            def emit(y, out):
                if dst is not None:
                    dst[at, tile_at(y), :] = out
                if keep[0] <= y < keep[1]:
                    put_split(s_ref, s_at, row, y, out)

            mask = mask if low < 0 else None
            stencil(tiles(src), coeffs, at, 4 - near, 12 + near, mask, mask_y, emit)

        mirrored(low, count, body)

    def save(row, rows):
        pair = (s_ref.at[pl.ds(0, 10), pl.ds(row, rows)], s_hbm.at[:, pl.ds(row, rows)])
        outs.extend(run_copies([pair], out_sems, len(outs)))

    none, block, both = (99, 99), (4, 12), (3, 13)
    sweep(operator_plane, e0, e1, ccoef, E1, -1, 1, 0, block)
    sweep(operator_plane, e0, e1, ccoef, E1, 0, 5, 1, both)
    save(E0, 48)
    sweep(source_plane, wide, v0, pcoef, V0, -3, 1, 0, none)
    sweep(source_plane, wide, v0, pcoef, V0, -2, 1, 1, none)
    sweep(source_plane, wide, v0, pcoef, V0, -1, 1, 2, both)
    sweep(source_plane, wide, v0, pcoef, V0, 0, 1, 3, both)
    save(V0, 32)
    sweep(operator_plane, v0, v1, ccoef, V1, -2, 1, 0, none)
    sweep(operator_plane, v0, v1, ccoef, V1, -1, 1, 1, both)
    sweep(operator_plane, v0, v1, ccoef, V1, 0, 2, 2, both)
    save(V1, 32)
    sweep(operator_plane, v1, v2, ccoef, V2, -1, 1, 0, block)
    sweep(operator_plane, v1, v2, ccoef, V2, 0, 3, 1, both)
    save(V2, 32)
    sweep(operator_plane, v2, None, ccoef, V3, 0, 4, 0, block)
    sweep(operator_plane, e1, None, ccoef, E2, 0, 4, 0, block)

    gram[...] = first_gram[...]

    def gram_step(i, carry):
        gram[...] += gram_of(s_ref, i)
        return carry

    lax.fori_loop(1, 9, gram_step, 0, unroll=8)

    def rows_of(row):
        if row == E0:
            return gram[row : row + F, :]
        return gram[row : row + F, :] + gram[row + F : row + 2 * F, :]

    summed = {row: rows_of(row) for row in (V0, V1, V2, E0, E1)}

    def block_of(row, col):
        rows = summed[row]
        if col == E0:
            return rows[:, col : col + F]
        return rows[:, col : col + F] + rows[:, col + F : col + 2 * F]

    order = [
        (V0, V0), (V0, V1), (V1, V1), (V1, V2), (V2, V2), (V2, V3), (V0, E0), (V1, E0),
        (V2, E0), (E0, V3), (E1, V3), (E0, E0), (E0, E1), (E1, E1), (E1, E2),
    ]
    blocks = [block_of(r, c) for r, c in order] + [jnp.zeros((F, F), jnp.float32)]
    pay_ref[0:16, :] = jnp.concatenate(blocks[:8], axis=1)
    pay_ref[16:32, :] = jnp.concatenate(blocks[8:], axis=1)
    wait_all(outs)


def edge(ids, a, b, a_corner, b_corner, kept, side, gram):
    vmem = pl.BlockSpec(memory_space=pltpu.VMEM)
    hbm = pl.BlockSpec(memory_space=pltpu.HBM)
    shape = jax.ShapeDtypeStruct
    count = len(kept)
    outs = pl.pallas_call(
        edge_kernel,
        out_shape=tuple(shape(v.shape, v.dtype) for v in kept)
        + (
            shape((32, LANES), jnp.float32),
            pltpu.HBM((10, KEPT, WIDE), jnp.bfloat16),
            pltpu.HBM((18, 160, LANES), jnp.float32),
        ),
        in_specs=[vmem] * (7 + count),
        out_specs=(vmem,) * (count + 1) + (hbm,) * 2,
        scratch_shapes=[pltpu.VMEM(FIELD, jnp.float32)] * 2
        + [
            pltpu.VMEM((11, ALL_ROWS, WIDE), jnp.bfloat16),
            pltpu.VMEM((KEPT, ALL_ROWS), jnp.float32),
            pltpu.SemaphoreType.DMA((5,)),
        ],
        input_output_aliases={7 + i: i for i in range(count)},
        compiler_params=pltpu.CompilerParams(vmem_limit_bytes=24 * MB),
        name="edge",
    )(ids, a, b, a_corner, b_corner, side, gram, *kept)
    return outs[count:]


def matmul(a, b, dims=((1,), (0,))):
    return lax.dot_general(
        a, b, (dims, ((), ())), precision=HIGHEST, preferred_element_type=jnp.float32
    )


def galerkin(m0, m1, m2, m3):
    a12 = m2 + SHIFT * m1
    work = jnp.concatenate(
        [
            jnp.concatenate([m1 + SHIFT * m0, a12, m0], axis=1),
            jnp.concatenate([a12, m3 + SHIFT * m2, m1], axis=1),
        ],
        axis=0,
    )
    work = jnp.concatenate([work, jnp.zeros((2 * F, LANES - 3 * F), jnp.float32)], axis=1)
    return eliminate(work)[:, 2 * F : 3 * F]


def eliminate(work, size=8):
    count = work.shape[0]
    sub = lax.broadcasted_iota(jnp.int32, work.shape, 0)

    def column(k):
        return jnp.take_along_axis(work, jnp.full(work.shape, k, jnp.int32), axis=1)

    def row(v, k):
        return jnp.broadcast_to(v[k : k + 1, :], (8, LANES))

    def tall(v):
        return jnp.concatenate([v] * (count // 8), axis=0)

    for k in range(0, count, size):
        cols = [column(k + j) for j in range(size)]
        rows = [row(work, k + i) for i in range(size)]
        p = [[row(cols[j], k + i) for j in range(size)] for i in range(size)]
        for s in range(0, size, 2):
            a, b, c, d = p[s][s], p[s][s + 1], p[s + 1][s], p[s + 1][s + 1]
            inverse = 1.0 / (a * d - b * c)
            a, b, c, d = d * inverse, -(b * inverse), -(c * inverse), a * inverse
            rows[s], rows[s + 1] = a * rows[s] + b * rows[s + 1], c * rows[s] + d * rows[s + 1]
            for j in range(s + 2, size):
                u, v = p[s][j], p[s + 1][j]
                p[s][j], p[s + 1][j] = a * u + b * v, c * u + d * v
            for i in range(size):
                if i in (s, s + 1):
                    continue
                u, v = p[i][s], p[i][s + 1]
                rows[i] = rows[i] - u * rows[s] - v * rows[s + 1]
                for j in range(s + 2, size):
                    p[i][j] = p[i][j] - u * p[s][j] - v * p[s + 1][j]
        for j in range(size):
            work = work - cols[j] * tall(rows[j])
        for j in range(size):
            work = jnp.where(sub == k + j, tall(rows[j]), work)
    return work


def final_kernel(
    pairing_hbm, parts_hbm, bg_hbm, mid_hbm, edge_hbm,
    out_ref, sens_ref, pairing_ref, parts_ref, bg, adj, s_ref, mix_ref, sems, *, damping,
):
    pairs = [
        (parts_hbm, parts_ref),
        (pairing_hbm, pairing_ref),
        (edge_hbm.at[pl.ds(0, 5)], s_ref.at[pl.ds(0, 5)]),
        (mid_hbm, s_ref.at[pl.ds(5, 8)]),
        (edge_hbm.at[pl.ds(5, 5)], s_ref.at[pl.ds(13, 5)]),
        (bg_hbm, bg),
    ]
    copies = [pltpu.make_async_copy(s, d, sems.at[i]) for i, (s, d) in enumerate(pairs)]

    @pl.when(lax.axis_index("gx") >= 0)
    def _():
        for c in copies:
            c.start()
        wait_all(copies[:2])

    total = jnp.sum(parts_ref[...], axis=0)

    def part(k):
        r, c = (k // 8) * F, (k % 8) * F
        return total[r : r + F, c : c + F]

    m = [part(k) for k in range(6)]
    p = [part(6), part(7), part(8), part(9).T, part(10).T]
    e = [part(k) for k in range(11, 15)]
    y = galerkin(*m[:4])

    pairing = pairing_ref[:, 0:F]
    w = matmul(8.0 * matmul(pairing, pairing, ((1,), (1,))), jnp.concatenate(p[:2], axis=0), ((1,), (1,)))
    forms = []
    for k in range(4):
        inside = jnp.concatenate(
            [
                jnp.concatenate([m[k], m[k + 1]], axis=1),
                jnp.concatenate([m[k + 1], m[k + 2]], axis=1),
            ],
            axis=0,
        )
        across = matmul(jnp.concatenate([p[k], p[k + 1]], axis=0), w)
        local = matmul(w, matmul(e[k], w), ((0,), (0,)))
        forms.append(damping * (damping * inside + across + across.T) + local)
    hy = matmul(jnp.concatenate(forms, axis=0), y)
    moments = [matmul(y, hy[32 * k : 32 * (k + 1)], ((0,), (0,))) for k in range(4)]
    z = jnp.concatenate([damping * y, matmul(w, y)], axis=0)
    q = galerkin(*moments)
    z0, z1 = matmul(z, q[0:F]), matmul(z, q[F:])
    none = jnp.zeros((F, F), jnp.float32)
    mix = [
        jnp.concatenate([y[0:F], z0[0:F]], axis=1),
        jnp.concatenate([y[F:], z0[F : 2 * F] + z1[0:F]], axis=1),
        jnp.concatenate([none, z1[F : 2 * F]], axis=1),
        jnp.concatenate([none, z0[2 * F :]], axis=1),
        jnp.concatenate([none, z1[2 * F :]], axis=1),
    ]
    mix = [mix[i] for i in (0, 0, 1, 1, 2, 2, 3, 4, 4)]
    mix = jnp.concatenate(mix, axis=0).T
    hi = mix.astype(jnp.bfloat16)
    mix_ref[0:32, :] = hi
    mix_ref[32:64, :] = (mix - hi.astype(jnp.float32)).astype(jnp.bfloat16)
    wait_all(copies[2:])
    both = mix_ref[...]

    def combine(x, lanes):
        out = jnp.dot(both, s_ref[x, :, lanes], preferred_element_type=jnp.float32)
        return out[0:32] + out[32:64]

    def store(x, out):
        for k in range(10):
            cols = slice(k * LANES, (k + 1) * LANES)
            if 0 < k < 9:
                out_ref[pl.ds(x * 8 + k - 9, F, stride=128), :] = out[0:F, cols]
            adj[x, tile_at(k), :] = out[F:, cols]

    def store_end(x, out):
        for k in range(8):
            adj[x, tile_at(k + 1), :] = out[F:, k * LANES : (k + 1) * LANES]

    lane = lane_ids(F)

    def sens_plane(x):
        b, a = bg[x, tile_at(1), :], adj[x, tile_at(1), :]
        before = (b - bg[x, tile_at(0), :]) * (a - adj[x, tile_at(0), :])
        for k in range(1, 9):
            bn, an = bg[x, tile_at(k + 1), :], adj[x, tile_at(k + 1), :]
            after = (bn - b) * (an - a)
            total = before + after
            for s in (x - 1, x + 1):
                total = total + (bg[s, tile_at(k), :] - b) * (adj[s, tile_at(k), :] - a)
            bu = jnp.where(lane == LANES - 1, 0.0, pltpu.roll(b, LANES - 1, 1))
            au = jnp.where(lane == LANES - 1, 0.0, pltpu.roll(a, LANES - 1, 1))
            bd = jnp.where(lane == 0, 0.0, pltpu.roll(b, 1, 1))
            ad = jnp.where(lane == 0, 0.0, pltpu.roll(a, 1, 1))
            total = total + (bu - b) * (au - a) + (bd - b) * (ad - a)
            sens_ref[x - 1, k - 1 : k, :] = -0.5 * jnp.sum(total, axis=0, keepdims=True)
            before, b, a = after, bn, an

    ends = slice(LANES, 9 * LANES)
    store_end(0, combine(0, ends))
    store(1, combine(1, slice(0, WIDE)))
    store(2, combine(2, slice(0, WIDE)))

    def plane(x, carry):
        out = combine(x + 2, slice(0, WIDE))
        sens_plane(x)
        store(x + 2, out)
        return carry

    lax.fori_loop(1, 15, plane, 0, unroll=14)
    out = combine(17, ends)
    sens_plane(15)
    store_end(17, out)
    sens_plane(16)


def final(pairing, parts, bg, mid, edges, damping):
    vmem = pl.BlockSpec(memory_space=pltpu.VMEM)
    hbm = pl.BlockSpec(memory_space=pltpu.HBM)

    def kernel(*refs):
        final_kernel(*refs, damping=damping)

    return pl.pallas_call(
        kernel,
        out_shape=(
            jax.ShapeDtypeStruct((2048, LANES), jnp.float32),
            jax.ShapeDtypeStruct((16, 8, LANES), jnp.float32),
        ),
        in_specs=[hbm] * 5,
        scratch_shapes=[
            pltpu.VMEM((F, LANES), jnp.float32),
            pltpu.VMEM((F, 32, LANES), jnp.float32),
            pltpu.VMEM((18, 160, LANES), jnp.float32),
            pltpu.VMEM((18, 160, LANES), jnp.float32),
            pltpu.VMEM((18, KEPT, WIDE), jnp.bfloat16),
            pltpu.VMEM((64, KEPT), jnp.bfloat16),
            pltpu.SemaphoreType.DMA((6,)),
        ],
        compiler_params=pltpu.CompilerParams(vmem_limit_bytes=56 * MB),
        name="final",
    )(pairing, pltpu.with_memory_space_constraint(parts, pltpu.HBM), bg, mid, edges)


def spread(block, axis, count, groups=None):
    copies = jnp.broadcast_to(block[None], (count,) + block.shape)
    return lax.all_to_all(copies, axis, 0, 0, axis_index_groups=groups)


def swaps(first, count):
    lows = range(first, count - 1, 2)
    return [(i, i + 1) for i in lows] + [(i + 1, i) for i in lows]


def on_device(background, conductivity, perturbation, electrodes, pattern):
    size_x, size_y, size_z = conductivity.shape
    count_x, count_y = lax.axis_size("gx"), lax.axis_size("gy")
    wide, core, chip, a, b, ids, pairing = pack(
        background, conductivity, perturbation, electrodes, pattern
    )
    a = lax.ppermute(a, "gx", swaps(0, count_x))
    b = lax.ppermute(b, "gx", swaps(1, count_x))
    chip = lax.ppermute(chip, "gy", swaps(1, count_y))
    core = lax.ppermute(core, "gy", swaps(0, count_y))
    fields = early(ids, wide)
    a_corner, b_corner = pack_corners(core, chip)
    a_corner = lax.ppermute(a_corner, "gx", swaps(0, count_x))
    b_corner = lax.ppermute(b_corner, "gx", swaps(1, count_x))
    wide, v0, v1, v2, _, _, _, side, gram, mid, *coeffs = inner(wide, fields, core, chip)
    pay, edges, bg = edge(
        ids, a, b, a_corner, b_corner, [wide, v0, v1, v2, *coeffs], side, gram
    )
    pay = pay + lax.ppermute(pay, "gy", swaps(0, count_y))
    pay = jnp.sum(spread(pay, "gx", count_x), axis=0)
    chips = count_y // 2
    groups = [[2 * i + c for i in range(chips)] for c in range(2)]
    parts = spread(pay, "gy", chips, groups)
    cells = size_x * size_y * size_z * count_x * count_y
    damping = 80.0 / math.sqrt(cells)
    tangent, sens = final(pairing, parts, bg, mid, edges, damping)
    return tangent.reshape(background.shape), sens


def solution(mesh):
    in_specs = (P(None, "gx", "gy", None), P("gx", "gy", None), P("gx", "gy", None), P(), P())
    out_specs = (P(None, "gx", "gy", None), P("gx", "gy", None))
    return jax.shard_map(
        on_device, mesh=mesh, in_specs=in_specs, out_specs=out_specs, check_vma=False
    )
```
